128 devices in a mesh: dp: 8 (over y, x_lo), seq: 16 (over z, x_hi, core).
Axes of the slice: x: 4 (x_hi: 2, x_lo: 2; x = x_hi * 2 + x_lo), y: 4, z: 4, core: 2. Of those that a mesh axis runs over, the one named last changes fastest.
Arguments:
- tokens: bfloat16 [16384, 1024], P(('dp', 'seq')), may hold values from -6 to 6
- segment_ids: int32 [8, 2048], P('dp', 'seq'), may hold values from 0 to 7, never falling along the last dimension, each value on 1 to 1024 neighbouring positions
- attn_gain: bfloat16 [1024], P('dp'), may hold values from 0.5 to 1.5
- w_query: bfloat16 [1024, 1024], P('dp'), may hold values from -0.1875 to 0.1875
- w_key: bfloat16 [1024, 512], P('dp'), may hold values from -0.1875 to 0.1875
- w_value: bfloat16 [1024, 512], P('dp'), may hold values from -0.1875 to 0.1875
- w_out: bfloat16 [1024, 1024], P('dp'), may hold values from -1 to 1
- ffn_gain: bfloat16 [1024], P('dp'), may hold values from 0.5 to 1.5
- w_gate: bfloat16 [1024, 4608], P('dp'), may hold values from -0.1875 to 0.1875
- w_up: bfloat16 [1024, 4608], P('dp'), may hold values from -0.1875 to 0.1875
- w_down: bfloat16 [4608, 1024], P('dp'), may hold values from -0.09375 to 0.09375
- query_gain: bfloat16 [64], replicated, may hold values from 0.25 to 1.75
- key_gain: bfloat16 [64], replicated, may hold values from 0.25 to 1.75
- cotangent: bfloat16 [16384, 1024], P(('dp', 'seq')), may hold values from -6 to 6
Outputs:
- block_out: bfloat16 [16384, 1024], P(('dp', 'seq'))
- input_grad: bfloat16 [16384, 1024], P(('dp', 'seq'))
- grad_attn_gain: float32 [1024], P('dp')
- grad_w_query: float32 [1024, 1024], P('dp')
- grad_w_key: float32 [1024, 512], P('dp')
- grad_w_value: float32 [1024, 512], P('dp')
- grad_w_out: float32 [1024, 1024], P('dp')
- grad_ffn_gain: float32 [1024], P('dp')
- grad_w_gate: float32 [1024, 4608], P('dp')
- grad_w_up: float32 [1024, 4608], P('dp')
- grad_w_down: float32 [4608, 1024], P('dp')
- grad_query_gain: float32 [64], replicated
- grad_key_gain: float32 [64], replicated
The draws below stay inside these ranges and needn't reach their ends.
Inputs may be any that keep to these rules, and one draw needn't show every extreme that they name: `segment_ids`: in each sequence the document numbers never fall along the tokens; each of the 8 documents has 1 to 1024 tokens and one has exactly 1024.
All inputs are finite; a program needn't handle non-finite values.
Results may differ from the reference program's by a relative error of at most 0.025.
Values may be sent and summed in bfloat16 or wider, within the bound.
A program may use at most 192 MiB of HBM per device.

```python
import math
import jax
import jax.numpy as jnp
import numpy as np
from jax import lax

D = 1024
FF = 4608
HEADS = 16
KVH = 8
HD = 64
SEQ_LEN = 2048
TOKENS = 16384
DOCS = 8
DOC_MOST = 1024
N_DP = 8
N_SEQ = 16


def steps_of(rng, shape, cuts, low, largest):
    gain = 1.0
    for position, shards_of in cuts:
        draws = jax.random.uniform(jax.random.fold_in(jax.random.fold_in(rng, 6), position), (shards_of,), jnp.float32, low / len(cuts), largest / len(cuts))
        gain = gain * jnp.repeat(jnp.exp(draws), shape[position] // shards_of).reshape((-1,) + (1,) * (len(shape) - 1 - position))
    return gain


def length_profile(count, total, bound, slope):
    loads = [(1 << 20) // math.isqrt(grade ** slope) + 1 for grade in range(2, count + 1)]
    spare, given = total - bound - (count - 1), [1] * (count - 1)
    while spare > 0:
        movable = [i for i in range(count - 1) if given[i] < bound]
        whole, budget = sum([loads[i] for i in movable]), spare
        for i in movable:
            addition = min(bound - given[i], max(1, budget * loads[i] // whole), spare)
            given[i] = given[i] + addition
            spare = spare - addition
    return np.array([bound] + given)


def ragged_sizes(own_key, count, total, bound, lean):
    if count == 2:
        one = jax.random.randint(own_key, (), max(1, total - bound), min(bound, total - 1) + 1)
        return jnp.stack([one, total - one])
    lengths = jnp.asarray(length_profile(count, total, bound, lean), jnp.int32)
    couples = (count - 1) // 2
    source_of, receiver = lengths[1:1 + 2 * couples:2], lengths[2:2 + 2 * couples:2]
    slack = jnp.minimum(source_of - 1, bound - receiver)
    moved = jax.random.randint(jax.random.fold_in(own_key, 1), (couples,), 0, 1 << 20) % (slack + 1)
    lengths = lengths.at[1:1 + 2 * couples:2].set(source_of - moved).at[2:2 + 2 * couples:2].set(receiver + moved)
    return lengths[jax.random.permutation(jax.random.fold_in(own_key, 2), count)]


def bell_draw(rng, extent, scale, reach, cuts=(), kind=jnp.bfloat16):
    loudness = steps_of(rng, extent, cuts, -0.22, 0.18) if cuts else 1.0
    entries = jax.random.normal(rng, extent, jnp.float32) * scale * loudness
    return jnp.minimum(jnp.maximum(entries, -reach), reach).astype(kind)


def setup_inputs(seed: int = 0) -> dict:
    key_list = jax.random.split(jax.random.key(seed), 15)
    tokens = bell_draw(key_list[0], (TOKENS, D), 1.0, 6.0, ((0, 128),))
    segment_ids = jax.vmap(lambda own: jnp.searchsorted(jnp.cumsum(ragged_sizes(own, DOCS, SEQ_LEN, DOC_MOST, 1)), jnp.arange(SEQ_LEN), side="right"))(jax.random.split(key_list[1], N_DP)).reshape((N_DP, SEQ_LEN)).astype(jnp.int32)
    attn_gain = jnp.clip(1.0 + 0.1 * jax.random.normal(key_list[2], (D,), jnp.float32), 0.5, 1.5).astype(jnp.bfloat16)
    w_query = bell_draw(key_list[3], (D, HEADS * HD), D ** -0.5, 0.1875, ((0, 8),))
    w_key = bell_draw(key_list[4], (D, KVH * HD), D ** -0.5, 0.1875, ((0, 8),))
    w_value = bell_draw(key_list[5], (D, KVH * HD), D ** -0.5, 0.1875, ((0, 8),))
    w_out = bell_draw(key_list[6], (HEADS * HD, D), (D // 32) ** -0.5, 1.0, ((0, 8),))
    ffn_gain = jnp.clip(1.0 + 0.1 * jax.random.normal(key_list[7], (D,), jnp.float32), 0.5, 1.5).astype(jnp.bfloat16)
    w_gate = bell_draw(key_list[8], (D, FF), D ** -0.5, 0.1875, ((0, 8),))
    w_up = bell_draw(key_list[9], (D, FF), D ** -0.5, 0.1875, ((0, 8),))
    w_down = bell_draw(key_list[10], (FF, D), FF ** -0.5, 0.09375, ((0, 8),))
    query_gain = jnp.clip(1.0 + 0.15 * jax.random.normal(key_list[11], (HD,), jnp.float32), 0.25, 1.75).astype(jnp.bfloat16)
    key_gain = jnp.clip(1.0 + 0.15 * jax.random.normal(key_list[12], (HD,), jnp.float32), 0.25, 1.75).astype(jnp.bfloat16)
    cotangent = bell_draw(key_list[13], (TOKENS, D), 1.0, 6.0, ((0, 128),))
    return dict(tokens=tokens, segment_ids=segment_ids, attn_gain=attn_gain, w_query=w_query, w_key=w_key, w_value=w_value, w_out=w_out, ffn_gain=ffn_gain, w_gate=w_gate, w_up=w_up, w_down=w_down, query_gain=query_gain, key_gain=key_gain, cotangent=cotangent)


@jax.custom_vjp
def low(v):
    return lax.optimization_barrier(v.astype(jnp.bfloat16)).astype(jnp.float32)

@jax.custom_vjp
def low_back(v):
    return v

def low_keep(v):
    return (low(v), None)

def low_pass(kept, grad):
    return (grad,)

def back_keep(v):
    return (v, None)

def back_low(kept, grad):
    return (low(grad),)
low.defvjp(low_keep, low_pass)
low_back.defvjp(back_keep, back_low)
EPSILON = 1e-05
ROPE_BASE = 1000000.0
HIGHEST = lax.Precision.HIGHEST

def product(left_side, right_side):
    return jnp.dot(left_side, right_side, precision=HIGHEST, preferred_element_type=jnp.float32)

def rms_apply(values, gain_vec):
    return values * lax.rsqrt(lax.optimization_barrier(jnp.mean(values * values, axis=-1, keepdims=True)) + EPSILON) * gain_vec

def rotate(values, cosine_table, sine_table):
    half_size = values.shape[-1] // 2
    first_half = values[..., :half_size]
    second_half = values[..., half_size:]
    return jnp.concatenate([first_half * cosine_table - second_half * sine_table, second_half * cosine_table + first_half * sine_table], axis=-1)

def rope_tables(positions, head_size):
    half_size = head_size // 2
    inverse = ROPE_BASE ** (-(jnp.arange(half_size).astype(jnp.float32) * 2.0 / head_size))
    angles = positions[:, None] * inverse[None, :]
    return (jnp.cos(angles)[:, None, :], jnp.sin(angles)[:, None, :])

def doc_positions(doc_ids):
    seq_length = doc_ids.shape[0]
    begins = lax.optimization_barrier(jnp.sum((doc_ids[None, :] < doc_ids[:, None]).astype(jnp.int32), axis=1))
    return (jnp.arange(seq_length, dtype=jnp.int32) - begins).astype(jnp.float32)

def attend(queries, key_copies, value_copies, doc_ids):
    seq_length = queries.shape[0]
    group_size = HEADS // N_SEQ
    keys_full = jnp.repeat(key_copies, group_size, axis=1)
    values_full = jnp.repeat(value_copies, group_size, axis=1)
    block_rows = min(512, seq_length)
    key_index = jnp.arange(seq_length, dtype=jnp.int32)
    factor = HD ** (-0.5)

    def one_block(row_start):
        query_block = lax.dynamic_slice_in_dim(queries, row_start, block_rows, 0)
        block_ids = lax.dynamic_slice_in_dim(doc_ids, row_start, block_rows, 0)
        rows_index = row_start + jnp.arange(block_rows, dtype=jnp.int32)
        allowed = (block_ids[:, None] == doc_ids[None, :]) & (key_index[None, :] <= rows_index[:, None])
        raw_scores = jnp.einsum('qhd,khd->hqk', query_block, keys_full, precision=HIGHEST, preferred_element_type=jnp.float32)
        scores = low_back(raw_scores * factor)
        scores = jnp.where(allowed[None], scores, -1e+30)
        row_max = lax.optimization_barrier(jnp.max(scores, axis=-1, keepdims=True))
        weights = jnp.exp(scores - row_max)
        softmax_out = low(weights / lax.optimization_barrier(jnp.sum(weights, axis=-1, keepdims=True)))
        return jnp.einsum('hqk,khd->qhd', softmax_out, values_full, precision=HIGHEST, preferred_element_type=jnp.float32)
    starts = jnp.arange(seq_length // block_rows, dtype=jnp.int32) * block_rows
    outputs = lax.map(jax.checkpoint(one_block), starts)
    return outputs.reshape(seq_length, HEADS * HD)

def block_forward(inputs, doc_ids, attn_gain, w_query, w_key, w_value, w_out, ffn_gain, w_gate, w_up, w_down, query_gain, key_gain):
    seq_length = inputs.shape[0]
    copies = N_SEQ // KVH
    cosine_table, sine_table = rope_tables(doc_positions(doc_ids), HD)
    hidden = low(rms_apply(inputs, attn_gain))
    queries = low_back(product(hidden, w_query)).reshape(seq_length, HEADS, HD)
    keys_raw = low_back(product(hidden, w_key)).reshape(seq_length, KVH, HD)
    values_raw = low_back(product(hidden, w_value)).reshape(seq_length, KVH, HD)
    queries = low_back(low(rotate(rms_apply(queries, query_gain), cosine_table, sine_table)))
    key_copies = low_back(jnp.repeat(low(rotate(rms_apply(keys_raw, key_gain), cosine_table, sine_table)), copies, axis=1))
    value_copies = low_back(jnp.repeat(low(values_raw), copies, axis=1))
    attended = low_back(low(attend(queries, key_copies, value_copies, doc_ids)))
    branch = low_back(product(attended, w_out))
    middle = inputs + branch
    hidden_two = low(rms_apply(middle, ffn_gain))
    gate_pre = low_back(product(hidden_two, w_gate))
    up_pre = low_back(product(hidden_two, w_up))
    mixed_act = low(gate_pre * jax.nn.sigmoid(gate_pre) * up_pre)
    return middle + product(mixed_act, w_down)

def reference(tokens, segment_ids, attn_gain, w_query, w_key, w_value, w_out, ffn_gain, w_gate, w_up, w_down, query_gain, key_gain, cotangent):
    weights_f = tuple((matrix.astype(jnp.float32) for matrix in (attn_gain, w_query, w_key, w_value, w_out, ffn_gain, w_gate, w_up, w_down, query_gain, key_gain)))
    inputs_all = tokens.astype(jnp.float32).reshape(N_DP, SEQ_LEN, D)
    cotangent_all = cotangent.astype(jnp.float32).reshape(N_DP, SEQ_LEN, D)
    zeros_init = tuple((jnp.zeros(matrix.shape, jnp.float32) for matrix in weights_f))

    def per_sequence(carried, scan_item):
        inputs, doc_ids, seq_cotangent = scan_item

        def forward(inputs_now, *params):
            return block_forward(inputs_now, doc_ids, *params)
        outputs, pullback = jax.vjp(forward, inputs, *weights_f)
        gradients = pullback(seq_cotangent)
        summed = tuple((earlier + later for earlier, later in zip(carried, gradients[1:])))
        return (summed, (outputs.astype(jnp.bfloat16), gradients[0].astype(jnp.bfloat16)))
    totals, (block_outs, input_grads) = lax.scan(per_sequence, zeros_init, (inputs_all, segment_ids, cotangent_all))
    return (block_outs.reshape(TOKENS, D), input_grads.reshape(TOKENS, D), totals[0], totals[1], totals[2], totals[3], totals[4], totals[5], totals[6], totals[7], totals[8], totals[9], totals[10])
```

```python
import math

import jax
import jax.numpy as jnp
import numpy as np
from jax import lax
from jax.experimental import pallas as pl
from jax.experimental.pallas import tpu as pltpu
from jax.sharding import PartitionSpec as P

MESH = pl.DeviceIdType.MESH
F32 = jnp.float32
BF = jnp.bfloat16
EPS = 1e-05
ROPE_BASE = 1000000.0
NN = (((1,), (0,)), ((), ()))
NT = (((1,), (1,)), ((), ()))
TN = (((0,), (0,)), ((), ()))
SCALE = 0.125
LOG2E = math.log2(math.e)


def dot(a, b, dims=NN, precision=None):
    return lax.dot_general(a, b, dims, preferred_element_type=F32, precision=precision)


def rem(a, b):
    return lax.rem(a, b)


class Place:
    def __init__(self):
        self.dp = lax.axis_index("dp")
        self.sq = lax.axis_index("seq")
        self.y = lax.div(self.dp, 2)
        self.xl = rem(self.dp, 2)
        self.z = lax.div(self.sq, 4)
        self.g = rem(self.sq, 4)
        self.xh = lax.div(self.g, 2)
        self.c = rem(self.sq, 2)

    def zpeer(self, dz):
        return (self.dp, rem(self.z + dz + 4, 4) * 4 + self.g)

    def sib(self):
        return (self.dp, self.sq + 1 - 2 * self.c)

    def xpeer(self):
        return (self.dp, self.z * 4 + (1 - self.xh) * 2 + self.c)

    def dpeer(self, k):
        return (rem(self.dp + k + 8, 8), self.sq)

    def speer(self, k):
        return (self.dp, rem(self.sq + k + 16, 16))

    def tpeer(self, t):
        xl = self.xl if t == 0 else 1 - self.xl
        return (self.z * 2 + xl, self.y * 4 + self.g)


def seg_rows(ids):
    start = jnp.zeros_like(ids)
    for j in range(1, 8):
        below = jnp.sum(jnp.where(ids < j, 1.0, 0.0), keepdims=True)
        start = jnp.where(ids == j, below, start)
    return start


def lane_half():
    return lax.rem(lax.broadcasted_iota(jnp.int32, (1, 128), 1), 64) < 32


def swap_halves(x):
    return jnp.where(lane_half(), pltpu.roll(x, 96, 1), pltpu.roll(x, 32, 1))


def head_mean(x):
    a = lax.div(lax.broadcasted_iota(jnp.int32, (128, 128), 0), 64)
    b = lax.div(lax.broadcasted_iota(jnp.int32, (128, 128), 1), 64)
    block = jnp.where(a == b, 1.0 / 64, 0.0)
    return dot(x, block, NN, lax.Precision.HIGHEST)


def spread_heads(first, second):
    lo = lax.broadcasted_iota(jnp.int32, (1, 128), 1) < 64
    return [
        jnp.where(lo, first, 0.0),
        jnp.where(lo, pltpu.roll(first, 64, 1), 0.0),
        jnp.where(lo, 0.0, pltpu.roll(second, 64, 1)),
        jnp.where(lo, 0.0, second),
    ]


INPUTS = ["tok", "meta", "wq", "wk", "wv", "wo", "wg", "wu", "wd", "cot"]
OUTPUTS = {
    "block_out": ((128, 1024), BF),
    "input_grad": ((128, 1024), BF),
    "fF": ((16, 32, 2304), BF),
    "fD": ((16, 3, 16, 1024), BF),
    "fA": ((16, 32, 768), BF),
    "g_small": ((8, 128), F32),
}
SCRATCH = {
    "tok_all": ((4, 128, 1024), BF),
    "cot_all": ((4, 128, 1024), BF),
    "h_all": ((4, 128, 1024), BF),
    "mseq": ((16, 8, 128), F32),
    "mdp": ((8, 8, 128), F32),
    "wqkv": ((8, 128, 512), BF),
    "wo_v": ((8, 128, 1024), BF),
    "wg_v": ((8, 128, 1152), BF),
    "wu_v": ((8, 128, 1152), BF),
    "wd_v": ((18, 64, 1024), BF),
    "wg_s": ((64, 1152), BF),
    "wu_s": ((64, 1152), BF),
    "st": ((16, 128), F32),
    "qk_raw": ((4, 128, 384), F32),
    "qz": ((4, 512, 128), BF),
    "kv": ((16, 128, 256), BF),
    "kt": ((16, 128, 128), BF),
    "vt": ((16, 128, 128), BF),
    "cosr": ((4, 128, 128), F32),
    "sinr": ((4, 128, 128), F32),
    "invl": ((4, 8, 512), F32),
    "oT": ((4, 256, 128), F32),
    "acc": ((128, 512), F32),
    "lacc": ((8, 512), F32),
    "o_s": ((4, 128, 256), BF),
    "o_in": ((4, 128, 256), BF),
    "o_own": ((128, 1024), BF),
    "o_full": ((4, 128, 1024), BF),
    "mid": ((128, 1024), F32),
    "h2": ((4, 128, 1024), BF),
    "dm": ((4, 128, 1152), F32),
    "mixed": ((4, 128, 1152), BF),
    "dg": ((4, 128, 1152), BF),
    "du": ((4, 128, 1152), BF),
    "p2s": ((3, 128, 1024), BF),
    "p2r": ((3, 128, 1024), BF),
    "own": ((128, 1024), F32),
    "p3s": ((3, 128, 1024), BF),
    "p3r": ((3, 128, 1024), BF),
    "own3": ((128, 1024), F32),
    "dmid": ((128, 1024), F32),
    "da": ((128, 1024), BF),
    "da_c": ((4, 128, 256), BF),
    "dob": ((128, 1024), BF),
    "do_all": ((4, 128, 256), BF),
    "doz": ((512, 128), BF),
    "dkv": ((16, 128, 256), F32),
    "dkvb": ((4, 4, 128, 256), BF),
    "dkvr": ((3, 4, 128, 256), BF),
    "dqr": ((4, 128, 256), F32),
    "dqkv": ((4, 128, 512), BF),
    "p4s": ((3, 128, 1024), BF),
    "p4r": ((3, 128, 1024), BF),
    "gF": ((8, 128, 2304), BF),
    "gD": ((18, 64, 1024), BF),
    "gA": ((8, 128, 768), BF),
    "r1F": ((8, 64, 2304), BF),
    "r1D": ((18, 32, 1024), BF),
    "r1A": ((8, 64, 768), BF),
    "r2F": ((16, 32, 2304), BF),
    "r2D": ((16, 3, 16, 1024), BF),
    "r2A": ((16, 32, 768), BF),
    "oF": ((32, 2304), BF),
    "oD": ((3, 16, 1024), BF),
    "oA": ((32, 768), BF),
    "gsm": ((8, 8, 128), F32),
    "gs1": ((8, 8, 128), F32),
    "gs1s": ((8, 128), F32),
    "gs2": ((16, 8, 128), F32),
}
NSEM = 320


class Refs:
    pass


class Comm:
    def __init__(self, place, ssem, rsem):
        self.p, self.ssem, self.rsem = place, ssem, rsem
        self.n = 0
        self.sent = []

    def take(self, count=1):
        base = self.n
        self.n += count
        return base

    def copy(self, src, dst, i, dev):
        return pltpu.make_async_remote_copy(
            src_ref=src, dst_ref=dst, send_sem=self.ssem.at[i], recv_sem=self.rsem.at[i],
            device_id=dev, device_id_type=MESH,
        )

    def send(self, src, dst, i, dev):
        self.copy(src, dst, i, dev).start()
        self.sent.append((src, i))

    def local(self, src, dst, i):
        return pltpu.make_async_copy(src, dst, self.rsem.at[i])

    def got(self, dst, i):
        self.copy(dst, dst, i, self.p.sib()).wait_recv()

    def finish(self):
        for src, i in self.sent:
            self.copy(src, src, i, self.p.sib()).wait_send()
        self.sent = []


def kernel(*refs):
    r = Refs()
    names = INPUTS + list(OUTPUTS) + list(SCRATCH)
    for name, ref in zip(names, refs):
        setattr(r, name, ref)
    ssem, rsem = refs[len(names):]
    p = Place()
    m = Comm(p, ssem, rsem)

    def z_of(dz):
        return rem(p.z - dz + 4, 4)

    half = pl.ds(pl.multiple_of(p.c * 64, 64), 64)
    other = pl.ds(pl.multiple_of(64 - p.c * 64, 64), 64)
    zq = pl.ds(pl.multiple_of(p.z * 256, 256), 256)
    zk = pl.ds(pl.multiple_of(p.z * 128, 128), 128)
    dps = [rem(p.dp + 8 - k, 8) for k in range(8)]

    i_loc = m.take(3)
    stage = []
    for src, dst, i in ((r.wg, r.wg_s, i_loc), (r.wu, r.wu_s, i_loc + 1)):
        for t in range(9):
            cols = pl.ds(pl.multiple_of(t * 512 + p.z * 128, 128), 128)
            m.local(src.at[half, cols], dst.at[:, pl.ds(t * 128, 128)], i).start()
        stage.append((dst, i))
    parts = ((r.wq, zq, 0, 256), (r.wk, zk, 256, 128), (r.wv, zk, 384, 128))
    for w, cols, at, wid in parts:
        m.local(w.at[half, cols], r.wqkv.at[p.dp, half, pl.ds(at, wid)], i_loc + 2).start()

    bar = pltpu.get_barrier_semaphore()
    for k in range(1, 16):
        pl.semaphore_signal(bar, inc=1, device_id=p.speer(k), device_id_type=MESH)
    for k in range(1, 8):
        pl.semaphore_signal(bar, inc=1, device_id=p.dpeer(k), device_id_type=MESH)
    far = []
    for k in range(8):
        far.append((p.dpeer(k)[0], (p.z * 4 + (1 - p.xh) * 2 + p.c)))
    for k in range(1, 8):
        pl.semaphore_signal(bar, inc=1, device_id=far[k], device_id_type=MESH)
    pl.semaphore_wait(bar, 29)

    i_tok = m.take(4)
    for dz in (1, 3, 2):
        m.send(r.tok, r.tok_all.at[dz], i_tok + dz, p.zpeer(dz))
    i_w = m.take(8)
    for k in range(1, 8):
        for w, cols, at, wid in parts:
            m.copy(w.at[half, cols], r.wqkv.at[p.dp, half, pl.ds(at, wid)], i_w + k, p.dpeer(k)).start()
        m.sent.append((r.wqkv.at[0, half], i_w + k))
    i_mseq = m.take(16)
    for k in range(1, 16):
        m.send(r.meta, r.mseq.at[p.sq], i_mseq + k, p.speer(k))
    i_mdp = m.take(8)
    for k in range(1, 8):
        m.send(r.meta, r.mdp.at[p.dp], i_mdp + k, p.dpeer(k))
    r.mseq[p.sq] = r.meta[...]
    r.mdp[p.dp] = r.meta[...]

    for k in range(1, 16):
        m.got(r.mseq.at[rem(p.sq + 16 - k, 16)], i_mseq + k)
    r.st[...] = seg_rows(r.mseq[:, 2, :])
    lanesign = jnp.where(lane_half(), -1.0, 1.0)
    freq = r.meta[5:6, :]
    for dz in range(4):
        i = 4 * z_of(dz) + p.g
        row = r.st[pl.ds(i, 1), :]
        pos = (lax.broadcasted_iota(jnp.int32, (1, 128), 1) + i * 128).astype(F32) - row
        ang = jnp.transpose(jnp.broadcast_to(pos, (128, 128))) * freq
        r.cosr[dz] = jnp.cos(ang)
        r.sinr[dz] = jnp.sin(ang) * lanesign
    for k in range(1, 8):
        m.got(r.mdp.at[dps[k]], i_mdp + k)
    gain1 = jnp.concatenate([r.mdp[j, 0:1, :] for j in range(8)], axis=1)
    gain2 = jnp.concatenate([r.mdp[j, 1:2, :] for j in range(8)], axis=1)

    m.local(r.wqkv.at[0, half], r.wqkv.at[0, half], i_loc + 2).wait()
    for k in range(1, 8):
        m.got(r.wqkv.at[dps[k], half], i_w + k)
    i_share = m.take(5)
    m.send(r.wqkv.at[:, half], r.wqkv.at[:, half], i_share, p.sib())

    i_wo = m.take(8)
    m.local(r.wo.at[half], r.wo_v.at[p.dp, half], i_wo).start()
    for k in range(1, 8):
        m.send(r.wo.at[half], r.wo_v.at[p.dp, half], i_wo + k, p.dpeer(k))
    for dst, i in stage:
        m.local(dst, dst, i).wait()
    i_wd = m.take(1)
    i_wds = m.take(24)
    i_wg = m.take(8)
    i_wu = m.take(8)

    def down_pieces(d):
        out = []
        for n in range(2):
            u = rem(2 * p.z + n - d + 8, 8)
            big = 9 * d + u
            out.append((u, 2 * lax.div(big, 8) + rem(big, 2)))
        big = 9 * d + 8
        return out, (8, 2 * lax.div(big, 8) + rem(big, 2)), lax.div(d, 2) == p.z

    pieces, extra, has_extra = down_pieces(p.dp)
    c32 = p.c * 32

    def down_copy(k, n, piece):
        u, hidx = piece
        src = r.wd.at[pl.ds(pl.multiple_of(u * 64 + c32, 32), 32)]
        dst = r.wd_v.at[hidx, pl.ds(pl.multiple_of(c32, 32), 32)]
        if k == 0:
            return pltpu.make_async_copy(src, dst, rsem.at[i_wd])
        return pltpu.make_async_remote_copy(
            src_ref=src, dst_ref=dst, send_sem=ssem.at[i_wds + 3 * k + n], recv_sem=rsem.at[i_wd],
            device_id=p.dpeer(k), device_id_type=MESH,
        )

    for k in range(8):
        for n in range(2):
            down_copy(k, n, pieces[n]).start()

    @pl.when(has_extra)
    def _():
        for k in range(8):
            down_copy(k, 2, extra).start()

    for src, dst, i in ((r.wg_s, r.wg_v, i_wg), (r.wu_s, r.wu_v, i_wu)):
        for k in range(1, 8):
            m.send(src, dst.at[p.dp, half], i + k, p.dpeer(k))
        dst[p.dp, half] = src[...]
    m.got(r.wqkv.at[:, other], i_share)

    wfull = r.wqkv[...].reshape(1024, 512)
    qg = r.meta[3:4, :]
    kg = r.meta[4:5, :]
    i_kv = m.take(4)
    i_kvx = m.take(4)
    i_kvf = m.take(4)

    def project(dz, x):
        x = x.astype(F32)
        r1 = lax.rsqrt(jnp.mean(x * x, axis=1, keepdims=True) + EPS)
        h = (x * r1 * gain1).astype(BF)
        r.h_all[dz] = h
        o = dot(h, wfull)
        cs, sn = r.cosr[dz], r.sinr[dz]
        r.qk_raw[dz] = o[:, 0:384]
        rot = []
        for b, gn in ((0, qg), (1, qg), (2, kg)):
            v = o[:, b * 128:(b + 1) * 128]
            v = v * lax.rsqrt(head_mean(v * v) + EPS) * gn
            rot.append(v * cs + swap_halves(v) * sn)
        for hd, v in enumerate(spread_heads(rot[0], rot[1])):
            r.qz[dz, pl.ds(hd * 128, 128), :] = v.astype(BF)
        i = 4 * z_of(dz) + p.g
        r.kv[i, :, 0:128] = rot[2].astype(BF)
        r.kv[i, :, 128:256] = o[:, 384:512].astype(BF)
        m.send(r.kv.at[i], r.kv.at[i], i_kvx + dz, p.xpeer())
        m.send(r.kv.at[i], r.kv.at[i], i_kv + dz, p.sib())

    project(0, r.tok[...])
    for dz in (1, 3, 2):
        m.got(r.tok_all.at[dz], i_tok + dz)
        project(dz, r.tok_all[dz])
    i_cot = m.take(4)
    for dz in (1, 3, 2):
        m.send(r.cot, r.cot_all.at[dz], i_cot + dz, p.zpeer(dz))
    r.cot_all[0] = r.cot[...]
    gs = p.g + 1 - 2 * p.c
    gx = (1 - p.xh) * 2 + p.c
    gxs = (1 - p.xh) * 2 + 1 - p.c
    for dz in (0, 1, 3, 2):
        zz = 4 * z_of(dz)
        m.got(r.kv.at[zz + gx], i_kvx + dz)
        m.send(r.kv.at[zz + gx], r.kv.at[zz + gx], i_kvf + dz, p.sib())
    for dz in (0, 1, 3, 2):
        zz = 4 * z_of(dz)
        m.got(r.kv.at[zz + gs], i_kv + dz)
        m.got(r.kv.at[zz + gxs], i_kvf + dz)

    def turn(j, carry):
        r.kt[j] = jnp.transpose(r.kv[j, :, 0:128].astype(F32)).astype(BF)
        r.vt[j] = jnp.transpose(r.kv[j, :, 128:256].astype(F32)).astype(BF)
        return carry

    lax.fori_loop(0, 16, turn, 0)

    def allowed_rows(i):
        row = r.st[pl.ds(i, 1), :].astype(jnp.int32)
        qi = lax.broadcasted_iota(jnp.int32, (1, 128), 1) + i * 128
        return jnp.concatenate([row] * 4, axis=1), jnp.concatenate([qi] * 4, axis=1)

    def weights_of(kb, qv, row4, qi4):
        s = dot(r.kv[kb, :, 0:128], qv, NT)
        ki = lax.broadcasted_iota(jnp.int32, (128, 512), 0) + kb * 128
        return jnp.where((ki >= row4) & (ki <= qi4), jnp.exp2(s * (SCALE * LOG2E)), 0.0)

    def forward_chunk(j, carry):
        dz = rem(j + 1, 4)
        i = 4 * z_of(dz) + p.g
        row4, qi4 = allowed_rows(i)
        r.acc[...] = jnp.zeros_like(r.acc)
        r.lacc[...] = jnp.zeros_like(r.lacc)
        qv = r.qz[dz]

        def body(kb, inner):
            w = weights_of(kb, qv, row4, qi4)
            r.lacc[...] += jnp.sum(w.reshape(16, 8, 512), axis=0)
            r.acc[...] += dot(r.vt[kb], w.astype(BF))
            return inner

        lax.fori_loop(jnp.maximum(i - 8, 0), i + 1, body, 0)
        il = 1.0 / jnp.sum(r.lacc[...], axis=0, keepdims=True)
        r.invl[dz] = jnp.broadcast_to(il, (8, 512))
        o = r.acc[...] * il
        full = jnp.concatenate(
            [o[(h // 2) * 64:(h // 2) * 64 + 64, h * 128:(h + 1) * 128] for h in range(4)], axis=0
        )
        r.oT[dz] = full
        r.o_s[dz] = jnp.transpose(full).astype(BF)
        return carry

    i_o = m.take(4)
    for j in range(4):
        forward_chunk(j, 0)
        dz = (j + 1) % 4
        if dz:
            m.send(r.o_s.at[dz], r.o_in.at[p.z], i_o + dz, p.zpeer(-dz))
        else:
            r.o_in[p.z] = r.o_s[0]

    m.local(r.wo_v.at[0, half], r.wo_v.at[0, half], i_wo).wait()
    for k in range(1, 8):
        m.got(r.wo_v.at[dps[k], half], i_wo + k)
    m.send(r.wo_v.at[:, half], r.wo_v.at[:, half], i_share + 1, p.sib())
    for dz in range(1, 4):
        m.got(r.o_in.at[rem(p.z + dz, 4)], i_o + dz)
    for j in range(4):
        r.o_own[:, j * 256:(j + 1) * 256] = r.o_in[j]
    m.got(r.wo_v.at[:, other], i_share + 1)
    x0 = r.tok[...].astype(F32)
    middle = x0 + dot(r.o_own[...], r.wo_v[...].reshape(1024, 1024))
    r.mid[...] = middle
    r2 = lax.rsqrt(jnp.mean(middle * middle, axis=1, keepdims=True) + EPS)
    r.h2[0] = (middle * r2 * gain2).astype(BF)
    i_h2 = m.take(4)
    for dz in (2, 1, 3):
        m.send(r.h2.at[0], r.h2.at[dz], i_h2 + dz, p.zpeer(dz))

    pltpu.make_async_copy(r.wd_v.at[:, pl.ds(0, 32)], r.wd_v.at[:, pl.ds(0, 32)], rsem.at[i_wd]).wait()
    h32 = pl.ds(pl.multiple_of(c32, 32), 32)
    o32 = pl.ds(pl.multiple_of(32 - c32, 32), 32)
    m.send(r.wd_v.at[:, h32], r.wd_v.at[:, h32], i_share + 2, p.sib())
    for n, (dst, i) in enumerate(((r.wg_v, i_wg), (r.wu_v, i_wu))):
        for k in range(1, 8):
            m.got(dst.at[dps[k], half], i + k)
        m.send(dst.at[:, half], dst.at[:, half], i_share + 3 + n, p.sib())
    for dz in range(1, 4):
        m.got(r.cot_all.at[dz], i_cot + dz)
    m.got(r.wd_v.at[:, o32], i_share + 2)
    wd = r.wd_v[...].reshape(1152, 1024)
    cots = r.cot_all[...].reshape(512, 1024)

    def cols384(t):
        return pl.ds(pl.multiple_of(t * 384, 128), 384)

    def dm_tile(t, carry):
        w = r.wd_v[pl.ds(t * 6, 6)].reshape(384, 1024)
        r.dm[:, :, cols384(t)] = dot(cots, w, NT).reshape(4, 128, 384)
        return carry

    lax.fori_loop(0, 3, dm_tile, 0)
    m.got(r.wg_v.at[:, other], i_share + 3)
    m.got(r.wu_v.at[:, other], i_share + 4)

    i_p2 = m.take(4)
    for pair in range(2):
        two = slice(2 * pair, 2 * pair + 2)
        for dz in ((1,), (2, 3))[pair]:
            m.got(r.h2.at[dz], i_h2 + dz)
        hh = r.h2[two].reshape(256, 1024)

        def ffn_tile(t, carry):
            cols = cols384(t)
            gate = dot(hh, r.wg_v[:, :, cols].reshape(1024, 384))
            up = dot(hh, r.wu_v[:, :, cols].reshape(1024, 384))
            sig = 1.0 / (1.0 + jnp.exp(-gate))
            act = gate * sig
            dmt = r.dm[two, :, cols].reshape(256, 384)
            r.mixed[two, :, cols] = (act * up).astype(BF).reshape(2, 128, 384)
            r.dg[two, :, cols] = (dmt * up * sig * (1.0 + gate * (1.0 - sig))).astype(BF).reshape(2, 128, 384)
            r.du[two, :, cols] = (dmt * act).astype(BF).reshape(2, 128, 384)
            return carry

        lax.fori_loop(0, 3, ffn_tile, 0)
        part = dot(r.dg[two].reshape(256, 1152), r.wg_v[...].reshape(1024, 1152), NT)
        part += dot(r.du[two].reshape(256, 1152), r.wu_v[...].reshape(1024, 1152), NT)
        if pair == 0:
            r.own[...] = part[0:128]
            r.p2s[0] = part[128:256].astype(BF)
            m.send(r.p2s.at[0], r.p2r.at[0], i_p2 + 1, p.zpeer(-1))
        else:
            r.p2s[1] = part[0:128].astype(BF)
            m.send(r.p2s.at[1], r.p2r.at[1], i_p2 + 2, p.zpeer(-2))
            r.p2s[2] = part[128:256].astype(BF)
            m.send(r.p2s.at[2], r.p2r.at[2], i_p2 + 3, p.zpeer(-3))

    i_r1 = m.take(3)
    h2t = r.h2[...].reshape(512, 1024)

    def gate_up_tile(t, carry):
        cols = cols384(t)
        r.gF[:, :, cols] = dot(h2t, r.dg[:, :, cols].reshape(512, 384), TN).astype(BF).reshape(8, 128, 384)
        r.gF[:, :, cols384(t + 3)] = dot(h2t, r.du[:, :, cols].reshape(512, 384), TN).astype(BF).reshape(8, 128, 384)
        return carry

    lax.fori_loop(0, 3, gate_up_tile, 0)
    m.send(r.gF.at[:, other], r.r1F, i_r1, p.sib())

    def down_tile(t, carry):
        w = r.mixed[:, :, cols384(t)].reshape(512, 384)
        r.gD[pl.ds(t * 6, 6)] = dot(w, cots, TN).astype(BF).reshape(6, 64, 1024)
        return carry

    lax.fori_loop(0, 3, down_tile, 0)
    m.send(r.gD.at[:, o32], r.r1D, i_r1 + 1, p.sib())
    r.own3[...] = dot(r.mixed[0], wd)

    def out_chunk(dz, carry):
        r.p3s[dz - 1] = dot(r.mixed[dz], wd).astype(BF)
        return carry

    lax.fori_loop(1, 4, out_chunk, 0)

    for dz in range(1, 4):
        m.got(r.p2r.at[dz - 1], i_p2 + dz)
    dh2 = r.own[...] + r.p2r[0].astype(F32) + r.p2r[1].astype(F32) + r.p2r[2].astype(F32)
    middle = r.mid[...]
    r2 = lax.rsqrt(jnp.mean(middle * middle, axis=1, keepdims=True) + EPS)
    small2 = jnp.sum(dh2 * middle * r2, axis=0, keepdims=True)
    wdh = dh2 * gain2
    dmid = r.cot[...].astype(F32) + r2 * wdh - middle * (r2 * r2 * r2) * jnp.mean(wdh * middle, axis=1, keepdims=True)
    r.dmid[...] = dmid
    r.da[...] = dmid.astype(BF)
    r.dob[...] = dot(r.da[...], r.wo_v[...].reshape(1024, 1024), NT).astype(BF)
    i_do = m.take(4)

    def zcols(z):
        return pl.ds(pl.multiple_of(z * 256, 256), 256)

    for dz in (2, 1, 3):
        m.send(r.dob.at[:, zcols(rem(p.z + dz, 4))], r.do_all.at[dz], i_do + dz, p.zpeer(dz))
    r.do_all[0] = r.dob[:, zq]
    i_p3 = m.take(4)
    i_of = m.take(4)
    i_dc = m.take(4)
    for dz in (2, 1, 3):
        m.send(r.o_own, r.o_full.at[dz], i_of + dz, p.zpeer(dz))
        m.send(r.da.at[:, zcols(rem(p.z + dz, 4))], r.da_c.at[dz], i_dc + dz, p.zpeer(dz))
    for dz in (2, 1, 3):
        m.send(r.p3s.at[dz - 1], r.p3r.at[dz - 1], i_p3 + dz, p.zpeer(-dz))
    r.o_full[0] = r.o_own[...]
    r.da_c[0] = r.da[:, zq]

    m.got(r.r1F, i_r1)
    m.got(r.r1D, i_r1 + 1)

    def add_core(d, carry):
        r.r1F[d] = (r.r1F[d].astype(F32) + r.gF[d, half].astype(F32)).astype(BF)
        return carry

    lax.fori_loop(0, 8, add_core, 0)

    def add_core_down(d, carry):
        r.r1D[d] = (r.r1D[d].astype(F32) + r.gD[d, h32].astype(F32)).astype(BF)
        return carry

    lax.fori_loop(0, 18, add_core_down, 0)
    i_r2 = m.take(16)
    i_r2d = m.take(16)
    i_r2e = m.take(16)

    def slots():
        for t in range(2):
            for k in range(8):
                yield t * 8 + k, t, k

    def target(t, k):
        return p.dpeer(k) if t == 0 else far[k]

    def rows32(t):
        x = p.xh if t == 0 else 1 - p.xh
        return pl.ds(pl.multiple_of(x * 32, 32), 32), pl.ds(pl.multiple_of(x * 16, 16), 16)

    for s, t, k in slots():
        d = rem(p.dp + k, 8)
        r32, r16 = rows32(t)
        two, more, cond = down_pieces(d)
        if s == 0:
            r.r2F[0] = r.r1F[d, r32]
            for n in range(2):
                r.r2D[0, n] = r.r1D[two[n][1], r16]

            @pl.when(cond)
            def _():
                r.r2D[0, 2] = r.r1D[more[1], r16]

            continue
        m.send(r.r1F.at[d, r32], r.r2F.at[s], i_r2 + s, target(t, k))
        for n in range(2):
            m.copy(r.r1D.at[two[n][1], r16], r.r2D.at[s, n], i_r2d + s, target(t, k)).start()
        m.sent.append((r.r2D.at[0, pl.ds(0, 2)], i_r2d + s))

        @pl.when(cond)
        def _():
            m.copy(r.r1D.at[more[1], r16], r.r2D.at[s, 2], i_r2e + s, target(t, k)).start()

    r.dkv[...] = jnp.zeros_like(r.dkv)
    for dz in (0, 1, 3, 2):
        if dz:
            m.got(r.do_all.at[dz], i_do + dz)

    def backward_chunk(j, carry):
        dz = j
        i = 4 * z_of(dz) + p.g
        row4, qi4 = allowed_rows(i)
        do = r.do_all[dz].astype(F32)
        for hd, v in enumerate(spread_heads(do[:, 0:128], do[:, 128:256])):
            r.doz[pl.ds(hd * 128, 128), :] = v.astype(BF)
        prod = jnp.transpose(do) * r.oT[dz]
        drow = jnp.concatenate(
            [jnp.sum(prod[h * 64:(h + 1) * 64], axis=0, keepdims=True) for h in range(4)], axis=1
        )
        il = r.invl[dz, 0:1, :]
        qv = r.qz[dz]
        dov = r.doz[...]
        r.acc[...] = jnp.zeros_like(r.acc)

        def body(kb, inner):
            w = weights_of(kb, qv, row4, qi4) * il
            dp = dot(r.kv[kb, :, 128:256], dov, NT)
            ds = (w * (dp - drow)).astype(BF)
            r.acc[...] += dot(r.kt[kb], ds)
            r.dkv[kb, :, 0:128] += dot(ds, qv)
            r.dkv[kb, :, 128:256] += dot(w.astype(BF), dov)
            return inner

        lax.fori_loop(jnp.maximum(i - 8, 0), i + 1, body, 0)
        o = r.acc[...] * SCALE
        full = jnp.concatenate(
            [o[(h // 2) * 64:(h // 2) * 64 + 64, h * 128:(h + 1) * 128] for h in range(4)], axis=0
        )
        r.dqr[dz] = jnp.transpose(full)
        return carry

    lax.fori_loop(0, 4, backward_chunk, 0)

    lane = lax.broadcasted_iota(jnp.int32, (1, 256), 1)
    kscale = jnp.where(lane < 128, SCALE, 1.0)
    r.dkvb[...] = (r.dkv[...] * kscale.reshape(1, 1, 256)).astype(BF).reshape(4, 4, 128, 256)
    i_dkv = m.take(3)
    xs = (p.dp, p.z * 4 + gxs)
    m.send(r.dkvb.at[:, gx], r.dkvr.at[1], i_dkv + 1, p.xpeer())
    m.send(r.dkvb.at[:, gxs], r.dkvr.at[2], i_dkv + 2, xs)
    m.send(r.dkvb.at[:, gs], r.dkvr.at[0], i_dkv, p.sib())

    for dz in range(1, 4):
        m.got(r.o_full.at[dz], i_of + dz)
        m.got(r.da_c.at[dz], i_dc + dz)
        m.got(r.p3r.at[dz - 1], i_p3 + dz)
    r.gA[:, :, 512:768] = dot(
        r.o_full[...].reshape(512, 1024), r.da_c[...].reshape(512, 256), TN
    ).astype(BF).reshape(8, 128, 256)
    r.block_out[...] = (
        r.mid[...] + r.own3[...] + r.p3r[0].astype(F32) + r.p3r[1].astype(F32) + r.p3r[2].astype(F32)
    ).astype(BF)

    def got_ffn():
        for s, t, k in slots():
            if s == 0:
                continue
            m.got(r.r2F.at[s], i_r2 + s)
            m.got(r.r2D.at[s, pl.ds(0, 2)], i_r2d + s)
        mine = lax.div(p.dp, 2) == p.z

        @pl.when(mine)
        def _():
            for s, t, k in slots():
                if s:
                    m.got(r.r2D.at[s, 2], i_r2e + s)

        def add(s, total):
            return total + r.r2F[s].astype(F32)

        r.oF[...] = lax.fori_loop(1, 16, add, r.r2F[0].astype(F32)).astype(BF)

        def addd(s, total):
            return total + r.r2D[s, 0:2].astype(F32)

        r.oD[0:2] = lax.fori_loop(1, 16, addd, r.r2D[0, 0:2].astype(F32)).astype(BF)

        @pl.when(mine)
        def _():
            def adde(s, total):
                return total + r.r2D[s, 2].astype(F32)

            r.oD[2] = lax.fori_loop(1, 16, adde, r.r2D[0, 2].astype(F32)).astype(BF)

        @pl.when(jnp.logical_not(mine))
        def _():
            r.oD[2] = jnp.zeros((16, 1024), BF)

    got_ffn()

    def seq_at(z, g):
        return rem(z + 8, 4) * 4 + g

    class Gather:
        def __init__(self, own, buf):
            self.own, self.buf = own, buf
            self.il = m.take(1)
            self.ix, self.iz, self.izx, self.ic = m.take(1), m.take(4), m.take(4), m.take(8)

        def first(self):
            s = self.buf.at[p.sq]
            m.send(self.own, s, self.ix, p.xpeer())
            for dz in (2, 1, 3):
                m.send(self.own, s, self.iz + dz, p.zpeer(dz))
            m.send(self.own, s, self.ic, p.sib())
            m.local(self.own, s, self.il).start()

        def second(self):
            s = self.buf.at[seq_at(p.z, gx)]
            m.got(s, self.ix)
            for dz in (2, 1, 3):
                m.send(s, s, self.izx + dz, p.zpeer(dz))
            m.send(s, s, self.ic + 4, p.sib())

        def third(self):
            for dz in (1, 3, 2):
                s = self.buf.at[seq_at(p.z - dz, p.g)]
                m.got(s, self.iz + dz)
                m.send(s, s, self.ic + dz, p.sib())
            for dz in (1, 3, 2):
                s = self.buf.at[seq_at(p.z - dz, gx)]
                m.got(s, self.izx + dz)
                m.send(s, s, self.ic + 4 + dz, p.sib())

        def last(self):
            for dz in (0, 1, 3, 2):
                m.got(self.buf.at[seq_at(p.z - dz, gs)], self.ic + dz)
                m.got(self.buf.at[seq_at(p.z - dz, gxs)], self.ic + 4 + dz)
            m.local(self.own, self.buf.at[p.sq], self.il).wait()

    ag_f = Gather(r.oF, r.fF)
    ag_d = Gather(r.oD, r.fD)
    ag_a = Gather(r.oA, r.fA)

    for n in range(3):
        m.got(r.dkvr.at[n], i_dkv + n)
    sq_acc = jnp.zeros((1, 128), F32)
    sk_acc = jnp.zeros((1, 128), F32)
    for dz in range(4):
        zz = z_of(dz)
        i = 4 * zz + p.g
        dkv = r.dkv[i] * kscale
        for n in range(3):
            dkv = dkv + r.dkvr[n, zz].astype(F32)
        cs, sn = r.cosr[dz], r.sinr[dz]
        grads = (r.dqr[dz, :, 0:128], r.dqr[dz, :, 128:256], dkv[:, 0:128])
        for b, gr in enumerate(grads):
            gn = qg if b < 2 else kg
            v = r.qk_raw[dz, :, b * 128:(b + 1) * 128]
            f = lax.rsqrt(head_mean(v * v) + EPS)
            dn = gr * cs - swap_halves(gr) * sn
            add = jnp.sum(dn * v * f, axis=0, keepdims=True)
            if b < 2:
                sq_acc = sq_acc + add
            else:
                sk_acc = sk_acc + add
            wn = dn * gn
            r.dqkv[dz, :, b * 128:(b + 1) * 128] = (f * wn - v * (f * f * f) * head_mean(wn * v)).astype(BF)
        r.dqkv[dz, :, 384:512] = dkv[:, 128:256].astype(BF)
    i_p4 = m.take(4)
    for dz in (2, 1, 3):
        r.p4s[dz - 1] = dot(r.dqkv[dz], r.wqkv[...].reshape(1024, 512), NT).astype(BF)
        m.send(r.p4s.at[dz - 1], r.p4r.at[dz - 1], i_p4 + dz, p.zpeer(-dz))
    r.own[...] = dot(r.dqkv[0], r.wqkv[...].reshape(1024, 512), NT)
    r.gA[:, :, 0:512] = dot(
        r.h_all[...].reshape(512, 1024), r.dqkv[...].reshape(512, 512), TN
    ).astype(BF).reshape(8, 128, 512)
    m.send(r.gA.at[:, other], r.r1A, i_r1 + 2, p.sib())
    ag_f.first()
    ag_d.first()
    m.got(r.r1A, i_r1 + 2)
    r.r1A[...] = (r.r1A[...].astype(F32) + r.gA[:, half].astype(F32)).astype(BF)
    i_r2a = m.take(16)
    for s, t, k in slots():
        d = rem(p.dp + k, 8)
        r32, _ = rows32(t)
        if s == 0:
            r.r2A[0] = r.r1A[d, r32]
        else:
            m.send(r.r1A.at[d, r32], r.r2A.at[s], i_r2a + s, target(t, k))
    ag_f.second()
    ag_d.second()

    for dz in range(1, 4):
        m.got(r.p4r.at[dz - 1], i_p4 + dz)
    dh = r.own[...] + r.p4r[0].astype(F32) + r.p4r[1].astype(F32) + r.p4r[2].astype(F32)
    x0 = r.tok[...].astype(F32)
    r1 = lax.rsqrt(jnp.mean(x0 * x0, axis=1, keepdims=True) + EPS)
    small1 = jnp.sum(dh * x0 * r1, axis=0, keepdims=True)
    wdh = dh * gain1
    r.input_grad[...] = (
        r.dmid[...] + r1 * wdh - x0 * (r1 * r1 * r1) * jnp.mean(wdh * x0, axis=1, keepdims=True)
    ).astype(BF)

    both = lambda v: v + pltpu.roll(v, 64, 1)
    for d in range(8):
        cols = slice(d * 128, (d + 1) * 128)
        r.gsm[d] = jnp.concatenate(
            [small1[:, cols], small2[:, cols], both(sq_acc), both(sk_acc), jnp.zeros((4, 128), F32)], axis=0
        )
    i_s1 = m.take(8)
    i_s2 = m.take(16)
    for k in range(1, 8):
        m.send(r.gsm.at[rem(p.dp + k, 8)], r.gs1.at[k], i_s1 + k, p.dpeer(k))
    r.gs1[0] = r.gsm[p.dp]
    for k in range(1, 8):
        m.got(r.gs1.at[k], i_s1 + k)
    r.gs1s[...] = jnp.sum(r.gs1[...], axis=0)
    for k in range(1, 16):
        m.send(r.gs1s, r.gs2.at[k], i_s2 + k, p.speer(k))
    r.gs2[0] = r.gs1s[...]

    for s, t, k in slots():
        if s:
            m.got(r.r2A.at[s], i_r2a + s)

    def adda(s, total):
        return total + r.r2A[s].astype(F32)

    r.oA[...] = lax.fori_loop(1, 16, adda, r.r2A[0].astype(F32)).astype(BF)
    ag_a.first()
    ag_f.third()
    ag_d.third()
    ag_a.second()
    ag_a.third()
    for k in range(1, 16):
        m.got(r.gs2.at[k], i_s2 + k)
    r.g_small[...] = jnp.sum(r.gs2[...], axis=0)
    ag_f.last()
    ag_d.last()
    ag_a.last()

    m.finish()
    for k in range(1, 8):
        for n in range(2):
            down_copy(k, n, pieces[n]).wait_send()

    @pl.when(has_extra)
    def _():
        for k in range(1, 8):
            down_copy(k, 2, extra).wait_send()

    for s, t, k in slots():
        if s:
            _, more, cond = down_pieces(rem(p.dp + k, 8))

            @pl.when(cond)
            def _():
                m.copy(r.r1D.at[more[1], pl.ds(0, 16)], r.r2D.at[s, 2], i_r2e + s, p.sib()).wait_send()

    assert m.n <= NSEM, m.n


def block(args):
    vm = pl.BlockSpec(memory_space=pltpu.VMEM)
    hb = pl.BlockSpec(memory_space=pl.ANY)
    return pl.pallas_call(
        kernel,
        out_shape=tuple(jax.ShapeDtypeStruct(s, d) for s, d in OUTPUTS.values()),
        in_specs=[vm, vm] + [hb] * 7 + [vm],
        out_specs=tuple(hb if name[0] == "f" else vm for name in OUTPUTS),
        scratch_shapes=[pltpu.VMEM(s, d) for s, d in SCRATCH.values()]
        + [pltpu.SemaphoreType.DMA((NSEM,)), pltpu.SemaphoreType.DMA((NSEM,))],
        compiler_params=pltpu.CompilerParams(
            collective_id=0, has_side_effects=True, vmem_limit_bytes=63 * 2**20
        ),
        name="block",
    )(*args)


LAID = {
    "g_gate": (128, 4608),
    "g_up": (128, 4608),
    "g_down": (576, 1024),
    "g_q": (128, 1024),
    "g_k": (128, 512),
    "g_v": (128, 512),
    "g_out": (128, 1024),
}


def lay_kernel(f_f, f_d, f_a, g_gate, g_up, g_down, g_q, g_k, g_v, g_out):
    p = Place()

    def lay(s, carry):
        z = lax.div(s, 4)
        g = rem(s, 4)
        row = pl.ds(pl.multiple_of(rem(g, 2) * 64 + lax.div(g, 2) * 32, 32), 32)
        for t in range(9):
            cols = pl.ds(pl.multiple_of(t * 512 + z * 128, 128), 128)
            g_gate[row, cols] = f_f[s, :, t * 128:(t + 1) * 128].astype(F32)
            g_up[row, cols] = f_f[s, :, 1152 + t * 128:1152 + (t + 1) * 128].astype(F32)
        c256 = pl.ds(pl.multiple_of(z * 256, 256), 256)
        c128 = pl.ds(pl.multiple_of(z * 128, 128), 128)
        g_q[row, c256] = f_a[s, :, 0:256].astype(F32)
        g_k[row, c128] = f_a[s, :, 256:384].astype(F32)
        g_v[row, c128] = f_a[s, :, 384:512].astype(F32)
        g_out[row, c256] = f_a[s, :, 512:768].astype(F32)
        sub = rem(g, 2) * 32 + lax.div(g, 2) * 16
        for n in range(2):
            u = rem(2 * z + n - p.dp + 8, 8)
            g_down[pl.ds(pl.multiple_of(u * 64 + sub, 16), 16), :] = f_d[s, n].astype(F32)

        @pl.when(lax.div(p.dp, 2) == z)
        def _():
            g_down[pl.ds(pl.multiple_of(8 * 64 + sub, 16), 16), :] = f_d[s, 2].astype(F32)

        return carry

    lax.fori_loop(0, 16, lay, 0)


def lay_out(f_f, f_d, f_a):
    vm = pl.BlockSpec(memory_space=pltpu.VMEM)
    o = pl.pallas_call(
        lay_kernel,
        out_shape=tuple(jax.ShapeDtypeStruct(s, F32) for s in LAID.values()),
        in_specs=[vm] * 3,
        out_specs=tuple(vm for _ in LAID),
        compiler_params=pltpu.CompilerParams(vmem_limit_bytes=40 * 2**20),
        name="lay",
    )(f_f, f_d, f_a)
    return dict(zip(LAID, o))


def local(
    tokens, segment_ids, attn_gain, w_query, w_key, w_value, w_out, ffn_gain, w_gate, w_up, w_down,
    query_gain, key_gain, cotangent,
):
    inverse = ROPE_BASE ** (-(np.arange(32).astype(np.float32) * np.float32(2.0) / np.float32(64)))
    freq = jnp.asarray(np.tile(inverse.astype(np.float32), 4)[None])
    meta = jnp.concatenate(
        [
            attn_gain.astype(F32)[None],
            ffn_gain.astype(F32)[None],
            segment_ids.astype(F32),
            jnp.tile(query_gain.astype(F32), 2)[None],
            jnp.tile(key_gain.astype(F32), 2)[None],
            freq,
            jnp.zeros((2, 128), F32),
        ],
        axis=0,
    )
    o = block((tokens, meta, w_query, w_key, w_value, w_out, w_gate, w_up, w_down, cotangent))
    o = dict(zip(OUTPUTS, o))
    small = o["g_small"]
    w = lay_out(o["fF"], o["fD"], o["fA"])
    return (
        o["block_out"], o["input_grad"], small[0], w["g_q"], w["g_k"], w["g_v"], w["g_out"], small[1],
        w["g_gate"], w["g_up"], w["g_down"], small[2, :64], small[3, :64],
    )


def solution(mesh):
    both = ("dp", "seq")
    w = P("dp", None)
    return jax.shard_map(
        local,
        mesh=mesh,
        in_specs=(P(both, None), P("dp", "seq"), P("dp"), w, w, w, w, P("dp"), w, w, w, P(), P(), P(both, None)),
        out_specs=(P(both, None), P(both, None), P("dp"), w, w, w, w, P("dp"), w, w, w, P(), P()),
        check_vma=False,
    )
```

```python
import math

import jax
import jax.numpy as jnp
import numpy as np
from jax import lax
from jax.experimental import pallas as pl
from jax.experimental.pallas import tpu as pltpu
from jax.sharding import PartitionSpec as P

MESH = pl.DeviceIdType.MESH
F32 = jnp.float32
BF = jnp.bfloat16
EPS = 1e-05
ROPE_BASE = 1000000.0
NN = (((1,), (0,)), ((), ()))
NT = (((1,), (1,)), ((), ()))
TN = (((0,), (0,)), ((), ()))
SCALE = 0.125
LOG2E = math.log2(math.e)


def dot(a, b, dims=NN, precision=None):
    return lax.dot_general(a, b, dims, preferred_element_type=F32, precision=precision)


def rem(a, b):
    return lax.rem(a, b)


class Place:
    def __init__(self):
        self.dp = lax.axis_index("dp")
        self.sq = lax.axis_index("seq")
        self.y = lax.div(self.dp, 2)
        self.xl = rem(self.dp, 2)
        self.z = lax.div(self.sq, 4)
        self.g = rem(self.sq, 4)
        self.xh = lax.div(self.g, 2)
        self.c = rem(self.sq, 2)

    def zpeer(self, dz):
        return (self.dp, rem(self.z + dz + 4, 4) * 4 + self.g)

    def sib(self):
        return (self.dp, self.sq + 1 - 2 * self.c)

    def xpeer(self):
        return (self.dp, self.z * 4 + (1 - self.xh) * 2 + self.c)

    def dpeer(self, k):
        return (rem(self.dp + k + 8, 8), self.sq)

    def speer(self, k):
        return (self.dp, rem(self.sq + k + 16, 16))

    def ypeer(self, k):
        return (rem(self.y + k + 4, 4) * 2 + self.xl, self.sq)

    def xring(self, t):
        xl = self.xl if t == 3 else 1 - self.xl
        return (self.y * 2 + xl, self.sq if t == 1 else self.z * 4 + (1 - self.xh) * 2 + self.c)

    def xplace(self, t):
        return (self.xl if t in (0, 3) else 1 - self.xl), (self.xh if t in (0, 1) else 1 - self.xh)


def seg_rows(ids):
    start = jnp.zeros_like(ids)
    for j in range(1, 8):
        below = jnp.sum(jnp.where(ids < j, 1.0, 0.0), keepdims=True)
        start = jnp.where(ids == j, below, start)
    return start


def lane_half():
    return lax.rem(lax.broadcasted_iota(jnp.int32, (1, 128), 1), 64) < 32


def swap_halves(x):
    return jnp.where(lane_half(), pltpu.roll(x, 96, 1), pltpu.roll(x, 32, 1))


def head_mean(x):
    a = lax.div(lax.broadcasted_iota(jnp.int32, (128, 128), 0), 64)
    b = lax.div(lax.broadcasted_iota(jnp.int32, (128, 128), 1), 64)
    block = jnp.where(a == b, 1.0 / 64, 0.0)
    return dot(x, block, NN, lax.Precision.HIGHEST)


def spread_heads(first, second):
    lo = lax.broadcasted_iota(jnp.int32, (1, 128), 1) < 64
    return [
        jnp.where(lo, first, 0.0),
        jnp.where(lo, pltpu.roll(first, 64, 1), 0.0),
        jnp.where(lo, 0.0, pltpu.roll(second, 64, 1)),
        jnp.where(lo, 0.0, second),
    ]


INPUTS = ["tok", "seg", "ga", "gf", "gqk", "freq", "wq", "wk", "wv", "wo", "wg", "wu", "wd", "cot"]
OUTPUTS = {
    "block_out": ((128, 1024), BF),
    "input_grad": ((128, 1024), BF),
    "fF": ((16, 32, 2304), BF),
    "fD": ((16, 3, 16, 1024), BF),
    "fA": ((16, 32, 768), BF),
    "g_small": ((8, 128), F32),
}
SCRATCH = {
    "tok_all": ((4, 128, 1024), BF),
    "cot_all": ((4, 128, 1024), BF),
    "meta": ((8, 128), F32),
    "mseq": ((16, 8, 128), F32),
    "mdp": ((8, 8, 128), F32),
    "wqkv": ((8, 128, 512), BF),
    "wo_v": ((8, 128, 1024), BF),
    "wg_v": ((8, 128, 1152), BF),
    "wu_v": ((8, 128, 1152), BF),
    "wd_v": ((18, 64, 1024), BF),
    "st": ((16, 128), F32),
    "qk_raw": ((4, 128, 384), F32),
    "qz": ((4, 512, 128), BF),
    "kv": ((16, 128, 256), BF),
    "kt": ((16, 128, 128), BF),
    "vt": ((16, 128, 128), BF),
    "cosr": ((4, 128, 128), F32),
    "sinr": ((4, 128, 128), F32),
    "invl": ((4, 8, 512), F32),
    "oT": ((4, 256, 128), F32),
    "acc": ((128, 512), F32),
    "lacc": ((8, 512), F32),
    "o_s": ((4, 128, 256), BF),
    "o_in": ((4, 128, 256), BF),
    "o_own": ((128, 1024), BF),
    "o_full": ((4, 128, 1024), BF),
    "mid": ((128, 1024), F32),
    "h2": ((4, 128, 1024), BF),
    "dm": ((4, 128, 1152), F32),
    "mixed": ((4, 128, 1152), BF),
    "dg": ((4, 128, 1152), BF),
    "du": ((4, 128, 1152), BF),
    "p2s": ((3, 128, 1024), BF),
    "p2r": ((3, 128, 1024), BF),
    "own": ((128, 1024), F32),
    "p3s": ((3, 128, 1024), BF),
    "p3r": ((3, 128, 1024), BF),
    "own3": ((128, 1024), F32),
    "dmid": ((128, 1024), F32),
    "da": ((128, 1024), BF),
    "da_c": ((4, 128, 256), BF),
    "dob": ((128, 1024), BF),
    "do_all": ((4, 128, 256), BF),
    "doz": ((512, 128), BF),
    "dkv": ((16, 128, 256), F32),
    "dkvb": ((4, 4, 128, 256), BF),
    "dkvr": ((3, 4, 128, 256), BF),
    "dqr": ((4, 128, 256), F32),
    "dqkv": ((4, 128, 512), BF),
    "p4r": ((3, 128, 1024), BF),
    "gF": ((4, 2, 128, 2304), BF),
    "gD": ((18, 64, 1024), BF),
    "gA": ((4, 2, 128, 768), BF),
    "r1F": ((4, 2, 64, 2304), BF),
    "r1D": ((18, 32, 1024), BF),
    "sD": ((4, 2, 2, 32, 1024), BF),
    "sX": ((2, 32, 1024), BF),
    "ax": ((3, 4, 32, 1152), BF),
    "at": ((4, 32, 1152), BF),
    "ay": ((3, 32, 1152), BF),
    "by": ((3, 2, 64, 1152), BF),
    "bt": ((2, 64, 1152), BF),
    "bx": ((3, 32, 1152), BF),
    "adx": ((3, 4, 2, 16, 512), BF),
    "adt": ((4, 2, 16, 512), BF),
    "ady": ((3, 2, 16, 512), BF),
    "bdy": ((3, 2, 2, 32, 512), BF),
    "bdt": ((2, 2, 32, 512), BF),
    "bdx": ((3, 2, 16, 512), BF),
    "xx": ((3, 16, 1024), BF),
    "xt": ((16, 1024), BF),
    "xy": ((3, 16, 1024), BF),
    "qax": ((3, 4, 32, 384), BF),
    "qat": ((4, 32, 384), BF),
    "qay": ((3, 32, 384), BF),
    "qby": ((3, 2, 64, 384), BF),
    "qbt": ((2, 64, 384), BF),
    "qbx": ((3, 32, 384), BF),
    "r1A": ((4, 2, 64, 768), BF),
    "oF": ((32, 2304), BF),
    "oD": ((3, 16, 1024), BF),
    "oA": ((32, 768), BF),
    "gsm": ((8, 8, 128), F32),
    "gs1": ((8, 8, 128), F32),
    "gs1s": ((8, 128), F32),
    "gs2": ((16, 8, 128), F32),
}
NSEM = 400


class Refs:
    pass


class Comm:
    def __init__(self, place, ssem, rsem):
        self.p, self.ssem, self.rsem = place, ssem, rsem
        self.n = 0
        self.sent = []

    def take(self, count=1):
        base = self.n
        self.n += count
        return base

    def copy(self, src, dst, i, dev):
        return pltpu.make_async_remote_copy(
            src_ref=src, dst_ref=dst, send_sem=self.ssem.at[i], recv_sem=self.rsem.at[i],
            device_id=dev, device_id_type=MESH,
        )

    def send(self, src, dst, i, dev):
        self.copy(src, dst, i, dev).start()
        self.sent.append((src, i))

    def local(self, src, dst, i):
        return pltpu.make_async_copy(src, dst, self.rsem.at[i])

    def got(self, dst, i):
        self.copy(dst, dst, i, self.p.sib()).wait_recv()

    def flush(self, i):
        for src, j in self.sent:
            if j == i:
                self.copy(src, src, i, self.p.sib()).wait_send()
        self.sent = [e for e in self.sent if e[1] != i]

    def finish(self):
        for src, i in self.sent:
            self.copy(src, src, i, self.p.sib()).wait_send()
        self.sent = []


def kernel(*refs):
    r = Refs()
    names = INPUTS + list(OUTPUTS) + list(SCRATCH)
    for name, ref in zip(names, refs):
        setattr(r, name, ref)
    ssem, rsem = refs[len(names):]
    p = Place()
    m = Comm(p, ssem, rsem)

    def z_of(dz):
        return rem(p.z - dz + 4, 4)

    half = pl.ds(pl.multiple_of(p.c * 64, 64), 64)
    other = pl.ds(pl.multiple_of(64 - p.c * 64, 64), 64)
    zq = pl.ds(pl.multiple_of(p.z * 256, 256), 256)
    zk = pl.ds(pl.multiple_of(p.z * 128, 128), 128)
    dps = [rem(p.dp + 8 - k, 8) for k in range(8)]

    i_loc = m.take(4)
    parts = ((r.wq, zq, 0, 256), (r.wk, zk, 256, 128), (r.wv, zk, 384, 128))
    for w, cols, at, wid in parts:
        m.local(w.at[half, cols], r.wqkv.at[p.dp, half, pl.ds(at, wid)], i_loc).start()
    m.local(r.wo.at[half], r.wo_v.at[p.dp, half], i_loc + 1).start()

    def down_pieces(d):
        out = []
        for n in range(2):
            u = rem(2 * p.z + n - d + 8, 8)
            big = 9 * d + u
            out.append((u, 2 * lax.div(big, 8) + rem(big, 2)))
        big = 9 * d + 8
        return out + [(8, 2 * lax.div(big, 8) + rem(big, 2))], lax.div(d, 2) == p.z

    c32 = p.c * 32
    h32 = pl.ds(pl.multiple_of(c32, 32), 32)
    o32 = pl.ds(pl.multiple_of(32 - c32, 32), 32)
    i_ld = m.take(3)
    pieces, has_extra = down_pieces(p.dp)

    def down_local(n):
        u, hidx = pieces[n]
        src = r.wd.at[pl.ds(pl.multiple_of(u * 64 + c32, 32), 32)]
        return pltpu.make_async_copy(src, r.wd_v.at[hidx, h32], rsem.at[i_ld + n])

    for n in range(2):
        down_local(n).start()

    @pl.when(has_extra)
    def _():
        down_local(2).start()

    for src, dst, i in ((r.wg, r.wg_v, i_loc + 2), (r.wu, r.wu_v, i_loc + 3)):
        for t in range(9):
            cols = pl.ds(pl.multiple_of(t * 512 + p.z * 128, 128), 128)
            m.local(src.at[half, cols], dst.at[p.dp, half, pl.ds(t * 128, 128)], i).start()

    r.meta[0:1, :] = r.ga[...].astype(F32)
    r.meta[1:2, :] = r.gf[...].astype(F32)
    r.meta[2:3, :] = r.seg[...].astype(F32)
    r.meta[3:8, :] = jnp.zeros((5, 128), F32)

    bar = pltpu.get_barrier_semaphore()
    for k in range(1, 16):
        pl.semaphore_signal(bar, inc=1, device_id=p.speer(k), device_id_type=MESH)
    for k in range(1, 8):
        pl.semaphore_signal(bar, inc=1, device_id=p.dpeer(k), device_id_type=MESH)
    pl.semaphore_signal(bar, inc=1, device_id=p.xring(2), device_id_type=MESH)
    pl.semaphore_wait(bar, 23)

    class Shards:
        def __init__(self, buf, i_share):
            self.buf, self.share = buf, i_share
            self.iy, self.ix = m.take(4), m.take(8)

        def row(self, k, xl):
            return rem(p.y - k + 4, 4) * 2 + xl

        def quarter(self, t):
            return pl.ds(pl.multiple_of(p.c * 64 + (t - 1) * 32, 32), 32)

        def along_y(self):
            s = self.buf.at[p.dp, half]
            for k in (2, 1, 3):
                m.send(s, s, self.iy + k, p.ypeer(k))

        def along_x(self, k):
            d = self.row(k, p.xl)
            if k:
                m.got(self.buf.at[d, half], self.iy + k)
            for t in (1, 2):
                s = self.buf.at[d, self.quarter(t)]
                m.send(s, s, self.ix + 2 * k + t - 1, p.xring(t))

        def to_core(self):
            for k in range(4):
                d = self.row(k, 1 - p.xl)
                for t in (1, 2):
                    m.got(self.buf.at[d, self.quarter(t)], self.ix + 2 * k + t - 1)
            s = self.buf.at[:, half]
            m.send(s, s, self.share, p.sib())

        def done(self):
            m.got(self.buf.at[:, other], self.share)

    class Down:
        def __init__(self, i_share):
            self.share = i_share
            self.iy, self.ix = m.take(12), m.take(24)

        def move(self, d, t, i, dev, act):
            where, more = down_pieces(d)
            for n in range(3):
                rows = h32 if t == 0 else pl.ds(pl.multiple_of(c32 + (t - 1) * 16, 16), 16)
                s = r.wd_v.at[where[n][1], rows]
                if n < 2:
                    act(m.copy(s, s, i + n, dev))
                else:

                    @pl.when(more)
                    def _():
                        act(m.copy(s, s, i + n, dev))

        def along_y(self):
            for k in (2, 1, 3):
                self.move(p.dp, 0, self.iy + 3 * k, p.ypeer(k), lambda q: q.start())

        def along_x(self, k):
            d = rem(p.y - k + 4, 4) * 2 + p.xl
            if k:
                self.move(d, 0, self.iy + 3 * k, p.sib(), lambda q: q.wait_recv())
            for t in (1, 2):
                self.move(d, t, self.ix + 6 * k + 3 * (t - 1), p.xring(t), lambda q: q.start())

        def to_core(self):
            for k in range(4):
                d = rem(p.y - k + 4, 4) * 2 + 1 - p.xl
                for t in (1, 2):
                    self.move(d, t, self.ix + 6 * k + 3 * (t - 1), p.sib(), lambda q: q.wait_recv())
            m.send(r.wd_v.at[:, h32], r.wd_v.at[:, h32], self.share, p.sib())

        def done(self):
            m.got(r.wd_v.at[:, o32], self.share)

        def finish(self):
            for k in (1, 2, 3):
                self.move(p.dp, 0, self.iy + 3 * k, p.sib(), lambda q: q.wait_send())
            for k in range(4):
                d = rem(p.y - k + 4, 4) * 2 + p.xl
                for t in (1, 2):
                    self.move(d, t, self.ix + 6 * k + 3 * (t - 1), p.sib(), lambda q: q.wait_send())

    i_share = m.take(5)
    w_qkv = Shards(r.wqkv, i_share)
    w_o = Shards(r.wo_v, i_share + 1)
    w_d = Down(i_share + 2)
    w_g = Shards(r.wg_v, i_share + 3)
    w_u = Shards(r.wu_v, i_share + 4)
    i_tok = m.take(4)
    for dz in (2, 1, 3):
        m.send(r.tok, r.tok_all.at[dz], i_tok + dz, p.zpeer(dz))
    m.local(r.wqkv.at[0, half], r.wqkv.at[0, half], i_loc).wait()
    w_qkv.along_y()
    w_qkv.along_x(0)
    i_mseq = m.take(16)
    for k in range(1, 16):
        m.send(r.meta, r.mseq.at[p.sq], i_mseq + k, p.speer(k))
    i_mdp = m.take(8)
    for k in range(1, 8):
        m.send(r.meta, r.mdp.at[p.dp], i_mdp + k, p.dpeer(k))
    r.mseq[p.sq] = r.meta[...]
    r.mdp[p.dp] = r.meta[...]
    m.local(r.wo_v.at[0, half], r.wo_v.at[0, half], i_loc + 1).wait()
    w_o.along_y()
    for n in range(2):
        down_local(n).wait()

    @pl.when(has_extra)
    def _():
        down_local(2).wait()

    w_d.along_y()
    m.local(r.wg_v.at[0, half], r.wg_v.at[0, half], i_loc + 2).wait()
    w_g.along_y()
    m.local(r.wu_v.at[0, half], r.wu_v.at[0, half], i_loc + 3).wait()
    w_u.along_y()

    for k in range(1, 16):
        m.got(r.mseq.at[rem(p.sq + 16 - k, 16)], i_mseq + k)
    r.st[...] = seg_rows(r.mseq[:, 2, :])
    lanesign = jnp.where(lane_half(), -1.0, 1.0)
    freq = r.freq[...]
    for dz in range(4):
        i = 4 * z_of(dz) + p.g
        row = r.st[pl.ds(i, 1), :]
        pos = (lax.broadcasted_iota(jnp.int32, (1, 128), 1) + i * 128).astype(F32) - row
        ang = jnp.transpose(jnp.broadcast_to(pos, (128, 128))) * freq
        r.cosr[dz] = jnp.cos(ang)
        r.sinr[dz] = jnp.sin(ang) * lanesign
    for k in range(1, 8):
        m.got(r.mdp.at[dps[k]], i_mdp + k)
    gain1 = jnp.concatenate([r.mdp[j, 0:1, :] for j in range(8)], axis=1)
    gain2 = jnp.concatenate([r.mdp[j, 1:2, :] for j in range(8)], axis=1)

    for k in (1, 3, 2):
        w_qkv.along_x(k)
    w_qkv.to_core()
    w_qkv.done()

    wfull = r.wqkv[...].reshape(1024, 512)
    qg = r.gqk[0:1, :].astype(F32)
    kg = r.gqk[1:2, :].astype(F32)
    i_kv = m.take(4)
    i_kvx = m.take(4)
    i_kvf = m.take(4)

    def project(dz, x):
        x = x.astype(F32)
        r1 = lax.rsqrt(jnp.mean(x * x, axis=1, keepdims=True) + EPS)
        h = (x * r1 * gain1).astype(BF)
        r.tok_all[dz] = h
        o = dot(h, wfull)
        cs, sn = r.cosr[dz], r.sinr[dz]
        r.qk_raw[dz] = o[:, 0:384]
        rot = []
        for b, gn in ((0, qg), (1, qg), (2, kg)):
            v = o[:, b * 128:(b + 1) * 128]
            v = v * lax.rsqrt(head_mean(v * v) + EPS) * gn
            rot.append(v * cs + swap_halves(v) * sn)
        for hd, v in enumerate(spread_heads(rot[0], rot[1])):
            r.qz[dz, pl.ds(hd * 128, 128), :] = v.astype(BF)
        i = 4 * z_of(dz) + p.g
        r.kv[i, :, 0:128] = rot[2].astype(BF)
        r.kv[i, :, 128:256] = o[:, 384:512].astype(BF)
        m.send(r.kv.at[i], r.kv.at[i], i_kvx + dz, p.xpeer())
        m.send(r.kv.at[i], r.kv.at[i], i_kv + dz, p.sib())

    project(0, r.tok[...])
    for dz in (1, 3, 2):
        m.got(r.tok_all.at[dz], i_tok + dz)
        project(dz, r.tok_all[dz])
    i_cot = m.take(4)
    for dz in (1, 3, 2):
        m.send(r.cot, r.cot_all.at[dz], i_cot + dz, p.zpeer(dz))
    r.cot_all[0] = r.cot[...]
    gs = p.g + 1 - 2 * p.c
    gx = (1 - p.xh) * 2 + p.c
    gxs = (1 - p.xh) * 2 + 1 - p.c
    for dz in (0, 1, 3, 2):
        zz = 4 * z_of(dz)
        m.got(r.kv.at[zz + gx], i_kvx + dz)
        m.send(r.kv.at[zz + gx], r.kv.at[zz + gx], i_kvf + dz, p.sib())
    for dz in (0, 1, 3, 2):
        zz = 4 * z_of(dz)
        m.got(r.kv.at[zz + gs], i_kv + dz)
        m.got(r.kv.at[zz + gxs], i_kvf + dz)

    def turn(j, carry):
        r.kt[j] = jnp.transpose(r.kv[j, :, 0:128].astype(F32)).astype(BF)
        r.vt[j] = jnp.transpose(r.kv[j, :, 128:256].astype(F32)).astype(BF)
        return carry

    lax.fori_loop(0, 16, turn, 0)
    for k in (0, 1, 3, 2):
        w_o.along_x(k)

    def allowed_rows(i):
        row = r.st[pl.ds(i, 1), :].astype(jnp.int32)
        qi = lax.broadcasted_iota(jnp.int32, (1, 128), 1) + i * 128
        return jnp.concatenate([row] * 4, axis=1), jnp.concatenate([qi] * 4, axis=1)

    def weights_of(kb, qv, row4, qi4):
        s = dot(r.kv[kb, :, 0:128], qv, NT)
        ki = lax.broadcasted_iota(jnp.int32, (128, 512), 0) + kb * 128
        return jnp.where((ki >= row4) & (ki <= qi4), jnp.exp2(s * (SCALE * LOG2E)), 0.0)

    def forward_chunk(j, carry):
        dz = rem(j + 1, 4)
        i = 4 * z_of(dz) + p.g
        row4, qi4 = allowed_rows(i)
        r.acc[...] = jnp.zeros_like(r.acc)
        r.lacc[...] = jnp.zeros_like(r.lacc)
        qv = r.qz[dz]

        def body(kb, inner):
            w = weights_of(kb, qv, row4, qi4)
            r.lacc[...] += jnp.sum(w.reshape(16, 8, 512), axis=0)
            r.acc[...] += dot(r.vt[kb], w.astype(BF))
            return inner

        lax.fori_loop(jnp.maximum(i - 8, 0), i + 1, body, 0)
        il = 1.0 / jnp.sum(r.lacc[...], axis=0, keepdims=True)
        r.invl[dz] = jnp.broadcast_to(il, (8, 512))
        o = r.acc[...] * il
        full = jnp.concatenate(
            [o[(h // 2) * 64:(h // 2) * 64 + 64, h * 128:(h + 1) * 128] for h in range(4)], axis=0
        )
        r.oT[dz] = full
        r.o_s[dz] = jnp.transpose(full).astype(BF)
        return carry

    i_o = m.take(4)
    for j in range(4):
        forward_chunk(j, 0)
        dz = (j + 1) % 4
        if dz:
            m.send(r.o_s.at[dz], r.o_in.at[p.z], i_o + dz, p.zpeer(-dz))
        else:
            r.o_in[p.z] = r.o_s[0]
        if j < 3:
            for k in (0, 1, 3, 2):
                (w_d, w_g, w_u)[j].along_x(k)
        if j == 1:
            w_o.to_core()

    for dz in range(1, 4):
        m.got(r.o_in.at[rem(p.z + dz, 4)], i_o + dz)
    for j in range(4):
        r.o_own[:, j * 256:(j + 1) * 256] = r.o_in[j]
    w_o.done()
    x0 = r.tok[...].astype(F32)
    middle = x0 + dot(r.o_own[...], r.wo_v[...].reshape(1024, 1024))
    r.mid[...] = middle
    r2 = lax.rsqrt(jnp.mean(middle * middle, axis=1, keepdims=True) + EPS)
    r.h2[0] = (middle * r2 * gain2).astype(BF)
    i_h2 = m.take(4)
    for dz in (2, 1, 3):
        m.send(r.h2.at[0], r.h2.at[dz], i_h2 + dz, p.zpeer(dz))

    w_d.to_core()
    w_g.to_core()
    w_u.to_core()
    for dz in range(1, 4):
        m.got(r.cot_all.at[dz], i_cot + dz)
    w_d.done()
    wd = r.wd_v[...].reshape(1152, 1024)
    cots = r.cot_all[...].reshape(512, 1024)

    def cols384(t):
        return pl.ds(pl.multiple_of(t * 384, 128), 384)

    def dm_tile(t, carry):
        w = r.wd_v[pl.ds(t * 6, 6)].reshape(384, 1024)
        r.dm[:, :, cols384(t)] = dot(cots, w, NT).reshape(4, 128, 384)
        return carry

    lax.fori_loop(0, 3, dm_tile, 0)
    w_g.done()
    w_u.done()

    i_p2 = m.take(4)
    for pair in range(2):
        two = slice(2 * pair, 2 * pair + 2)
        for dz in ((1,), (2, 3))[pair]:
            m.got(r.h2.at[dz], i_h2 + dz)
        hh = r.h2[two].reshape(256, 1024)

        def ffn_tile(t, carry):
            cols = cols384(t)
            gate = dot(hh, r.wg_v[:, :, cols].reshape(1024, 384))
            up = dot(hh, r.wu_v[:, :, cols].reshape(1024, 384))
            sig = 1.0 / (1.0 + jnp.exp(-gate))
            act = gate * sig
            dmt = r.dm[two, :, cols].reshape(256, 384)
            r.mixed[two, :, cols] = (act * up).astype(BF).reshape(2, 128, 384)
            r.dg[two, :, cols] = (dmt * up * sig * (1.0 + gate * (1.0 - sig))).astype(BF).reshape(2, 128, 384)
            r.du[two, :, cols] = (dmt * act).astype(BF).reshape(2, 128, 384)
            return carry

        lax.fori_loop(0, 3, ffn_tile, 0)
        part = dot(r.dg[two].reshape(256, 1152), r.wg_v[...].reshape(1024, 1152), NT)
        part += dot(r.du[two].reshape(256, 1152), r.wu_v[...].reshape(1024, 1152), NT)
        if pair == 0:
            r.own[...] = part[0:128]
            r.p2s[0] = part[128:256].astype(BF)
            m.send(r.p2s.at[0], r.p2r.at[0], i_p2 + 1, p.zpeer(-1))
        else:
            r.p2s[1] = part[0:128].astype(BF)
            m.send(r.p2s.at[1], r.p2r.at[1], i_p2 + 2, p.zpeer(-2))
            r.p2s[2] = part[128:256].astype(BF)
            m.send(r.p2s.at[2], r.p2r.at[2], i_p2 + 3, p.zpeer(-3))

    i_r1 = m.take(3)
    h2t = r.h2[...].reshape(512, 1024)

    def gate_up_tile(t, carry):
        cols = cols384(t)
        r.gF[:, :, :, cols] = dot(h2t, r.dg[:, :, cols].reshape(512, 384), TN).astype(BF).reshape(4, 2, 128, 384)
        r.gF[:, :, :, cols384(t + 3)] = dot(h2t, r.du[:, :, cols].reshape(512, 384), TN).astype(BF).reshape(4, 2, 128, 384)
        return carry

    lax.fori_loop(0, 3, gate_up_tile, 0)
    m.send(r.gF.at[:, :, other], r.r1F, i_r1, p.sib())

    def down_tile(t, carry):
        w = r.mixed[:, :, cols384(t)].reshape(512, 384)
        r.gD[pl.ds(t * 6, 6)] = dot(w, cots, TN).astype(BF).reshape(6, 64, 1024)
        return carry

    lax.fori_loop(0, 3, down_tile, 0)
    m.send(r.gD.at[:, o32], r.r1D, i_r1 + 1, p.sib())
    r.own3[...] = dot(r.mixed[0], wd)

    def out_chunk(dz, carry):
        r.p3s[dz - 1] = dot(r.mixed[dz], wd).astype(BF)
        return carry

    lax.fori_loop(1, 4, out_chunk, 0)

    for dz in range(1, 4):
        m.got(r.p2r.at[dz - 1], i_p2 + dz)
    dh2 = r.own[...] + r.p2r[0].astype(F32) + r.p2r[1].astype(F32) + r.p2r[2].astype(F32)
    middle = r.mid[...]
    r2 = lax.rsqrt(jnp.mean(middle * middle, axis=1, keepdims=True) + EPS)
    small2 = jnp.sum(dh2 * middle * r2, axis=0, keepdims=True)
    wdh = dh2 * gain2
    dmid = r.cot[...].astype(F32) + r2 * wdh - middle * (r2 * r2 * r2) * jnp.mean(wdh * middle, axis=1, keepdims=True)
    r.dmid[...] = dmid
    r.da[...] = dmid.astype(BF)
    r.dob[...] = dot(r.da[...], r.wo_v[...].reshape(1024, 1024), NT).astype(BF)
    i_do = m.take(4)

    def zcols(z):
        return pl.ds(pl.multiple_of(z * 256, 256), 256)

    for dz in (2, 1, 3):
        m.send(r.dob.at[:, zcols(rem(p.z + dz, 4))], r.do_all.at[dz], i_do + dz, p.zpeer(dz))
    r.do_all[0] = r.dob[:, zq]
    i_p3 = m.take(4)
    i_of = m.take(4)
    i_dc = m.take(4)
    for dz in (2, 1, 3):
        m.send(r.o_own, r.o_full.at[dz], i_of + dz, p.zpeer(dz))
        m.send(r.da.at[:, zcols(rem(p.z + dz, 4))], r.da_c.at[dz], i_dc + dz, p.zpeer(dz))
    for dz in (2, 1, 3):
        m.send(r.p3s.at[dz - 1], r.p3r.at[dz - 1], i_p3 + dz, p.zpeer(-dz))
    r.o_full[0] = r.o_own[...]
    r.da_c[0] = r.da[:, zq]

    m.got(r.r1F, i_r1)
    m.got(r.r1D, i_r1 + 1)

    def add_core(d, carry):
        a, b = lax.div(d, 2), rem(d, 2)
        r.r1F[a, b] = (r.r1F[a, b].astype(F32) + r.gF[a, b, half].astype(F32)).astype(BF)
        where, more = down_pieces(d)
        for n in range(2):
            t = where[n][1]
            r.sD[a, b, n] = (r.r1D[t].astype(F32) + r.gD[t, h32].astype(F32)).astype(BF)

        @pl.when(more)
        def _():
            t = where[2][1]
            r.sX[b] = (r.r1D[t].astype(F32) + r.gD[t, h32].astype(F32)).astype(BF)

        return carry

    lax.fori_loop(0, 8, add_core, 0)

    def rows_of(x, n):
        return pl.ds(pl.multiple_of(x * n, n), n)

    class XFirst:
        def __init__(self, src, mid1, tot, mid2):
            self.src, self.mid1, self.tot, self.mid2 = src, mid1, tot, mid2
            self.i1, self.i2 = m.take(4), m.take(4)

        def one(self):
            for t in (3, 1, 2):
                m.send(self.src(t), self.mid1.at[t - 1], self.i1 + t, p.xring(t))

        def two(self):
            for t in (1, 2, 3):
                m.got(self.mid1.at[t - 1], self.i1 + t)

            def add(n, carry):
                v = self.src(0).at[n][...].astype(F32)
                for t in range(3):
                    v = v + self.mid1[t, n].astype(F32)
                self.tot[n] = v.astype(BF)
                return carry

            lax.fori_loop(0, 4, add, 0)
            for k in (2, 1, 3):
                m.send(self.tot.at[rem(p.y + k, 4)], self.mid2.at[k - 1], self.i2 + k, p.ypeer(k))

        def sum(self):
            for k in (1, 2, 3):
                m.got(self.mid2.at[k - 1], self.i2 + k)
            v = self.tot[p.y].astype(F32)
            for k in range(3):
                v = v + self.mid2[k].astype(F32)
            return v.astype(BF)

    class YFirst:
        def __init__(self, src, part, mid1, tot, mid2):
            self.src, self.part, self.mid1, self.tot, self.mid2 = src, part, mid1, tot, mid2
            self.i1, self.i2 = m.take(4), m.take(4)

        def one(self):
            for k in (2, 1, 3):
                m.send(self.src(rem(p.y + k, 4)), self.mid1.at[k - 1], self.i1 + k, p.ypeer(k))

        def two(self):
            for k in (1, 2, 3):
                m.got(self.mid1.at[k - 1], self.i1 + k)

            def add(n, carry):
                v = self.src(p.y).at[n][...].astype(F32)
                for k in range(3):
                    v = v + self.mid1[k, n].astype(F32)
                self.tot[n] = v.astype(BF)
                return carry

            lax.fori_loop(0, 2, add, 0)
            for t in (3, 1, 2):
                m.send(self.part(self.tot, t), self.mid2.at[t - 1], self.i2 + t, p.xring(t))

        def sum(self):
            for t in (1, 2, 3):
                m.got(self.mid2.at[t - 1], self.i2 + t)
            v = self.part(self.tot, 0)[...].astype(F32)
            for t in range(3):
                v = v + self.mid2[t].astype(F32)
            return v.astype(BF)

    def rows_x(buf, c0, c1):
        return lambda t: buf.at[:, p.xplace(t)[0], rows_of(p.xplace(t)[1], 32), c0:c1]

    def rows_y(buf, c0, c1):
        return lambda y: buf.at[y, :, :, c0:c1]

    def part_y(tot, t):
        xl, xh = p.xplace(t)
        return tot.at[xl, rows_of(xh, 32)]

    def part_d(tot, t):
        xl, xh = p.xplace(t)
        return tot.at[xl, :, rows_of(xh, 16)]

    sums = [
        XFirst(rows_x(r.r1F, 0, 1152), r.ax, r.at, r.ay),
        YFirst(rows_y(r.r1F, 1152, 2304), part_y, r.by, r.bt, r.bx),
        XFirst(
            lambda t: r.sD.at[:, p.xplace(t)[0], :, rows_of(p.xplace(t)[1], 16), 0:512], r.adx, r.adt, r.ady
        ),
        YFirst(lambda y: r.sD.at[y, :, :, :, 512:1024], part_d, r.bdy, r.bdt, r.bdx),
    ]
    for e in sums:
        e.one()
    i_x1 = m.take(4)
    i_x2 = m.take(4)
    for t in (3, 1, 2):
        xl, xh = p.xplace(t)
        m.send(r.sX.at[xl, rows_of(xh, 16)], r.xx.at[t - 1], i_x1 + t, p.xring(t))

    r.dkv[...] = jnp.zeros_like(r.dkv)
    for dz in (0, 1, 3, 2):
        if dz:
            m.got(r.do_all.at[dz], i_do + dz)

    def backward_chunk(j, carry):
        dz = j
        i = 4 * z_of(dz) + p.g
        row4, qi4 = allowed_rows(i)
        do = r.do_all[dz].astype(F32)
        for hd, v in enumerate(spread_heads(do[:, 0:128], do[:, 128:256])):
            r.doz[pl.ds(hd * 128, 128), :] = v.astype(BF)
        prod = jnp.transpose(do) * r.oT[dz]
        drow = jnp.concatenate(
            [jnp.sum(prod[h * 64:(h + 1) * 64], axis=0, keepdims=True) for h in range(4)], axis=1
        )
        il = r.invl[dz, 0:1, :]
        qv = r.qz[dz]
        dov = r.doz[...]
        r.acc[...] = jnp.zeros_like(r.acc)

        def body(kb, inner):
            w = weights_of(kb, qv, row4, qi4) * il
            dp = dot(r.kv[kb, :, 128:256], dov, NT)
            ds = (w * (dp - drow)).astype(BF)
            r.acc[...] += dot(r.kt[kb], ds)
            r.dkv[kb, :, 0:128] += dot(ds, qv)
            r.dkv[kb, :, 128:256] += dot(w.astype(BF), dov)
            return inner

        lax.fori_loop(jnp.maximum(i - 8, 0), i + 1, body, 0)
        o = r.acc[...] * SCALE
        full = jnp.concatenate(
            [o[(h // 2) * 64:(h // 2) * 64 + 64, h * 128:(h + 1) * 128] for h in range(4)], axis=0
        )
        r.dqr[dz] = jnp.transpose(full)
        return carry

    lax.fori_loop(0, 4, backward_chunk, 0)

    lane = lax.broadcasted_iota(jnp.int32, (1, 256), 1)
    kscale = jnp.where(lane < 128, SCALE, 1.0)
    r.dkvb[...] = (r.dkv[...] * kscale.reshape(1, 1, 256)).astype(BF).reshape(4, 4, 128, 256)
    i_dkv = m.take(3)
    xs = (p.dp, p.z * 4 + gxs)
    m.send(r.dkvb.at[:, gx], r.dkvr.at[1], i_dkv + 1, p.xpeer())
    m.send(r.dkvb.at[:, gxs], r.dkvr.at[2], i_dkv + 2, xs)
    m.send(r.dkvb.at[:, gs], r.dkvr.at[0], i_dkv, p.sib())

    for e in sums:
        e.two()
    for t in (1, 2, 3):
        m.got(r.xx.at[t - 1], i_x1 + t)
    v = r.sX[p.xl, rows_of(p.xh, 16)].astype(F32)
    for t in range(3):
        v = v + r.xx[t].astype(F32)
    r.xt[...] = v.astype(BF)
    kz = rem(p.z - p.y + 4, 4)

    @pl.when(kz != 0)
    def _():
        m.copy(r.xt, r.xy.at[kz - 1], i_x2 + kz, (p.z * 2 + p.xl, p.sq)).start()

    for dz in range(1, 4):
        m.got(r.o_full.at[dz], i_of + dz)
        m.got(r.da_c.at[dz], i_dc + dz)
        m.got(r.p3r.at[dz - 1], i_p3 + dz)
    r.gA[:, :, :, 512:768] = dot(
        r.o_full[...].reshape(512, 1024), r.da_c[...].reshape(512, 256), TN
    ).astype(BF).reshape(4, 2, 128, 256)
    r.block_out[...] = (
        r.mid[...] + r.own3[...] + r.p3r[0].astype(F32) + r.p3r[1].astype(F32) + r.p3r[2].astype(F32)
    ).astype(BF)

    r.oF[:, 0:1152] = sums[0].sum()
    r.oF[:, 1152:2304] = sums[1].sum()
    r.oD[0:2, :, 0:512] = sums[2].sum()
    r.oD[0:2, :, 512:1024] = sums[3].sum()

    @pl.when(kz == 0)
    def _():
        v = r.xt[...].astype(F32)
        for k in (1, 2, 3):
            m.got(r.xy.at[k - 1], i_x2 + k)
            v = v + r.xy[k - 1].astype(F32)
        r.oD[2] = v.astype(BF)

    @pl.when(kz != 0)
    def _():
        r.oD[2] = jnp.zeros((16, 1024), BF)

    def seq_at(z, g):
        return rem(z + 8, 4) * 4 + g

    class Gather:
        def __init__(self, own, buf):
            self.own, self.buf = own, buf
            self.il = m.take(1)
            self.ix, self.iz, self.izx, self.ic = m.take(1), m.take(4), m.take(4), m.take(8)

        def first(self):
            s = self.buf.at[p.sq]
            m.send(self.own, s, self.ix, p.xpeer())
            for dz in (2, 1, 3):
                m.send(self.own, s, self.iz + dz, p.zpeer(dz))
            m.send(self.own, s, self.ic, p.sib())
            m.local(self.own, s, self.il).start()

        def second(self):
            s = self.buf.at[seq_at(p.z, gx)]
            m.got(s, self.ix)
            for dz in (2, 1, 3):
                m.send(s, s, self.izx + dz, p.zpeer(dz))
            m.send(s, s, self.ic + 4, p.sib())

        def third(self):
            for dz in (1, 3, 2):
                s = self.buf.at[seq_at(p.z - dz, p.g)]
                m.got(s, self.iz + dz)
                m.send(s, s, self.ic + dz, p.sib())
            for dz in (1, 3, 2):
                s = self.buf.at[seq_at(p.z - dz, gx)]
                m.got(s, self.izx + dz)
                m.send(s, s, self.ic + 4 + dz, p.sib())

        def last(self):
            for dz in (0, 1, 3, 2):
                m.got(self.buf.at[seq_at(p.z - dz, gs)], self.ic + dz)
                m.got(self.buf.at[seq_at(p.z - dz, gxs)], self.ic + 4 + dz)
            m.local(self.own, self.buf.at[p.sq], self.il).wait()

    ag_f = Gather(r.oF, r.fF)
    ag_d = Gather(r.oD, r.fD)
    ag_a = Gather(r.oA, r.fA)

    for n in range(3):
        m.got(r.dkvr.at[n], i_dkv + n)
    sq_acc = jnp.zeros((1, 128), F32)
    sk_acc = jnp.zeros((1, 128), F32)
    for dz in range(4):
        zz = z_of(dz)
        i = 4 * zz + p.g
        dkv = r.dkv[i] * kscale
        for n in range(3):
            dkv = dkv + r.dkvr[n, zz].astype(F32)
        cs, sn = r.cosr[dz], r.sinr[dz]
        grads = (r.dqr[dz, :, 0:128], r.dqr[dz, :, 128:256], dkv[:, 0:128])
        for b, gr in enumerate(grads):
            gn = qg if b < 2 else kg
            v = r.qk_raw[dz, :, b * 128:(b + 1) * 128]
            f = lax.rsqrt(head_mean(v * v) + EPS)
            dn = gr * cs - swap_halves(gr) * sn
            add = jnp.sum(dn * v * f, axis=0, keepdims=True)
            if b < 2:
                sq_acc = sq_acc + add
            else:
                sk_acc = sk_acc + add
            wn = dn * gn
            r.dqkv[dz, :, b * 128:(b + 1) * 128] = (f * wn - v * (f * f * f) * head_mean(wn * v)).astype(BF)
        r.dqkv[dz, :, 384:512] = dkv[:, 128:256].astype(BF)
    i_p4 = m.take(4)
    for dz in range(1, 4):
        m.flush(i_p2 + dz)
    for dz in (2, 1, 3):
        r.p2s[dz - 1] = dot(r.dqkv[dz], r.wqkv[...].reshape(1024, 512), NT).astype(BF)
        m.send(r.p2s.at[dz - 1], r.p4r.at[dz - 1], i_p4 + dz, p.zpeer(-dz))
    r.own[...] = dot(r.dqkv[0], r.wqkv[...].reshape(1024, 512), NT)
    r.gA[:, :, :, 0:512] = dot(
        r.tok_all[...].reshape(512, 1024), r.dqkv[...].reshape(512, 512), TN
    ).astype(BF).reshape(4, 2, 128, 512)
    m.send(r.gA.at[:, :, other], r.r1A, i_r1 + 2, p.sib())
    ag_f.first()
    ag_d.first()
    m.got(r.r1A, i_r1 + 2)
    r.r1A[...] = (r.r1A[...].astype(F32) + r.gA[:, :, half].astype(F32)).astype(BF)
    sums_a = [
        XFirst(rows_x(r.r1A, 0, 384), r.qax, r.qat, r.qay),
        YFirst(rows_y(r.r1A, 384, 768), part_y, r.qby, r.qbt, r.qbx),
    ]
    for e in sums_a:
        e.one()
    ag_f.second()
    ag_d.second()

    for e in sums_a:
        e.two()

    for dz in range(1, 4):
        m.got(r.p4r.at[dz - 1], i_p4 + dz)
    dh = r.own[...] + r.p4r[0].astype(F32) + r.p4r[1].astype(F32) + r.p4r[2].astype(F32)
    x0 = r.tok[...].astype(F32)
    r1 = lax.rsqrt(jnp.mean(x0 * x0, axis=1, keepdims=True) + EPS)
    small1 = jnp.sum(dh * x0 * r1, axis=0, keepdims=True)
    wdh = dh * gain1
    r.input_grad[...] = (
        r.dmid[...] + r1 * wdh - x0 * (r1 * r1 * r1) * jnp.mean(wdh * x0, axis=1, keepdims=True)
    ).astype(BF)

    both = lambda v: v + pltpu.roll(v, 64, 1)
    for d in range(8):
        cols = slice(d * 128, (d + 1) * 128)
        r.gsm[d] = jnp.concatenate(
            [small1[:, cols], small2[:, cols], both(sq_acc), both(sk_acc), jnp.zeros((4, 128), F32)], axis=0
        )
    i_s1 = m.take(8)
    i_s2 = m.take(16)
    for k in range(1, 8):
        m.send(r.gsm.at[rem(p.dp + k, 8)], r.gs1.at[k], i_s1 + k, p.dpeer(k))
    r.gs1[0] = r.gsm[p.dp]
    for k in range(1, 8):
        m.got(r.gs1.at[k], i_s1 + k)
    r.gs1s[...] = jnp.sum(r.gs1[...], axis=0)
    for k in range(1, 16):
        m.send(r.gs1s, r.gs2.at[k], i_s2 + k, p.speer(k))
    r.gs2[0] = r.gs1s[...]

    r.oA[:, 0:384] = sums_a[0].sum()
    r.oA[:, 384:768] = sums_a[1].sum()
    ag_a.first()
    ag_f.third()
    ag_d.third()
    ag_a.second()
    ag_a.third()
    for k in range(1, 16):
        m.got(r.gs2.at[k], i_s2 + k)
    r.g_small[...] = jnp.sum(r.gs2[...], axis=0)
    ag_f.last()
    ag_d.last()
    ag_a.last()

    m.finish()
    w_d.finish()

    @pl.when(kz != 0)
    def _():
        m.copy(r.xt, r.xt, i_x2 + kz, p.sib()).wait_send()

    assert m.n <= NSEM, m.n


def block(args):
    vm = pl.BlockSpec(memory_space=pltpu.VMEM)
    hb = pl.BlockSpec(memory_space=pl.ANY)
    return pl.pallas_call(
        kernel,
        out_shape=tuple(jax.ShapeDtypeStruct(s, d) for s, d in OUTPUTS.values()),
        in_specs=[vm] * 6 + [hb] * 7 + [vm],
        out_specs=tuple(hb if name[0] == "f" else vm for name in OUTPUTS),
        scratch_shapes=[pltpu.VMEM(s, d) for s, d in SCRATCH.values()]
        + [pltpu.SemaphoreType.DMA((NSEM,)), pltpu.SemaphoreType.DMA((NSEM,))],
        compiler_params=pltpu.CompilerParams(
            collective_id=0, has_side_effects=True, vmem_limit_bytes=63 * 2**20
        ),
        name="block",
    )(*args)


LAID = {
    "g_gate": (128, 4608),
    "g_up": (128, 4608),
    "g_down": (576, 1024),
    "g_q": (128, 1024),
    "g_k": (128, 512),
    "g_v": (128, 512),
    "g_out": (128, 1024),
}


def lay_kernel(f_f, f_d, f_a, g_gate, g_up, g_down, g_q, g_k, g_v, g_out):
    p = Place()

    def lay(s, carry):
        z = lax.div(s, 4)
        g = rem(s, 4)
        row = pl.ds(pl.multiple_of(rem(g, 2) * 64 + lax.div(g, 2) * 32, 32), 32)
        for t in range(9):
            cols = pl.ds(pl.multiple_of(t * 512 + z * 128, 128), 128)
            g_gate[row, cols] = f_f[s, :, t * 128:(t + 1) * 128].astype(F32)
            g_up[row, cols] = f_f[s, :, 1152 + t * 128:1152 + (t + 1) * 128].astype(F32)
        c256 = pl.ds(pl.multiple_of(z * 256, 256), 256)
        c128 = pl.ds(pl.multiple_of(z * 128, 128), 128)
        g_q[row, c256] = f_a[s, :, 0:256].astype(F32)
        g_k[row, c128] = f_a[s, :, 256:384].astype(F32)
        g_v[row, c128] = f_a[s, :, 384:512].astype(F32)
        g_out[row, c256] = f_a[s, :, 512:768].astype(F32)
        sub = rem(g, 2) * 32 + lax.div(g, 2) * 16
        for n in range(2):
            u = rem(2 * z + n - p.dp + 8, 8)
            g_down[pl.ds(pl.multiple_of(u * 64 + sub, 16), 16), :] = f_d[s, n].astype(F32)

        @pl.when(lax.div(p.dp, 2) == z)
        def _():
            g_down[pl.ds(pl.multiple_of(8 * 64 + sub, 16), 16), :] = f_d[s, 2].astype(F32)

        return carry

    lax.fori_loop(0, 16, lay, 0)


def lay_out(f_f, f_d, f_a):
    vm = pl.BlockSpec(memory_space=pltpu.VMEM)
    o = pl.pallas_call(
        lay_kernel,
        out_shape=tuple(jax.ShapeDtypeStruct(s, F32) for s in LAID.values()),
        in_specs=[vm] * 3,
        out_specs=tuple(vm for _ in LAID),
        compiler_params=pltpu.CompilerParams(vmem_limit_bytes=40 * 2**20),
        name="lay",
    )(f_f, f_d, f_a)
    return dict(zip(LAID, o))


def local(
    tokens, segment_ids, attn_gain, w_query, w_key, w_value, w_out, ffn_gain, w_gate, w_up, w_down,
    query_gain, key_gain, cotangent,
):
    inverse = ROPE_BASE ** (-(np.arange(32).astype(np.float32) * np.float32(2.0) / np.float32(64)))
    freq = jnp.asarray(np.tile(inverse.astype(np.float32), 4)[None])
    gqk = jnp.stack([jnp.tile(query_gain, 2), jnp.tile(key_gain, 2)])
    o = block(
        (
            tokens, segment_ids, attn_gain[None], ffn_gain[None], gqk, freq, w_query, w_key, w_value,
            w_out, w_gate, w_up, w_down, cotangent,
        )
    )
    o = dict(zip(OUTPUTS, o))
    small = o["g_small"]
    w = lay_out(o["fF"], o["fD"], o["fA"])
    return (
        o["block_out"], o["input_grad"], small[0], w["g_q"], w["g_k"], w["g_v"], w["g_out"], small[1],
        w["g_gate"], w["g_up"], w["g_down"], small[2, :64], small[3, :64],
    )


def solution(mesh):
    both = ("dp", "seq")
    w = P("dp", None)
    return jax.shard_map(
        local,
        mesh=mesh,
        in_specs=(P(both, None), P("dp", "seq"), P("dp"), w, w, w, w, P("dp"), w, w, w, P(), P(), P(both, None)),
        out_specs=(P(both, None), P(both, None), P("dp"), w, w, w, w, P("dp"), w, w, w, P(), P()),
        check_vma=False,
    )
```

```python
import math

import jax
import jax.numpy as jnp
import numpy as np
from jax import lax
from jax.experimental import pallas as pl
from jax.experimental.pallas import tpu as pltpu
from jax.sharding import PartitionSpec as P

MESH = pl.DeviceIdType.MESH
F32 = jnp.float32
BF = jnp.bfloat16
EPS = 1e-05
ROPE_BASE = 1000000.0
NN = (((1,), (0,)), ((), ()))
NT = (((1,), (1,)), ((), ()))
TN = (((0,), (0,)), ((), ()))
SCALE = 0.125
LOG2E = math.log2(math.e)


def dot(a, b, dims=NN, precision=None):
    return lax.dot_general(a, b, dims, preferred_element_type=F32, precision=precision)


def rem(a, b):
    return lax.rem(a, b)


class Place:
    def __init__(self):
        self.dp = lax.axis_index("dp")
        self.sq = lax.axis_index("seq")
        self.y = lax.div(self.dp, 2)
        self.xl = rem(self.dp, 2)
        self.z = lax.div(self.sq, 4)
        self.g = rem(self.sq, 4)
        self.xh = lax.div(self.g, 2)
        self.c = rem(self.sq, 2)

    def zpeer(self, dz):
        return (self.dp, rem(self.z + dz + 4, 4) * 4 + self.g)

    def sib(self):
        return (self.dp, self.sq + 1 - 2 * self.c)

    def xpeer(self):
        return (self.dp, self.z * 4 + (1 - self.xh) * 2 + self.c)

    def dpeer(self, k):
        return (rem(self.dp + k + 8, 8), self.sq)

    def speer(self, k):
        return (self.dp, rem(self.sq + k + 16, 16))

    def ypeer(self, k):
        return (rem(self.y + k + 4, 4) * 2 + self.xl, self.sq)

    def xring(self, t):
        xl = self.xl if t == 3 else 1 - self.xl
        return (self.y * 2 + xl, self.sq if t == 1 else self.z * 4 + (1 - self.xh) * 2 + self.c)

    def xplace(self, t):
        return (self.xl if t in (0, 3) else 1 - self.xl), (self.xh if t in (0, 1) else 1 - self.xh)


def seg_rows(ids):
    start = jnp.zeros_like(ids)
    for j in range(1, 8):
        below = jnp.sum(jnp.where(ids < j, 1.0, 0.0), keepdims=True)
        start = jnp.where(ids == j, below, start)
    return start


def lane_half():
    return lax.rem(lax.broadcasted_iota(jnp.int32, (1, 128), 1), 64) < 32


def swap_halves(x):
    return jnp.where(lane_half(), pltpu.roll(x, 96, 1), pltpu.roll(x, 32, 1))


def head_mean(x):
    a = lax.div(lax.broadcasted_iota(jnp.int32, (128, 128), 0), 64)
    b = lax.div(lax.broadcasted_iota(jnp.int32, (128, 128), 1), 64)
    block = jnp.where(a == b, 1.0 / 64, 0.0)
    return dot(x, block, NN, lax.Precision.HIGHEST)


def spread_heads(first, second):
    lo = lax.broadcasted_iota(jnp.int32, (1, 128), 1) < 64
    return [
        jnp.where(lo, first, 0.0),
        jnp.where(lo, pltpu.roll(first, 64, 1), 0.0),
        jnp.where(lo, 0.0, pltpu.roll(second, 64, 1)),
        jnp.where(lo, 0.0, second),
    ]


INPUTS = ["tok", "seg", "ga", "gf", "gqk", "freq", "wq", "wk", "wv", "wo", "wg", "wu", "wd", "cot"]
OUTPUTS = {
    "block_out": ((128, 1024), BF),
    "input_grad": ((128, 1024), BF),
    "fF": ((16, 32, 2304), BF),
    "fD": ((16, 3, 16, 1024), BF),
    "fA": ((16, 32, 768), BF),
    "g_small": ((8, 128), F32),
}
SCRATCH = {
    "tok_all": ((4, 128, 1024), BF),
    "cot_all": ((4, 128, 1024), BF),
    "meta": ((8, 128), F32),
    "mseq": ((16, 8, 128), F32),
    "mdp": ((8, 8, 128), F32),
    "wqkv": ((8, 128, 512), BF),
    "wo_v": ((8, 128, 1024), BF),
    "wg_v": ((8, 128, 1152), BF),
    "wu_v": ((8, 128, 1152), BF),
    "wd_v": ((18, 64, 1024), BF),
    "st": ((16, 128), F32),
    "qk_raw": ((4, 128, 384), F32),
    "qz": ((4, 512, 128), BF),
    "kv": ((16, 128, 256), BF),
    "kvt": ((128, 2048), BF),
    "pT": ((1152, 512), BF),
    "dsT": ((1152, 512), BF),
    "cosr": ((4, 128, 128), F32),
    "sinr": ((4, 128, 128), F32),
    "invl": ((4, 8, 512), F32),
    "oT": ((4, 256, 128), F32),
    "o_s": ((4, 128, 256), BF),
    "o_in": ((4, 128, 256), BF),
    "o_own": ((128, 1024), BF),
    "o_full": ((4, 128, 1024), BF),
    "mid": ((128, 1024), F32),
    "h2": ((4, 128, 1024), BF),
    "dm": ((4, 128, 1152), BF),
    "mixed": ((4, 128, 1152), BF),
    "dg": ((4, 128, 1152), BF),
    "du": ((4, 128, 1152), BF),
    "p2s": ((3, 128, 1024), BF),
    "p2r": ((3, 128, 1024), BF),
    "own": ((128, 1024), F32),
    "p3s": ((3, 128, 1024), BF),
    "p3r": ((3, 128, 1024), BF),
    "own3": ((128, 1024), F32),
    "dmid": ((128, 1024), F32),
    "da": ((128, 1024), BF),
    "da_c": ((4, 128, 256), BF),
    "dob": ((128, 1024), BF),
    "do_all": ((4, 128, 256), BF),
    "doz": ((512, 128), BF),
    "dkv": ((16, 128, 256), F32),
    "dkvb": ((4, 4, 128, 256), BF),
    "dkvr": ((3, 4, 128, 256), BF),
    "dqr": ((4, 128, 256), F32),
    "dqkv": ((4, 128, 512), BF),
    "p4r": ((3, 128, 1024), BF),
    "gF": ((4, 2, 128, 2304), BF),
    "gD": ((18, 64, 1024), BF),
    "gA": ((4, 2, 128, 768), BF),
    "r1F": ((4, 2, 64, 2304), BF),
    "r1D": ((18, 32, 1024), BF),
    "sD": ((4, 2, 2, 32, 1024), BF),
    "sX": ((2, 32, 1024), BF),
    "ax": ((3, 4, 32, 1152), BF),
    "at": ((4, 32, 1152), BF),
    "ay": ((3, 32, 1152), BF),
    "by": ((3, 2, 64, 1152), BF),
    "bt": ((2, 64, 1152), BF),
    "bx": ((3, 32, 1152), BF),
    "adx": ((3, 4, 2, 16, 512), BF),
    "adt": ((4, 2, 16, 512), BF),
    "ady": ((3, 2, 16, 512), BF),
    "bdy": ((3, 2, 2, 32, 512), BF),
    "bdt": ((2, 2, 32, 512), BF),
    "bdx": ((3, 2, 16, 512), BF),
    "xx": ((3, 16, 1024), BF),
    "xt": ((16, 1024), BF),
    "xy": ((3, 16, 1024), BF),
    "qax": ((3, 4, 32, 384), BF),
    "qat": ((4, 32, 384), BF),
    "qay": ((3, 32, 384), BF),
    "qby": ((3, 2, 64, 384), BF),
    "qbt": ((2, 64, 384), BF),
    "qbx": ((3, 32, 384), BF),
    "r1A": ((4, 2, 64, 768), BF),
    "oF": ((32, 2304), BF),
    "oD": ((3, 16, 1024), BF),
    "oA": ((32, 768), BF),
    "gsm": ((8, 8, 128), F32),
    "gs1": ((8, 8, 128), F32),
    "gs1s": ((8, 128), F32),
    "gs2": ((16, 8, 128), F32),
}
NSEM = 112


class Refs:
    pass


class Comm:
    def __init__(self, place, ssem, rsem):
        self.p, self.ssem, self.rsem = place, ssem, rsem
        self.n = 0
        self.sent = []

    def take(self, count=1):
        base = self.n
        self.n += count
        return base

    def copy(self, src, dst, i, dev):
        return pltpu.make_async_remote_copy(
            src_ref=src, dst_ref=dst, send_sem=self.ssem.at[i], recv_sem=self.rsem.at[i],
            device_id=dev, device_id_type=MESH,
        )

    def send(self, src, dst, i, dev):
        self.copy(src, dst, i, dev).start()
        self.sent.append((src, i))

    def part(self, src, dst, i, dev):
        self.copy(src, dst, i, dev).start()

    def whole(self, ref, i):
        self.sent.append((ref, i))

    def local(self, src, dst, i):
        return pltpu.make_async_copy(src, dst, self.rsem.at[i])

    def got(self, dst, i):
        self.copy(dst, dst, i, self.p.sib()).wait_recv()

    def flush(self, i):
        for src, j in self.sent:
            if j == i:
                self.copy(src, src, i, self.p.sib()).wait_send()
        self.sent = [e for e in self.sent if e[1] != i]

    def finish(self):
        for src, i in self.sent:
            self.copy(src, src, i, self.p.sib()).wait_send()
        self.sent = []


def kernel(*refs):
    r = Refs()
    names = INPUTS + list(OUTPUTS) + list(SCRATCH)
    for name, ref in zip(names, refs):
        setattr(r, name, ref)
    ssem, rsem = refs[len(names):]
    p = Place()
    m = Comm(p, ssem, rsem)

    def z_of(dz):
        return rem(p.z - dz + 4, 4)

    half = pl.ds(pl.multiple_of(p.c * 64, 64), 64)
    other = pl.ds(pl.multiple_of(64 - p.c * 64, 64), 64)
    zq = pl.ds(pl.multiple_of(p.z * 256, 256), 256)
    zk = pl.ds(pl.multiple_of(p.z * 128, 128), 128)
    dps = [rem(p.dp + 8 - k, 8) for k in range(8)]

    i_loc = m.take(4)
    parts = ((r.wq, zq, 0, 256), (r.wk, zk, 256, 128), (r.wv, zk, 384, 128))
    for w, cols, at, wid in parts:
        m.local(w.at[half, cols], r.wqkv.at[p.dp, half, pl.ds(at, wid)], i_loc).start()
    m.local(r.wo.at[half], r.wo_v.at[p.dp, half], i_loc + 1).start()

    def down_pieces(d):
        out = []
        for n in range(2):
            u = rem(2 * p.z + n - d + 8, 8)
            big = 9 * d + u
            out.append((u, 2 * lax.div(big, 8) + rem(big, 2)))
        big = 9 * d + 8
        return out + [(8, 2 * lax.div(big, 8) + rem(big, 2))], lax.div(d, 2) == p.z

    c32 = p.c * 32
    h32 = pl.ds(pl.multiple_of(c32, 32), 32)
    o32 = pl.ds(pl.multiple_of(32 - c32, 32), 32)
    i_ld = m.take(3)
    pieces, has_extra = down_pieces(p.dp)

    def down_local(n):
        u, hidx = pieces[n]
        src = r.wd.at[pl.ds(pl.multiple_of(u * 64 + c32, 32), 32)]
        return pltpu.make_async_copy(src, r.wd_v.at[hidx, h32], rsem.at[i_ld + n])

    for n in range(2):
        down_local(n).start()

    @pl.when(has_extra)
    def _():
        down_local(2).start()

    for src, dst, i in ((r.wg, r.wg_v, i_loc + 2), (r.wu, r.wu_v, i_loc + 3)):
        for t in range(9):
            cols = pl.ds(pl.multiple_of(t * 512 + p.z * 128, 128), 128)
            m.local(src.at[half, cols], dst.at[p.dp, half, pl.ds(t * 128, 128)], i).start()

    r.meta[0:1, :] = r.ga[...].astype(F32)
    r.meta[1:2, :] = r.gf[...].astype(F32)
    r.meta[2:3, :] = r.seg[...].astype(F32)
    r.meta[3:8, :] = jnp.zeros((5, 128), F32)

    bar = pltpu.get_barrier_semaphore()
    for k in range(1, 16):
        pl.semaphore_signal(bar, inc=1, device_id=p.speer(k), device_id_type=MESH)
    for k in range(1, 8):
        pl.semaphore_signal(bar, inc=1, device_id=p.dpeer(k), device_id_type=MESH)
    pl.semaphore_signal(bar, inc=1, device_id=p.xring(2), device_id_type=MESH)
    pl.semaphore_wait(bar, 23)

    class Shards:
        def __init__(self, buf, i_share):
            self.buf, self.share = buf, i_share
            self.iy, self.ix = m.take(3) - 1, m.take(1)

        def row(self, k, xl):
            return rem(p.y - k + 4, 4) * 2 + xl

        def quarter(self, t):
            return pl.ds(pl.multiple_of(p.c * 64 + (t - 1) * 32, 32), 32)

        def along_y(self):
            s = self.buf.at[p.dp, half]
            for k in (2, 1, 3):
                m.send(s, s, self.iy + k, p.ypeer(k))

        def along_x(self, k):
            d = self.row(k, p.xl)
            if k:
                m.got(self.buf.at[d, half], self.iy + k)
            for t in (1, 2):
                s = self.buf.at[d, self.quarter(t)]
                m.part(s, s, self.ix, p.xring(t))

        def to_core(self):
            m.whole(self.buf.at[0:4, half], self.ix)
            m.got(self.buf.at[0:4, half], self.ix)
            s = self.buf.at[:, half]
            m.send(s, s, self.share, p.sib())

        def done(self):
            m.got(self.buf.at[:, other], self.share)

    class Down:
        def __init__(self, i_share):
            self.share = i_share
            self.iy, self.ix = m.take(3) - 1, m.take(1)

        def start(self, d, t, i, dev):
            where, more = down_pieces(d)
            for n in range(3):
                rows = h32 if t == 0 else pl.ds(pl.multiple_of(c32 + (t - 1) * 16, 16), 16)
                s = r.wd_v.at[where[n][1], rows]
                if n < 2:
                    m.part(s, s, i, dev)
                else:

                    @pl.when(more)
                    def _():
                        m.part(s, s, i, dev)

        def wait(self, d, act):
            _, more = down_pieces(d)

            @pl.when(more)
            def _():
                act(r.wd_v.at[0:3, h32])

            @pl.when(jnp.logical_not(more))
            def _():
                act(r.wd_v.at[0:2, h32])

        def along_y(self):
            for k in (2, 1, 3):
                self.start(p.dp, 0, self.iy + k, p.ypeer(k))

        def along_x(self, k):
            d = rem(p.y - k + 4, 4) * 2 + p.xl
            if k:
                self.wait(d, lambda ref: m.got(ref, self.iy + k))
            for t in (1, 2):
                self.start(d, t, self.ix, p.xring(t))

        def to_core(self):
            m.whole(r.wd_v.at[0:9, h32], self.ix)
            m.got(r.wd_v.at[0:9, h32], self.ix)
            m.send(r.wd_v.at[:, h32], r.wd_v.at[:, h32], self.share, p.sib())

        def done(self):
            m.got(r.wd_v.at[:, o32], self.share)

        def finish(self):
            for k in (1, 2, 3):
                self.wait(p.dp, lambda ref: m.copy(ref, ref, self.iy + k, p.sib()).wait_send())

    i_share = m.take(5)
    w_qkv = Shards(r.wqkv, i_share)
    w_o = Shards(r.wo_v, i_share + 1)
    w_d = Down(i_share + 2)
    w_g = Shards(r.wg_v, i_share + 3)
    w_u = Shards(r.wu_v, i_share + 4)
    i_tok = m.take(3) - 1
    for dz in (2, 1, 3):
        m.send(r.tok, r.tok_all.at[dz], i_tok + dz, p.zpeer(dz))
    m.local(r.wqkv.at[0, half], r.wqkv.at[0, half], i_loc).wait()
    w_qkv.along_y()
    w_qkv.along_x(0)
    i_mseq = m.take()
    for k in range(1, 16):
        m.part(r.meta, r.mseq.at[p.sq], i_mseq, p.speer(k))
    m.whole(r.mseq.at[0:15], i_mseq)
    i_mdp = m.take()
    for k in range(1, 8):
        m.part(r.meta, r.mdp.at[p.dp], i_mdp, p.dpeer(k))
    m.whole(r.mdp.at[0:7], i_mdp)
    r.mseq[p.sq] = r.meta[...]
    r.mdp[p.dp] = r.meta[...]
    for k in (1, 3, 2):
        w_qkv.along_x(k)
    m.local(r.wo_v.at[0, half], r.wo_v.at[0, half], i_loc + 1).wait()
    w_o.along_y()
    for n in range(2):
        down_local(n).wait()

    @pl.when(has_extra)
    def _():
        down_local(2).wait()

    w_d.along_y()

    m.got(r.mseq.at[0:15], i_mseq)
    r.st[...] = seg_rows(r.mseq[:, 2, :])
    m.got(r.mdp.at[0:7], i_mdp)
    gain1 = jnp.concatenate([r.mdp[j, 0:1, :] for j in range(8)], axis=1)
    gain2 = jnp.concatenate([r.mdp[j, 1:2, :] for j in range(8)], axis=1)
    w_qkv.to_core()
    m.local(r.wg_v.at[0, half], r.wg_v.at[0, half], i_loc + 2).wait()
    w_g.along_y()
    m.local(r.wu_v.at[0, half], r.wu_v.at[0, half], i_loc + 3).wait()
    w_u.along_y()

    lanesign = jnp.where(lane_half(), -1.0, 1.0)
    freq = r.freq[...]
    for dz in range(4):
        i = 4 * z_of(dz) + p.g
        row = r.st[pl.ds(i, 1), :]
        pos = (lax.broadcasted_iota(jnp.int32, (1, 128), 1) + i * 128).astype(F32) - row
        ang = jnp.transpose(jnp.broadcast_to(pos, (128, 128))) * freq
        r.cosr[dz] = jnp.cos(ang)
        r.sinr[dz] = jnp.sin(ang) * lanesign
    w_qkv.done()

    wfull = r.wqkv[...].reshape(1024, 512)
    qg = r.gqk[0:1, :].astype(F32)
    kg = r.gqk[1:2, :].astype(F32)
    i_kv = m.take()
    i_kvx = m.take(4)
    i_kvf = m.take()

    def project(dz, x):
        x = x.astype(F32)
        r1 = lax.rsqrt(jnp.mean(x * x, axis=1, keepdims=True) + EPS)
        h = (x * r1 * gain1).astype(BF)
        r.tok_all[dz] = h
        o = dot(h, wfull)
        cs, sn = r.cosr[dz], r.sinr[dz]
        r.qk_raw[dz] = o[:, 0:384]
        rot = []
        for b, gn in ((0, qg), (1, qg), (2, kg)):
            v = o[:, b * 128:(b + 1) * 128]
            v = v * lax.rsqrt(head_mean(v * v) + EPS) * gn
            rot.append(v * cs + swap_halves(v) * sn)
        for hd, v in enumerate(spread_heads(rot[0], rot[1])):
            r.qz[dz, pl.ds(hd * 128, 128), :] = v.astype(BF)
        i = 4 * z_of(dz) + p.g
        r.kv[i, :, 0:128] = rot[2].astype(BF)
        r.kv[i, :, 128:256] = o[:, 384:512].astype(BF)
        m.send(r.kv.at[i], r.kv.at[i], i_kvx + dz, p.xpeer())
        m.part(r.kv.at[i], r.kv.at[i], i_kv, p.sib())

    project(0, r.tok[...])
    for dz in (1, 3, 2):
        m.got(r.tok_all.at[dz], i_tok + dz)
        project(dz, r.tok_all[dz])
    i_cot = m.take()
    for dz in (1, 3, 2):
        m.part(r.cot, r.cot_all.at[dz], i_cot, p.zpeer(dz))
    m.whole(r.cot_all.at[1:4], i_cot)
    r.cot_all[0] = r.cot[...]
    for w in (w_o, w_d):
        for k in (0, 1, 3, 2):
            w.along_x(k)
    gs = p.g + 1 - 2 * p.c
    gx = (1 - p.xh) * 2 + p.c
    gxs = (1 - p.xh) * 2 + 1 - p.c
    for dz in (0, 1, 3, 2):
        zz = 4 * z_of(dz)
        m.got(r.kv.at[zz + gx], i_kvx + dz)
        m.part(r.kv.at[zz + gx], r.kv.at[zz + gx], i_kvf, p.sib())
    four = r.kv.at[0:4]
    for i in (i_kv, i_kvf):
        m.whole(four, i)
        m.got(four, i)

    def turn(first):
        def one(j, carry):
            t = jnp.transpose(r.kv[j, :, first:first + 128].astype(F32))
            r.kvt[:, pl.ds(pl.multiple_of(j * 128, 128), 128)] = t.astype(BF)
            return carry

        lax.fori_loop(0, 16, one, 0)

    turn(128)

    def allowed_rows(i):
        row = r.st[pl.ds(i, 1), :].astype(jnp.int32)
        qi = lax.broadcasted_iota(jnp.int32, (1, 128), 1) + i * 128
        return jnp.concatenate([row] * 4, axis=1), jnp.concatenate([qi] * 4, axis=1)

    def window(i):
        return jnp.minimum(jnp.maximum(i - 8, 0), 7)

    def weights_of(kb, qv, row4, qi4):
        s = dot(r.kv[pl.ds(kb, 3), :, 0:128].reshape(384, 128), qv, NT)
        ki = lax.broadcasted_iota(jnp.int32, (384, 512), 0) + kb * 128
        return jnp.where((ki >= row4) & (ki <= qi4), jnp.exp2(s * (SCALE * LOG2E)), 0.0)

    def keys_turned(k0):
        return r.kvt[:, pl.ds(pl.multiple_of(k0 * 128, 128), 1152)]

    def heads_down(o):
        return jnp.concatenate(
            [o[(h // 2) * 64:(h // 2) * 64 + 64, h * 128:(h + 1) * 128] for h in range(4)], axis=0
        )

    def forward_chunk(dz):
        i = 4 * z_of(dz) + p.g
        k0 = window(i)
        row4, qi4 = allowed_rows(i)
        qv = r.qz[dz]
        total = jnp.zeros((8, 512), F32)
        for t in range(3):
            w = weights_of(k0 + 3 * t, qv, row4, qi4)
            total = total + jnp.sum(w.reshape(48, 8, 512), axis=0)
            r.pT[t * 384:(t + 1) * 384] = w.astype(BF)
        il = 1.0 / jnp.sum(total, axis=0, keepdims=True)
        r.invl[dz] = jnp.broadcast_to(il, (8, 512))
        full = heads_down(dot(keys_turned(k0), r.pT[...]) * il)
        r.oT[dz] = full
        r.o_s[dz] = jnp.transpose(full).astype(BF)

    i_o = m.take()
    for j in range(4):
        dz = (j + 1) % 4
        forward_chunk(dz)
        if dz:
            m.part(r.o_s.at[dz], r.o_in.at[p.z], i_o, p.zpeer(-dz))
        else:
            r.o_in[p.z] = r.o_s[0]
        if j in (0, 2):
            for k in (0, 1, 3, 2):
                (w_g, None, w_u)[j].along_x(k)
        if j == 1:
            w_o.to_core()
    m.whole(r.o_in.at[0:3], i_o)

    w_d.to_core()
    m.got(r.o_in.at[0:3], i_o)
    for j in range(4):
        r.o_own[:, j * 256:(j + 1) * 256] = r.o_in[j]
    w_o.done()
    x0 = r.tok[...].astype(F32)
    middle = x0 + dot(r.o_own[...], r.wo_v[...].reshape(1024, 1024))
    r.mid[...] = middle
    r2 = lax.rsqrt(jnp.mean(middle * middle, axis=1, keepdims=True) + EPS)
    r.h2[0] = (middle * r2 * gain2).astype(BF)
    i_h2 = m.take(3) - 1
    for dz in (2, 1, 3):
        m.send(r.h2.at[0], r.h2.at[dz], i_h2 + dz, p.zpeer(dz))
    i_of = m.take()
    for dz in (2, 1, 3):
        m.part(r.o_own, r.o_full.at[dz], i_of, p.zpeer(dz))
    m.whole(r.o_full.at[1:4], i_of)
    r.o_full[0] = r.o_own[...]

    turn(0)
    w_g.to_core()
    w_u.to_core()
    m.got(r.cot_all.at[1:4], i_cot)
    w_d.done()
    wd = r.wd_v[...].reshape(1152, 1024)
    cots = r.cot_all[...].reshape(512, 1024)

    def cols384(t):
        return pl.ds(pl.multiple_of(t * 384, 128), 384)

    def dm_tile(t, carry):
        w = r.wd_v[pl.ds(t * 6, 6)].reshape(384, 1024)
        r.dm[:, :, cols384(t)] = dot(cots, w, NT).astype(BF).reshape(4, 128, 384)
        return carry

    lax.fori_loop(0, 3, dm_tile, 0)
    w_g.done()
    w_u.done()

    i_p2 = m.take()
    for pair in range(2):
        two = slice(2 * pair, 2 * pair + 2)
        for dz in ((1,), (2, 3))[pair]:
            m.got(r.h2.at[dz], i_h2 + dz)
        hh = r.h2[two].reshape(256, 1024)

        def ffn_tile(t, carry):
            cols = cols384(t)
            gate = dot(hh, r.wg_v[:, :, cols].reshape(1024, 384))
            up = dot(hh, r.wu_v[:, :, cols].reshape(1024, 384))
            sig = 1.0 / (1.0 + jnp.exp(-gate))
            act = gate * sig
            dmt = r.dm[two, :, cols].astype(F32).reshape(256, 384)
            r.mixed[two, :, cols] = (act * up).astype(BF).reshape(2, 128, 384)
            r.dg[two, :, cols] = (dmt * up * sig * (1.0 + gate * (1.0 - sig))).astype(BF).reshape(2, 128, 384)
            r.du[two, :, cols] = (dmt * act).astype(BF).reshape(2, 128, 384)
            return carry

        lax.fori_loop(0, 3, ffn_tile, 0)
        part = dot(r.dg[two].reshape(256, 1152), r.wg_v[...].reshape(1024, 1152), NT)
        part += dot(r.du[two].reshape(256, 1152), r.wu_v[...].reshape(1024, 1152), NT)
        if pair == 0:
            r.own[...] = part[0:128]
            r.p2s[0] = part[128:256].astype(BF)
            m.part(r.p2s.at[0], r.p2r.at[0], i_p2, p.zpeer(-1))
        else:
            r.p2s[1] = part[0:128].astype(BF)
            m.part(r.p2s.at[1], r.p2r.at[1], i_p2, p.zpeer(-2))
            r.p2s[2] = part[128:256].astype(BF)
            m.part(r.p2s.at[2], r.p2r.at[2], i_p2, p.zpeer(-3))

    i_r1 = m.take(3)
    h2t = r.h2[...].reshape(512, 1024)

    def gate_up_tile(t, carry):
        cols = cols384(t)
        r.gF[:, :, :, cols] = dot(h2t, r.dg[:, :, cols].reshape(512, 384), TN).astype(BF).reshape(4, 2, 128, 384)
        r.gF[:, :, :, cols384(t + 3)] = dot(h2t, r.du[:, :, cols].reshape(512, 384), TN).astype(BF).reshape(4, 2, 128, 384)
        return carry

    lax.fori_loop(0, 3, gate_up_tile, 0)
    m.send(r.gF.at[:, :, other], r.r1F, i_r1, p.sib())

    def down_tile(t, carry):
        w = r.mixed[:, :, cols384(t)].reshape(512, 384)
        r.gD[pl.ds(t * 6, 6)] = dot(w, cots, TN).astype(BF).reshape(6, 64, 1024)
        return carry

    lax.fori_loop(0, 3, down_tile, 0)
    m.send(r.gD.at[:, o32], r.r1D, i_r1 + 1, p.sib())
    r.own3[...] = dot(r.mixed[0], wd)

    def out_chunk(dz, carry):
        r.p3s[dz - 1] = dot(r.mixed[dz], wd).astype(BF)
        return carry

    lax.fori_loop(1, 4, out_chunk, 0)

    m.whole(r.p2s, i_p2)
    m.got(r.p2r, i_p2)
    dh2 = r.own[...] + r.p2r[0].astype(F32) + r.p2r[1].astype(F32) + r.p2r[2].astype(F32)
    middle = r.mid[...]
    r2 = lax.rsqrt(jnp.mean(middle * middle, axis=1, keepdims=True) + EPS)
    small2 = jnp.sum(dh2 * middle * r2, axis=0, keepdims=True)
    wdh = dh2 * gain2
    dmid = r.cot[...].astype(F32) + r2 * wdh - middle * (r2 * r2 * r2) * jnp.mean(wdh * middle, axis=1, keepdims=True)
    r.dmid[...] = dmid
    r.da[...] = dmid.astype(BF)
    r.dob[...] = dot(r.da[...], r.wo_v[...].reshape(1024, 1024), NT).astype(BF)
    i_do = m.take()

    def zcols(z):
        return pl.ds(pl.multiple_of(z * 256, 256), 256)

    for dz in (2, 1, 3):
        m.part(r.dob.at[:, zcols(rem(p.z + dz, 4))], r.do_all.at[dz], i_do, p.zpeer(dz))
    m.whole(r.do_all.at[1:4], i_do)
    r.do_all[0] = r.dob[:, zq]
    i_p3 = m.take()
    i_dc = m.take()
    for dz in (2, 1, 3):
        m.part(r.da.at[:, zcols(rem(p.z + dz, 4))], r.da_c.at[dz], i_dc, p.zpeer(dz))
    m.whole(r.da_c.at[1:4], i_dc)
    for dz in (2, 1, 3):
        m.part(r.p3s.at[dz - 1], r.p3r.at[dz - 1], i_p3, p.zpeer(-dz))
    m.whole(r.p3s, i_p3)
    r.da_c[0] = r.da[:, zq]

    m.got(r.r1F, i_r1)
    m.got(r.r1D, i_r1 + 1)

    def add_core(d, carry):
        a, b = lax.div(d, 2), rem(d, 2)
        r.r1F[a, b] = (r.r1F[a, b].astype(F32) + r.gF[a, b, half].astype(F32)).astype(BF)
        where, more = down_pieces(d)
        for n in range(2):
            t = where[n][1]
            r.sD[a, b, n] = (r.r1D[t].astype(F32) + r.gD[t, h32].astype(F32)).astype(BF)

        @pl.when(more)
        def _():
            t = where[2][1]
            r.sX[b] = (r.r1D[t].astype(F32) + r.gD[t, h32].astype(F32)).astype(BF)

        return carry

    lax.fori_loop(0, 8, add_core, 0)

    def rows_of(x, n):
        return pl.ds(pl.multiple_of(x * n, n), n)

    class XFirst:
        def __init__(self, src, mid1, tot, mid2):
            self.src, self.mid1, self.tot, self.mid2 = src, mid1, tot, mid2
            self.i1, self.i2 = m.take(), m.take()

        def one(self):
            for t in (3, 1, 2):
                m.part(self.src(t), self.mid1.at[t - 1], self.i1, p.xring(t))
            m.whole(self.mid1, self.i1)

        def two(self):
            m.got(self.mid1, self.i1)

            def add(n, carry):
                v = self.src(0).at[n][...].astype(F32)
                for t in range(3):
                    v = v + self.mid1[t, n].astype(F32)
                self.tot[n] = v.astype(BF)
                return carry

            lax.fori_loop(0, 4, add, 0)
            for k in (2, 1, 3):
                m.part(self.tot.at[rem(p.y + k, 4)], self.mid2.at[k - 1], self.i2, p.ypeer(k))
            m.whole(self.mid2, self.i2)

        def sum(self):
            m.got(self.mid2, self.i2)
            v = self.tot[p.y].astype(F32)
            for k in range(3):
                v = v + self.mid2[k].astype(F32)
            return v.astype(BF)

    class YFirst:
        def __init__(self, src, part, mid1, tot, mid2):
            self.src, self.part, self.mid1, self.tot, self.mid2 = src, part, mid1, tot, mid2
            self.i1, self.i2 = m.take(), m.take()

        def one(self):
            for k in (2, 1, 3):
                m.part(self.src(rem(p.y + k, 4)), self.mid1.at[k - 1], self.i1, p.ypeer(k))
            m.whole(self.mid1, self.i1)

        def two(self):
            m.got(self.mid1, self.i1)

            def add(n, carry):
                v = self.src(p.y).at[n][...].astype(F32)
                for k in range(3):
                    v = v + self.mid1[k, n].astype(F32)
                self.tot[n] = v.astype(BF)
                return carry

            lax.fori_loop(0, 2, add, 0)
            for t in (3, 1, 2):
                m.part(self.part(self.tot, t), self.mid2.at[t - 1], self.i2, p.xring(t))
            m.whole(self.mid2, self.i2)

        def sum(self):
            m.got(self.mid2, self.i2)
            v = self.part(self.tot, 0)[...].astype(F32)
            for t in range(3):
                v = v + self.mid2[t].astype(F32)
            return v.astype(BF)

    def rows_x(buf, c0, c1):
        return lambda t: buf.at[:, p.xplace(t)[0], rows_of(p.xplace(t)[1], 32), c0:c1]

    def rows_y(buf, c0, c1):
        return lambda y: buf.at[y, :, :, c0:c1]

    def part_y(tot, t):
        xl, xh = p.xplace(t)
        return tot.at[xl, rows_of(xh, 32)]

    def part_d(tot, t):
        xl, xh = p.xplace(t)
        return tot.at[xl, :, rows_of(xh, 16)]

    sums = [
        XFirst(rows_x(r.r1F, 0, 1152), r.ax, r.at, r.ay),
        YFirst(rows_y(r.r1F, 1152, 2304), part_y, r.by, r.bt, r.bx),
        XFirst(
            lambda t: r.sD.at[:, p.xplace(t)[0], :, rows_of(p.xplace(t)[1], 16), 0:512], r.adx, r.adt, r.ady
        ),
        YFirst(lambda y: r.sD.at[y, :, :, :, 512:1024], part_d, r.bdy, r.bdt, r.bdx),
    ]
    for e in sums:
        e.one()
    i_x1 = m.take()
    i_x2 = m.take()
    for t in (3, 1, 2):
        xl, xh = p.xplace(t)
        m.part(r.sX.at[xl, rows_of(xh, 16)], r.xx.at[t - 1], i_x1, p.xring(t))
    m.whole(r.xx, i_x1)

    r.dkv[...] = jnp.zeros_like(r.dkv)
    m.got(r.do_all.at[1:4], i_do)

    def backward_chunk(j, carry):
        dz = j
        i = 4 * z_of(dz) + p.g
        row4, qi4 = allowed_rows(i)
        do = r.do_all[dz].astype(F32)
        for hd, v in enumerate(spread_heads(do[:, 0:128], do[:, 128:256])):
            r.doz[pl.ds(hd * 128, 128), :] = v.astype(BF)
        prod = jnp.transpose(do) * r.oT[dz]
        drow = jnp.concatenate(
            [jnp.sum(prod[h * 64:(h + 1) * 64], axis=0, keepdims=True) for h in range(4)], axis=1
        )
        il = r.invl[dz, 0:1, :]
        qv = r.qz[dz]
        dov = r.doz[...]
        k0 = window(i)
        for t in range(3):
            rows = slice(t * 384, (t + 1) * 384)
            w = weights_of(k0 + 3 * t, qv, row4, qi4) * il
            r.pT[rows] = w.astype(BF)
            dp = dot(r.kv[pl.ds(k0 + 3 * t, 3), :, 128:256].reshape(384, 128), dov, NT)
            r.dsT[rows] = (w * (dp - drow)).astype(BF)
        nine = pl.ds(k0, 9)
        r.dkv[nine, :, 0:128] += dot(r.dsT[...], qv).reshape(9, 128, 128)
        r.dkv[nine, :, 128:256] += dot(r.pT[...], dov).reshape(9, 128, 128)
        r.dqr[dz] = jnp.transpose(heads_down(dot(keys_turned(k0), r.dsT[...]) * SCALE))
        return carry

    lax.fori_loop(0, 4, backward_chunk, 0)

    lane = lax.broadcasted_iota(jnp.int32, (1, 256), 1)
    kscale = jnp.where(lane < 128, SCALE, 1.0)
    r.dkvb[...] = (r.dkv[...] * kscale.reshape(1, 1, 256)).astype(BF).reshape(4, 4, 128, 256)
    i_dkv = m.take()
    xs = (p.dp, p.z * 4 + gxs)
    m.part(r.dkvb.at[:, gx], r.dkvr.at[1], i_dkv, p.xpeer())
    m.part(r.dkvb.at[:, gxs], r.dkvr.at[2], i_dkv, xs)
    m.part(r.dkvb.at[:, gs], r.dkvr.at[0], i_dkv, p.sib())
    m.whole(r.dkvr, i_dkv)

    for e in sums:
        e.two()
    m.got(r.xx, i_x1)
    v = r.sX[p.xl, rows_of(p.xh, 16)].astype(F32)
    for t in range(3):
        v = v + r.xx[t].astype(F32)
    r.xt[...] = v.astype(BF)
    kz = rem(p.z - p.y + 4, 4)

    @pl.when(kz != 0)
    def _():
        m.part(r.xt, r.xy.at[kz - 1], i_x2, (p.z * 2 + p.xl, p.sq))

    m.got(r.o_full.at[1:4], i_of)
    m.got(r.da_c.at[1:4], i_dc)
    m.got(r.p3r, i_p3)
    r.gA[:, :, :, 512:768] = dot(
        r.o_full[...].reshape(512, 1024), r.da_c[...].reshape(512, 256), TN
    ).astype(BF).reshape(4, 2, 128, 256)
    r.block_out[...] = (
        r.mid[...] + r.own3[...] + r.p3r[0].astype(F32) + r.p3r[1].astype(F32) + r.p3r[2].astype(F32)
    ).astype(BF)

    r.oF[:, 0:1152] = sums[0].sum()
    r.oF[:, 1152:2304] = sums[1].sum()
    r.oD[0:2, :, 0:512] = sums[2].sum()
    r.oD[0:2, :, 512:1024] = sums[3].sum()

    @pl.when(kz == 0)
    def _():
        v = r.xt[...].astype(F32)
        m.got(r.xy, i_x2)
        for k in range(3):
            v = v + r.xy[k].astype(F32)
        r.oD[2] = v.astype(BF)

    @pl.when(kz != 0)
    def _():
        r.oD[2] = jnp.zeros((16, 1024), BF)

    def seq_at(z, g):
        return rem(z + 8, 4) * 4 + g

    class Gather:
        def __init__(self, own, buf, order):
            self.own, self.buf, self.order = own, buf, order
            self.il, self.ix, self.iz, self.ic = m.take(), m.take(), m.take(), m.take()

        def on(self, src, s, where):
            if "x" in where:
                m.part(src, s, self.ix, p.xpeer())
            if "z" in where:
                for dz in (2, 1, 3):
                    m.part(src, s, self.iz, p.zpeer(dz))
            if "b" in where:
                for dz in (2, 1, 3):
                    m.part(src, s, self.iz, (p.dp, seq_at(p.z + dz, gx)))
            if "c" in where:
                m.part(src, s, self.ic, p.sib())

        def got(self, n, i):
            m.got(self.buf.at[0:n], i)

        def slot(self, dz, g):
            return self.buf.at[seq_at(p.z - dz, g)]

        def first(self):
            m.local(self.own, self.slot(0, p.g), self.il).start()
            self.on(self.own, self.slot(0, p.g), "zxcb" if self.order == "zx" else "zxc")

        def second(self):
            if self.order == "x":
                self.got(1, self.ix)
                s = self.slot(0, gx)
                self.on(s, s, "zc")
            elif self.order == "z":
                self.got(3, self.iz)
                for dz in (1, 2, 3):
                    s = self.slot(dz, p.g)
                    self.on(s, s, "xc")
            else:
                self.got(1, self.ix)
                self.got(6, self.iz)
                for dz in range(4):
                    for g in (p.g, gx)[dz == 0:]:
                        s = self.slot(dz, g)
                        self.on(s, s, "c")

        def third(self):
            if self.order == "x":
                self.got(6, self.iz)
                for dz in (1, 2, 3):
                    for g in (p.g, gx):
                        s = self.slot(dz, g)
                        self.on(s, s, "c")
            elif self.order == "z":
                self.got(4, self.ix)
                for dz in range(4):
                    s = self.slot(dz, gx)
                    self.on(s, s, "c")

        def last(self):
            n = {"x": (1, 6), "z": (4, 3), "zx": (1, 6)}[self.order]
            m.whole(self.buf.at[0:n[0]], self.ix)
            m.whole(self.buf.at[0:n[1]], self.iz)
            m.whole(self.buf.at[0:8], self.ic)
            self.got(8, self.ic)
            m.local(self.own, self.slot(0, p.g), self.il).wait()

    ag_f = Gather(r.oF, r.fF, "z")
    ag_d = Gather(r.oD, r.fD, "x")
    ag_a = Gather(r.oA, r.fA, "zx")
    ag_f.first()
    ag_d.first()

    m.got(r.dkvr, i_dkv)
    sq_acc = jnp.zeros((1, 128), F32)
    sk_acc = jnp.zeros((1, 128), F32)
    for dz in range(4):
        zz = z_of(dz)
        i = 4 * zz + p.g
        dkv = r.dkv[i] * kscale
        for n in range(3):
            dkv = dkv + r.dkvr[n, zz].astype(F32)
        cs, sn = r.cosr[dz], r.sinr[dz]
        grads = (r.dqr[dz, :, 0:128], r.dqr[dz, :, 128:256], dkv[:, 0:128])
        for b, gr in enumerate(grads):
            gn = qg if b < 2 else kg
            v = r.qk_raw[dz, :, b * 128:(b + 1) * 128]
            f = lax.rsqrt(head_mean(v * v) + EPS)
            dn = gr * cs - swap_halves(gr) * sn
            add = jnp.sum(dn * v * f, axis=0, keepdims=True)
            if b < 2:
                sq_acc = sq_acc + add
            else:
                sk_acc = sk_acc + add
            wn = dn * gn
            r.dqkv[dz, :, b * 128:(b + 1) * 128] = (f * wn - v * (f * f * f) * head_mean(wn * v)).astype(BF)
        r.dqkv[dz, :, 384:512] = dkv[:, 128:256].astype(BF)
    r.gA[:, :, :, 0:512] = dot(
        r.tok_all[...].reshape(512, 1024), r.dqkv[...].reshape(512, 512), TN
    ).astype(BF).reshape(4, 2, 128, 512)
    m.send(r.gA.at[:, :, other], r.r1A, i_r1 + 2, p.sib())
    i_p4 = m.take()
    m.flush(i_p2)
    for dz in (2, 1, 3):
        r.p2s[dz - 1] = dot(r.dqkv[dz], r.wqkv[...].reshape(1024, 512), NT).astype(BF)
        m.part(r.p2s.at[dz - 1], r.p4r.at[dz - 1], i_p4, p.zpeer(-dz))
    m.whole(r.p2s, i_p4)
    r.own[...] = dot(r.dqkv[0], r.wqkv[...].reshape(1024, 512), NT)
    m.got(r.r1A, i_r1 + 2)
    r.r1A[...] = (r.r1A[...].astype(F32) + r.gA[:, :, half].astype(F32)).astype(BF)
    sums_a = [
        XFirst(rows_x(r.r1A, 0, 384), r.qax, r.qat, r.qay),
        YFirst(rows_y(r.r1A, 384, 768), part_y, r.qby, r.qbt, r.qbx),
    ]
    for e in sums_a:
        e.one()
    ag_f.second()
    ag_d.second()

    for e in sums_a:
        e.two()

    m.got(r.p4r, i_p4)
    dh = r.own[...] + r.p4r[0].astype(F32) + r.p4r[1].astype(F32) + r.p4r[2].astype(F32)
    x0 = r.tok[...].astype(F32)
    r1 = lax.rsqrt(jnp.mean(x0 * x0, axis=1, keepdims=True) + EPS)
    small1 = jnp.sum(dh * x0 * r1, axis=0, keepdims=True)
    wdh = dh * gain1
    r.input_grad[...] = (
        r.dmid[...] + r1 * wdh - x0 * (r1 * r1 * r1) * jnp.mean(wdh * x0, axis=1, keepdims=True)
    ).astype(BF)

    both = lambda v: v + pltpu.roll(v, 64, 1)
    for d in range(8):
        cols = slice(d * 128, (d + 1) * 128)
        r.gsm[d] = jnp.concatenate(
            [small1[:, cols], small2[:, cols], both(sq_acc), both(sk_acc), jnp.zeros((4, 128), F32)], axis=0
        )
    i_s1 = m.take()
    i_s2 = m.take()
    for k in range(1, 8):
        m.part(r.gsm.at[rem(p.dp + k, 8)], r.gs1.at[k], i_s1, p.dpeer(k))
    m.whole(r.gs1.at[1:8], i_s1)
    r.gs1[0] = r.gsm[p.dp]
    m.got(r.gs1.at[1:8], i_s1)
    r.gs1s[...] = jnp.sum(r.gs1[...], axis=0)
    for k in range(1, 16):
        m.part(r.gs1s, r.gs2.at[k], i_s2, p.speer(k))
    m.whole(r.gs2.at[1:16], i_s2)
    r.gs2[0] = r.gs1s[...]

    r.oA[:, 0:384] = sums_a[0].sum()
    r.oA[:, 384:768] = sums_a[1].sum()
    ag_a.first()
    ag_f.third()
    ag_d.third()
    ag_a.second()
    m.got(r.gs2.at[1:16], i_s2)
    r.g_small[...] = jnp.sum(r.gs2[...], axis=0)
    ag_f.last()
    ag_d.last()
    ag_a.last()

    m.finish()
    w_d.finish()

    @pl.when(kz != 0)
    def _():
        m.copy(r.xt, r.xt, i_x2, p.sib()).wait_send()

    assert m.n <= NSEM, m.n


def block(args):
    vm = pl.BlockSpec(memory_space=pltpu.VMEM)
    hb = pl.BlockSpec(memory_space=pl.ANY)
    return pl.pallas_call(
        kernel,
        out_shape=tuple(jax.ShapeDtypeStruct(s, d) for s, d in OUTPUTS.values()),
        in_specs=[vm] * 6 + [hb] * 7 + [vm],
        out_specs=tuple(hb if name[0] == "f" else vm for name in OUTPUTS),
        scratch_shapes=[pltpu.VMEM(s, d) for s, d in SCRATCH.values()]
        + [pltpu.SemaphoreType.DMA((NSEM,)), pltpu.SemaphoreType.DMA((NSEM,))],
        compiler_params=pltpu.CompilerParams(
            collective_id=0, has_side_effects=True, vmem_limit_bytes=63 * 2**20
        ),
        name="block",
    )(*args)


PLACED = {
    "g_gate": (128, 4608),
    "g_up": (128, 4608),
    "g_down": (576, 1024),
    "g_q": (128, 1024),
    "g_k": (128, 512),
    "g_v": (128, 512),
    "g_out": (128, 1024),
}

LAID = {
    "g_attn": ((1, 128), F32),
    "g_ffn": ((1, 128), F32),
    "g_qg": ((1, 64), F32),
    "g_kg": ((1, 64), F32),
    **{name: (shape, F32) for name, shape in PLACED.items()},
}


def lay_kernel(f_f, f_d, f_a, sm, *refs):
    outs = dict(zip(LAID, refs[:len(LAID)]))
    v_f, v_d, v_a = refs[len(LAID):len(LAID) + 3]
    stage = dict(zip(PLACED, refs[len(LAID) + 3:len(LAID) + 3 + len(PLACED)]))
    isem, osem = refs[len(LAID) + 3 + len(PLACED):]
    p = Place()
    ins = [
        pltpu.make_async_copy(f_f, v_f, isem.at[0]),
        pltpu.make_async_copy(f_d, v_d, isem.at[1]),
        pltpu.make_async_copy(f_a, v_a, isem.at[2]),
    ]
    for q in ins:
        q.start()
    outs["g_attn"][...] = sm[0:1, :]
    outs["g_ffn"][...] = sm[1:2, :]
    outs["g_qg"][...] = sm[2:3, 0:64]
    outs["g_kg"][...] = sm[3:4, 0:64]

    def place(name):
        n = list(PLACED).index(name)
        return pltpu.make_async_copy(stage[name], outs[name], osem.at[n])

    def row_of(s):
        g = rem(s, 4)
        return pl.ds(pl.multiple_of(rem(g, 2) * 64 + lax.div(g, 2) * 32, 32), 32)

    ins[0].wait()
    for name, base in (("g_gate", 0), ("g_up", 1152)):

        def lay(s, carry):
            z = lax.div(s, 4)
            for t in range(9):
                cols = pl.ds(pl.multiple_of(t * 512 + z * 128, 128), 128)
                stage[name][row_of(s), cols] = v_f[s, :, base + t * 128:base + (t + 1) * 128].astype(F32)
            return carry

        lax.fori_loop(0, 16, lay, 0)
        place(name).start()
    ins[1].wait()

    def lay_down(s, carry):
        z = lax.div(s, 4)
        g = rem(s, 4)
        sub = rem(g, 2) * 32 + lax.div(g, 2) * 16
        for n in range(2):
            u = rem(2 * z + n - p.dp + 8, 8)
            stage["g_down"][pl.ds(pl.multiple_of(u * 64 + sub, 16), 16), :] = v_d[s, n].astype(F32)

        @pl.when(lax.div(p.dp, 2) == z)
        def _():
            stage["g_down"][pl.ds(pl.multiple_of(8 * 64 + sub, 16), 16), :] = v_d[s, 2].astype(F32)

        return carry

    lax.fori_loop(0, 16, lay_down, 0)
    place("g_down").start()
    ins[2].wait()

    def lay_attn(s, carry):
        z = lax.div(s, 4)
        row = row_of(s)
        c256 = pl.ds(pl.multiple_of(z * 256, 256), 256)
        c128 = pl.ds(pl.multiple_of(z * 128, 128), 128)
        stage["g_q"][row, c256] = v_a[s, :, 0:256].astype(F32)
        stage["g_k"][row, c128] = v_a[s, :, 256:384].astype(F32)
        stage["g_v"][row, c128] = v_a[s, :, 384:512].astype(F32)
        stage["g_out"][row, c256] = v_a[s, :, 512:768].astype(F32)
        return carry

    lax.fori_loop(0, 16, lay_attn, 0)
    for name in ("g_q", "g_k", "g_v", "g_out"):
        place(name).start()
    for name in PLACED:
        place(name).wait()


def lay_out(o):
    hb = pl.BlockSpec(memory_space=pl.ANY)
    vm = pl.BlockSpec(memory_space=pltpu.VMEM)
    small = ("g_attn", "g_ffn", "g_qg", "g_kg")
    got = pl.pallas_call(
        lay_kernel,
        out_shape=tuple(jax.ShapeDtypeStruct(s, d) for s, d in LAID.values()),
        in_specs=[hb] * 3 + [vm],
        out_specs=tuple(vm if n in small else hb for n in LAID),
        scratch_shapes=[pltpu.VMEM(*OUTPUTS[n]) for n in ("fF", "fD", "fA")]
        + [pltpu.VMEM(s, F32) for s in PLACED.values()]
        + [pltpu.SemaphoreType.DMA((3,)), pltpu.SemaphoreType.DMA((len(PLACED),))],
        compiler_params=pltpu.CompilerParams(vmem_limit_bytes=62 * 2**20),
        name="lay",
    )(o["fF"], o["fD"], o["fA"], o["g_small"])
    return dict(zip(LAID, got))


def local(
    tokens, segment_ids, attn_gain, w_query, w_key, w_value, w_out, ffn_gain, w_gate, w_up, w_down,
    query_gain, key_gain, cotangent,
):
    inverse = ROPE_BASE ** (-(np.arange(32).astype(np.float32) * np.float32(2.0) / np.float32(64)))
    freq = jnp.asarray(np.tile(inverse.astype(np.float32), 4)[None])
    gqk = jnp.stack([jnp.tile(query_gain, 2), jnp.tile(key_gain, 2)])
    o = block(
        (
            tokens, segment_ids, attn_gain[None], ffn_gain[None], gqk, freq, w_query, w_key, w_value,
            w_out, w_gate, w_up, w_down, cotangent,
        )
    )
    o = dict(zip(OUTPUTS, o))
    w = lay_out(o)
    return (
        o["block_out"], o["input_grad"], w["g_attn"].reshape(128), w["g_q"], w["g_k"], w["g_v"], w["g_out"],
        w["g_ffn"].reshape(128), w["g_gate"], w["g_up"], w["g_down"], w["g_qg"].reshape(64),
        w["g_kg"].reshape(64),
    )


def solution(mesh):
    both = ("dp", "seq")
    w = P("dp", None)
    return jax.shard_map(
        local,
        mesh=mesh,
        in_specs=(P(both, None), P("dp", "seq"), P("dp"), w, w, w, w, P("dp"), w, w, w, P(), P(), P(both, None)),
        out_specs=(P(both, None), P(both, None), P("dp"), w, w, w, w, P("dp"), w, w, w, P(), P()),
        check_vma=False,
    )
```

```python
import math

import jax
import jax.numpy as jnp
import numpy as np
from jax import lax
from jax.experimental import pallas as pl
from jax.experimental.pallas import tpu as pltpu
from jax.sharding import PartitionSpec as P

MESH = pl.DeviceIdType.MESH
F32 = jnp.float32
BF = jnp.bfloat16
EPS = 1e-05
ROPE_BASE = 1000000.0
NN = (((1,), (0,)), ((), ()))
NT = (((1,), (1,)), ((), ()))
TN = (((0,), (0,)), ((), ()))
SCALE = 0.125
LOG2E = math.log2(math.e)


def dot(a, b, dims=NN, precision=None):
    return lax.dot_general(a, b, dims, preferred_element_type=F32, precision=precision)


def rem(a, b):
    return lax.rem(a, b)


class Place:
    def __init__(self):
        self.dp = lax.axis_index("dp")
        self.sq = lax.axis_index("seq")
        self.y = lax.div(self.dp, 2)
        self.xl = rem(self.dp, 2)
        self.z = lax.div(self.sq, 4)
        self.g = rem(self.sq, 4)
        self.xh = lax.div(self.g, 2)
        self.c = rem(self.sq, 2)

    def zpeer(self, dz):
        return (self.dp, rem(self.z + dz + 4, 4) * 4 + self.g)

    def sib(self):
        return (self.dp, self.sq + 1 - 2 * self.c)

    def xpeer(self):
        return (self.dp, self.z * 4 + (1 - self.xh) * 2 + self.c)

    def dpeer(self, k):
        return (rem(self.dp + k + 8, 8), self.sq)

    def speer(self, k):
        return (self.dp, rem(self.sq + k + 16, 16))

    def ypeer(self, k):
        return (rem(self.y + k + 4, 4) * 2 + self.xl, self.sq)

    def xring(self, t):
        xl = self.xl if t == 3 else 1 - self.xl
        return (self.y * 2 + xl, self.sq if t == 1 else self.z * 4 + (1 - self.xh) * 2 + self.c)

    def xplace(self, t):
        return (self.xl if t in (0, 3) else 1 - self.xl), (self.xh if t in (0, 1) else 1 - self.xh)


def seg_rows(ids):
    start = jnp.zeros_like(ids)
    for j in range(1, 8):
        below = jnp.sum(jnp.where(ids < j, 1.0, 0.0), keepdims=True)
        start = jnp.where(ids == j, below, start)
    return start


def lane_half():
    return lax.rem(lax.broadcasted_iota(jnp.int32, (1, 128), 1), 64) < 32


def swap_halves(x):
    return jnp.where(lane_half(), pltpu.roll(x, 96, 1), pltpu.roll(x, 32, 1))


def head_mean(x):
    a = lax.div(lax.broadcasted_iota(jnp.int32, (128, 128), 0), 64)
    b = lax.div(lax.broadcasted_iota(jnp.int32, (128, 128), 1), 64)
    block = jnp.where(a == b, 1.0 / 64, 0.0)
    return dot(x, block, NN, lax.Precision.HIGHEST)


def spread_heads(first, second):
    lo = lax.broadcasted_iota(jnp.int32, (1, 128), 1) < 64
    return [
        jnp.where(lo, first, 0.0),
        jnp.where(lo, pltpu.roll(first, 64, 1), 0.0),
        jnp.where(lo, 0.0, pltpu.roll(second, 64, 1)),
        jnp.where(lo, 0.0, second),
    ]


INPUTS = ["tok", "seg", "ga", "gf", "gq", "gk", "freq", "wq", "wk", "wv", "wo", "wg", "wu", "wd", "cot"]
OUTPUTS = {
    "block_out": ((128, 1024), BF),
    "input_grad": ((128, 1024), BF),
    "fF": ((16, 32, 2304), BF),
    "fD": ((16, 3, 16, 1024), BF),
    "fA": ((16, 32, 768), BF),
    "g_small": ((8, 128), F32),
}
SCRATCH = {
    "tok_all": ((4, 128, 1024), BF),
    "cot_all": ((4, 128, 1024), BF),
    "meta": ((8, 128), F32),
    "mseq": ((16, 8, 128), F32),
    "mdp": ((8, 8, 128), F32),
    "wqkv": ((8, 128, 512), BF),
    "wo_v": ((8, 128, 1024), BF),
    "wg_v": ((8, 128, 1152), BF),
    "wu_v": ((8, 128, 1152), BF),
    "wd_v": ((18, 64, 1024), BF),
    "st": ((16, 128), F32),
    "qk_raw": ((4, 128, 384), F32),
    "qz": ((4, 512, 128), BF),
    "kv": ((16, 128, 256), BF),
    "kvt": ((128, 2048), BF),
    "pT": ((1152, 512), BF),
    "dsT": ((1152, 512), BF),
    "cosr": ((4, 128, 128), F32),
    "sinr": ((4, 128, 128), F32),
    "invl": ((4, 8, 512), F32),
    "oT": ((4, 256, 128), F32),
    "o_s": ((4, 128, 256), BF),
    "o_in": ((4, 128, 256), BF),
    "o_own": ((128, 1024), BF),
    "o_full": ((4, 128, 1024), BF),
    "mid": ((128, 1024), F32),
    "h2": ((4, 128, 1024), BF),
    "dm": ((4, 128, 1152), BF),
    "mixed": ((4, 128, 1152), BF),
    "dg": ((4, 128, 1152), BF),
    "du": ((4, 128, 1152), BF),
    "p2s": ((3, 128, 1024), BF),
    "p2r": ((3, 128, 1024), BF),
    "own": ((128, 1024), F32),
    "p3s": ((3, 128, 1024), BF),
    "p3r": ((3, 128, 1024), BF),
    "own3": ((128, 1024), F32),
    "dmid": ((128, 1024), F32),
    "da": ((128, 1024), BF),
    "da_c": ((4, 128, 256), BF),
    "dob": ((128, 1024), BF),
    "do_all": ((4, 128, 256), BF),
    "doz": ((512, 128), BF),
    "dkv": ((16, 128, 256), F32),
    "dkvb": ((4, 4, 128, 256), BF),
    "dkvr": ((3, 4, 128, 256), BF),
    "dqr": ((4, 128, 256), F32),
    "dqkv": ((4, 128, 512), BF),
    "p4r": ((3, 128, 1024), BF),
    "gF": ((4, 2, 128, 2304), BF),
    "gD": ((18, 64, 1024), BF),
    "gA": ((4, 2, 128, 768), BF),
    "r1F": ((4, 2, 64, 2304), BF),
    "r1D": ((18, 32, 1024), BF),
    "sD": ((4, 2, 2, 32, 1024), BF),
    "sX": ((2, 32, 1024), BF),
    "ax": ((3, 4, 32, 1152), BF),
    "at": ((4, 32, 1152), BF),
    "ay": ((3, 32, 1152), BF),
    "by": ((3, 2, 64, 1152), BF),
    "bt": ((2, 64, 1152), BF),
    "bx": ((3, 32, 1152), BF),
    "adx": ((3, 4, 2, 16, 512), BF),
    "adt": ((4, 2, 16, 512), BF),
    "ady": ((3, 2, 16, 512), BF),
    "bdy": ((3, 2, 2, 32, 512), BF),
    "bdt": ((2, 2, 32, 512), BF),
    "bdx": ((3, 2, 16, 512), BF),
    "xx": ((3, 16, 1024), BF),
    "xt": ((16, 1024), BF),
    "xy": ((3, 16, 1024), BF),
    "qax": ((3, 4, 32, 384), BF),
    "qat": ((4, 32, 384), BF),
    "qay": ((3, 32, 384), BF),
    "qby": ((3, 2, 64, 384), BF),
    "qbt": ((2, 64, 384), BF),
    "qbx": ((3, 32, 384), BF),
    "r1A": ((4, 2, 64, 768), BF),
    "oF": ((32, 2304), BF),
    "oD": ((3, 16, 1024), BF),
    "oA": ((32, 768), BF),
    "gsm": ((8, 8, 128), F32),
    "gs1": ((8, 8, 128), F32),
    "gs1s": ((8, 128), F32),
    "gs2": ((16, 8, 128), F32),
}
NSEM = 112


class Refs:
    pass


class Comm:
    def __init__(self, place, ssem, rsem):
        self.p, self.ssem, self.rsem = place, ssem, rsem
        self.n = 0
        self.sent = []

    def take(self, count=1):
        base = self.n
        self.n += count
        return base

    def copy(self, src, dst, i, dev):
        return pltpu.make_async_remote_copy(
            src_ref=src, dst_ref=dst, send_sem=self.ssem.at[i], recv_sem=self.rsem.at[i],
            device_id=dev, device_id_type=MESH,
        )

    def send(self, src, dst, i, dev):
        self.copy(src, dst, i, dev).start()
        self.sent.append((src, i))

    def part(self, src, dst, i, dev):
        self.copy(src, dst, i, dev).start()

    def whole(self, ref, i):
        self.sent.append((ref, i))

    def local(self, src, dst, i):
        return pltpu.make_async_copy(src, dst, self.rsem.at[i])

    def got(self, dst, i):
        self.copy(dst, dst, i, self.p.sib()).wait_recv()

    def flush(self, i):
        for src, j in self.sent:
            if j == i:
                self.copy(src, src, i, self.p.sib()).wait_send()
        self.sent = [e for e in self.sent if e[1] != i]

    def finish(self):
        for src, i in self.sent:
            self.copy(src, src, i, self.p.sib()).wait_send()
        self.sent = []


def kernel(*refs):
    r = Refs()
    names = INPUTS + list(OUTPUTS) + list(SCRATCH)
    for name, ref in zip(names, refs):
        setattr(r, name, ref)
    ssem, rsem = refs[len(names):]
    p = Place()
    m = Comm(p, ssem, rsem)

    def z_of(dz):
        return rem(p.z - dz + 4, 4)

    half = pl.ds(pl.multiple_of(p.c * 64, 64), 64)
    other = pl.ds(pl.multiple_of(64 - p.c * 64, 64), 64)
    zq = pl.ds(pl.multiple_of(p.z * 256, 256), 256)
    zk = pl.ds(pl.multiple_of(p.z * 128, 128), 128)
    dps = [rem(p.dp + 8 - k, 8) for k in range(8)]

    i_loc = m.take(4)
    parts = ((r.wq, zq, 0, 256), (r.wk, zk, 256, 128), (r.wv, zk, 384, 128))
    for w, cols, at, wid in parts:
        m.local(w.at[half, cols], r.wqkv.at[p.dp, half, pl.ds(at, wid)], i_loc).start()
    m.local(r.wo.at[half], r.wo_v.at[p.dp, half], i_loc + 1).start()

    def down_pieces(d):
        out = []
        for n in range(2):
            u = rem(2 * p.z + n - d + 8, 8)
            big = 9 * d + u
            out.append((u, 2 * lax.div(big, 8) + rem(big, 2)))
        big = 9 * d + 8
        return out + [(8, 2 * lax.div(big, 8) + rem(big, 2))], lax.div(d, 2) == p.z

    c32 = p.c * 32
    h32 = pl.ds(pl.multiple_of(c32, 32), 32)
    o32 = pl.ds(pl.multiple_of(32 - c32, 32), 32)
    i_ld = m.take(3)
    pieces, has_extra = down_pieces(p.dp)

    def down_local(n):
        u, hidx = pieces[n]
        src = r.wd.at[pl.ds(pl.multiple_of(u * 64 + c32, 32), 32)]
        return pltpu.make_async_copy(src, r.wd_v.at[hidx, h32], rsem.at[i_ld + n])

    for n in range(2):
        down_local(n).start()

    @pl.when(has_extra)
    def _():
        down_local(2).start()

    for src, dst, i in ((r.wg, r.wg_v, i_loc + 2), (r.wu, r.wu_v, i_loc + 3)):
        for t in range(9):
            cols = pl.ds(pl.multiple_of(t * 512 + p.z * 128, 128), 128)
            m.local(src.at[half, cols], dst.at[p.dp, half, pl.ds(t * 128, 128)], i).start()

    r.meta[0:1, :] = r.ga[...].astype(F32)
    r.meta[1:2, :] = r.gf[...].astype(F32)
    r.meta[2:3, :] = r.seg[...].astype(F32)
    r.meta[3:8, :] = jnp.zeros((5, 128), F32)

    bar = pltpu.get_barrier_semaphore()
    for k in range(1, 16):
        pl.semaphore_signal(bar, inc=1, device_id=p.speer(k), device_id_type=MESH)
    for k in range(1, 8):
        pl.semaphore_signal(bar, inc=1, device_id=p.dpeer(k), device_id_type=MESH)
    pl.semaphore_signal(bar, inc=1, device_id=p.xring(2), device_id_type=MESH)
    pl.semaphore_wait(bar, 23)

    class Shards:
        def __init__(self, buf, i_share):
            self.buf, self.share = buf, i_share
            self.iy, self.ix = m.take(3) - 1, m.take(1)

        def row(self, k, xl):
            return rem(p.y - k + 4, 4) * 2 + xl

        def quarter(self, t):
            return pl.ds(pl.multiple_of(p.c * 64 + (t - 1) * 32, 32), 32)

        def along_y(self):
            s = self.buf.at[p.dp, half]
            for k in (2, 1, 3):
                m.send(s, s, self.iy + k, p.ypeer(k))

        def along_x(self, k):
            d = self.row(k, p.xl)
            if k:
                m.got(self.buf.at[d, half], self.iy + k)
            for t in (1, 2):
                s = self.buf.at[d, self.quarter(t)]
                m.part(s, s, self.ix, p.xring(t))

        def to_core(self):
            m.whole(self.buf.at[0:4, half], self.ix)
            m.got(self.buf.at[0:4, half], self.ix)
            s = self.buf.at[:, half]
            m.send(s, s, self.share, p.sib())

        def done(self):
            m.got(self.buf.at[:, other], self.share)

    class Down:
        def __init__(self, i_share):
            self.share = i_share
            self.iy, self.ix = m.take(3) - 1, m.take(1)

        def start(self, d, t, i, dev):
            where, more = down_pieces(d)
            for n in range(3):
                rows = h32 if t == 0 else pl.ds(pl.multiple_of(c32 + (t - 1) * 16, 16), 16)
                s = r.wd_v.at[where[n][1], rows]
                if n < 2:
                    m.part(s, s, i, dev)
                else:

                    @pl.when(more)
                    def _():
                        m.part(s, s, i, dev)

        def wait(self, d, act):
            _, more = down_pieces(d)

            @pl.when(more)
            def _():
                act(r.wd_v.at[0:3, h32])

            @pl.when(jnp.logical_not(more))
            def _():
                act(r.wd_v.at[0:2, h32])

        def along_y(self):
            for k in (2, 1, 3):
                self.start(p.dp, 0, self.iy + k, p.ypeer(k))

        def along_x(self, k):
            d = rem(p.y - k + 4, 4) * 2 + p.xl
            if k:
                self.wait(d, lambda ref: m.got(ref, self.iy + k))
            for t in (1, 2):
                self.start(d, t, self.ix, p.xring(t))

        def to_core(self):
            m.whole(r.wd_v.at[0:9, h32], self.ix)
            m.got(r.wd_v.at[0:9, h32], self.ix)
            m.send(r.wd_v.at[:, h32], r.wd_v.at[:, h32], self.share, p.sib())

        def done(self):
            m.got(r.wd_v.at[:, o32], self.share)

        def finish(self):
            for k in (1, 2, 3):
                self.wait(p.dp, lambda ref: m.copy(ref, ref, self.iy + k, p.sib()).wait_send())

    i_share = m.take(5)
    w_qkv = Shards(r.wqkv, i_share)
    w_o = Shards(r.wo_v, i_share + 1)
    w_d = Down(i_share + 2)
    w_g = Shards(r.wg_v, i_share + 3)
    w_u = Shards(r.wu_v, i_share + 4)
    i_tok = m.take(3) - 1
    for dz in (2, 1, 3):
        m.send(r.tok, r.tok_all.at[dz], i_tok + dz, p.zpeer(dz))
    m.local(r.wqkv.at[0, half], r.wqkv.at[0, half], i_loc).wait()
    w_qkv.along_y()
    w_qkv.along_x(0)
    i_mseq = m.take()
    for k in range(1, 16):
        m.part(r.meta, r.mseq.at[p.sq], i_mseq, p.speer(k))
    m.whole(r.mseq.at[0:15], i_mseq)
    i_mdp = m.take()
    for k in range(1, 8):
        m.part(r.meta, r.mdp.at[p.dp], i_mdp, p.dpeer(k))
    m.whole(r.mdp.at[0:7], i_mdp)
    r.mseq[p.sq] = r.meta[...]
    r.mdp[p.dp] = r.meta[...]
    for k in (1, 3, 2):
        w_qkv.along_x(k)
    m.local(r.wo_v.at[0, half], r.wo_v.at[0, half], i_loc + 1).wait()
    w_o.along_y()
    for n in range(2):
        down_local(n).wait()

    @pl.when(has_extra)
    def _():
        down_local(2).wait()

    w_d.along_y()

    m.got(r.mseq.at[0:15], i_mseq)
    r.st[...] = seg_rows(r.mseq[:, 2, :])
    m.got(r.mdp.at[0:7], i_mdp)
    gain1 = jnp.concatenate([r.mdp[j, 0:1, :] for j in range(8)], axis=1)
    gain2 = jnp.concatenate([r.mdp[j, 1:2, :] for j in range(8)], axis=1)
    w_qkv.to_core()
    m.local(r.wg_v.at[0, half], r.wg_v.at[0, half], i_loc + 2).wait()
    w_g.along_y()
    m.local(r.wu_v.at[0, half], r.wu_v.at[0, half], i_loc + 3).wait()
    w_u.along_y()

    lanesign = jnp.where(lane_half(), -1.0, 1.0)
    freq = r.freq[...]
    for dz in range(4):
        i = 4 * z_of(dz) + p.g
        row = r.st[pl.ds(i, 1), :]
        pos = (lax.broadcasted_iota(jnp.int32, (1, 128), 1) + i * 128).astype(F32) - row
        ang = jnp.transpose(jnp.broadcast_to(pos, (128, 128))) * freq
        r.cosr[dz] = jnp.cos(ang)
        r.sinr[dz] = jnp.sin(ang) * lanesign
    w_qkv.done()

    wfull = r.wqkv[...].reshape(1024, 512)
    qg = jnp.concatenate([r.gq[...].astype(F32)] * 2, axis=1)
    kg = jnp.concatenate([r.gk[...].astype(F32)] * 2, axis=1)
    i_kv = m.take()
    i_kvx = m.take(4)
    i_kvf = m.take()

    def project(dz, x):
        x = x.astype(F32)
        r1 = lax.rsqrt(jnp.mean(x * x, axis=1, keepdims=True) + EPS)
        h = (x * r1 * gain1).astype(BF)
        r.tok_all[dz] = h
        o = dot(h, wfull)
        cs, sn = r.cosr[dz], r.sinr[dz]
        r.qk_raw[dz] = o[:, 0:384]
        rot = []
        for b, gn in ((0, qg), (1, qg), (2, kg)):
            v = o[:, b * 128:(b + 1) * 128]
            v = v * lax.rsqrt(head_mean(v * v) + EPS) * gn
            rot.append(v * cs + swap_halves(v) * sn)
        for hd, v in enumerate(spread_heads(rot[0], rot[1])):
            r.qz[dz, pl.ds(hd * 128, 128), :] = v.astype(BF)
        i = 4 * z_of(dz) + p.g
        r.kv[i, :, 0:128] = rot[2].astype(BF)
        r.kv[i, :, 128:256] = o[:, 384:512].astype(BF)
        m.send(r.kv.at[i], r.kv.at[i], i_kvx + dz, p.xpeer())
        m.part(r.kv.at[i], r.kv.at[i], i_kv, p.sib())

    project(0, r.tok[...])
    for k in (0, 1, 3, 2):
        w_o.along_x(k)
    for dz in (1, 3, 2):
        m.got(r.tok_all.at[dz], i_tok + dz)
        project(dz, r.tok_all[dz])
    i_cot = m.take()
    for dz in (1, 3, 2):
        m.part(r.cot, r.cot_all.at[dz], i_cot, p.zpeer(dz))
    m.whole(r.cot_all.at[1:4], i_cot)
    r.cot_all[0] = r.cot[...]
    for k in (0, 1, 3, 2):
        w_d.along_x(k)
    gs = p.g + 1 - 2 * p.c
    gx = (1 - p.xh) * 2 + p.c
    gxs = (1 - p.xh) * 2 + 1 - p.c
    for dz in (0, 1, 3, 2):
        zz = 4 * z_of(dz)
        m.got(r.kv.at[zz + gx], i_kvx + dz)
        m.part(r.kv.at[zz + gx], r.kv.at[zz + gx], i_kvf, p.sib())
    for k in (0, 1, 3, 2):
        w_g.along_x(k)
    four = r.kv.at[0:4]
    for i in (i_kv, i_kvf):
        m.whole(four, i)
        m.got(four, i)

    def turn(first):
        def one(j, carry):
            t = jnp.transpose(r.kv[j, :, first:first + 128].astype(F32))
            r.kvt[:, pl.ds(pl.multiple_of(j * 128, 128), 128)] = t.astype(BF)
            return carry

        lax.fori_loop(0, 16, one, 0)

    turn(128)
    w_o.to_core()
    for k in (0, 1, 3, 2):
        w_u.along_x(k)

    def allowed_rows(i):
        row = r.st[pl.ds(i, 1), :].astype(jnp.int32)
        qi = lax.broadcasted_iota(jnp.int32, (1, 128), 1) + i * 128
        return jnp.concatenate([row] * 4, axis=1), jnp.concatenate([qi] * 4, axis=1)

    def window(i):
        return jnp.minimum(jnp.maximum(i - 8, 0), 7)

    def weights_of(kb, qv, row4, qi4):
        s = dot(r.kv[pl.ds(kb, 3), :, 0:128].reshape(384, 128), qv, NT)
        ki = lax.broadcasted_iota(jnp.int32, (384, 512), 0) + kb * 128
        return jnp.where((ki >= row4) & (ki <= qi4), jnp.exp2(s * (SCALE * LOG2E)), 0.0)

    def keys_turned(k0):
        return r.kvt[:, pl.ds(pl.multiple_of(k0 * 128, 128), 1152)]

    def heads_down(o):
        return jnp.concatenate(
            [o[(h // 2) * 64:(h // 2) * 64 + 64, h * 128:(h + 1) * 128] for h in range(4)], axis=0
        )

    def forward_chunk(dz):
        i = 4 * z_of(dz) + p.g
        k0 = window(i)
        row4, qi4 = allowed_rows(i)
        qv = r.qz[dz]
        total = jnp.zeros((8, 512), F32)
        for t in range(3):
            w = weights_of(k0 + 3 * t, qv, row4, qi4)
            total = total + jnp.sum(w.reshape(48, 8, 512), axis=0)
            r.pT[t * 384:(t + 1) * 384] = w.astype(BF)
        il = 1.0 / jnp.sum(total, axis=0, keepdims=True)
        r.invl[dz] = jnp.broadcast_to(il, (8, 512))
        full = heads_down(dot(keys_turned(k0), r.pT[...]) * il)
        r.oT[dz] = full
        r.o_s[dz] = jnp.transpose(full).astype(BF)

    i_o = m.take()
    for j in range(4):
        dz = (j + 1) % 4
        forward_chunk(dz)
        if dz:
            m.part(r.o_s.at[dz], r.o_in.at[p.z], i_o, p.zpeer(-dz))
        else:
            r.o_in[p.z] = r.o_s[0]
        if j == 1:
            w_d.to_core()
    m.whole(r.o_in.at[0:3], i_o)

    w_g.to_core()
    m.got(r.o_in.at[0:3], i_o)
    for j in range(4):
        r.o_own[:, j * 256:(j + 1) * 256] = r.o_in[j]
    w_o.done()
    x0 = r.tok[...].astype(F32)
    middle = x0 + dot(r.o_own[...], r.wo_v[...].reshape(1024, 1024))
    r.mid[...] = middle
    r2 = lax.rsqrt(jnp.mean(middle * middle, axis=1, keepdims=True) + EPS)
    r.h2[0] = (middle * r2 * gain2).astype(BF)
    i_h2 = m.take(3) - 1
    for dz in (2, 1, 3):
        m.send(r.h2.at[0], r.h2.at[dz], i_h2 + dz, p.zpeer(dz))
    i_of = m.take()
    for dz in (2, 1, 3):
        m.part(r.o_own, r.o_full.at[dz], i_of, p.zpeer(dz))
    m.whole(r.o_full.at[1:4], i_of)
    r.o_full[0] = r.o_own[...]

    turn(0)
    w_u.to_core()
    m.got(r.cot_all.at[1:4], i_cot)
    w_d.done()
    wd = r.wd_v[...].reshape(1152, 1024)
    cots = r.cot_all[...].reshape(512, 1024)

    def cols384(t):
        return pl.ds(pl.multiple_of(t * 384, 128), 384)

    def dm_tile(t, carry):
        w = r.wd_v[pl.ds(t * 6, 6)].reshape(384, 1024)
        r.dm[:, :, cols384(t)] = dot(cots, w, NT).astype(BF).reshape(4, 128, 384)
        return carry

    lax.fori_loop(0, 3, dm_tile, 0)
    w_g.done()
    w_u.done()

    i_p2 = m.take()
    for pair in range(2):
        two = slice(2 * pair, 2 * pair + 2)
        for dz in ((1,), (2, 3))[pair]:
            m.got(r.h2.at[dz], i_h2 + dz)
        hh = r.h2[two].reshape(256, 1024)

        def ffn_tile(t, carry):
            cols = cols384(t)
            gate = dot(hh, r.wg_v[:, :, cols].reshape(1024, 384))
            up = dot(hh, r.wu_v[:, :, cols].reshape(1024, 384))
            sig = 1.0 / (1.0 + jnp.exp(-gate))
            act = gate * sig
            dmt = r.dm[two, :, cols].astype(F32).reshape(256, 384)
            r.mixed[two, :, cols] = (act * up).astype(BF).reshape(2, 128, 384)
            r.dg[two, :, cols] = (dmt * up * sig * (1.0 + gate * (1.0 - sig))).astype(BF).reshape(2, 128, 384)
            r.du[two, :, cols] = (dmt * act).astype(BF).reshape(2, 128, 384)
            return carry

        lax.fori_loop(0, 3, ffn_tile, 0)

    i_r1 = m.take(4)
    h2t = r.h2[...].reshape(512, 1024)

    def gate_tile(t, carry):
        w = r.dg[:, :, cols384(t)].reshape(512, 384)
        r.gF[:, :, :, cols384(t)] = dot(h2t, w, TN).astype(BF).reshape(4, 2, 128, 384)
        return carry

    def up_tile(t, carry):
        w = r.du[:, :, cols384(t)].reshape(512, 384)
        r.gF[:, :, :, cols384(t + 3)] = dot(h2t, w, TN).astype(BF).reshape(4, 2, 128, 384)
        return carry

    lax.fori_loop(0, 3, gate_tile, 0)
    m.send(r.gF.at[:, :, other, 0:1152], r.r1F.at[:, :, :, 0:1152], i_r1, p.sib())
    lax.fori_loop(0, 3, up_tile, 0)
    m.send(r.gF.at[:, :, other, 1152:2304], r.r1F.at[:, :, :, 1152:2304], i_r1 + 3, p.sib())
    for pair in (1, 0):
        two = slice(2 * pair, 2 * pair + 2)
        part = dot(r.dg[two].reshape(256, 1152), r.wg_v[...].reshape(1024, 1152), NT)
        part += dot(r.du[two].reshape(256, 1152), r.wu_v[...].reshape(1024, 1152), NT)
        if pair:
            r.p2s[1] = part[0:128].astype(BF)
            m.part(r.p2s.at[1], r.p2r.at[1], i_p2, p.zpeer(-2))
            r.p2s[2] = part[128:256].astype(BF)
            m.part(r.p2s.at[2], r.p2r.at[2], i_p2, p.zpeer(-3))
        else:
            r.p2s[0] = part[128:256].astype(BF)
            m.part(r.p2s.at[0], r.p2r.at[0], i_p2, p.zpeer(-1))
            r.own[...] = part[0:128]

    def down_tile(t, carry):
        w = r.mixed[:, :, cols384(t)].reshape(512, 384)
        r.gD[pl.ds(t * 6, 6)] = dot(w, cots, TN).astype(BF).reshape(6, 64, 1024)
        return carry

    lax.fori_loop(0, 3, down_tile, 0)
    m.send(r.gD.at[:, o32], r.r1D, i_r1 + 1, p.sib())

    m.got(r.r1F.at[:, :, :, 0:1152], i_r1)
    m.got(r.r1F.at[:, :, :, 1152:2304], i_r1 + 3)

    def add_core(d, carry):
        a, b = lax.div(d, 2), rem(d, 2)
        r.r1F[a, b] = (r.r1F[a, b].astype(F32) + r.gF[a, b, half].astype(F32)).astype(BF)
        return carry

    lax.fori_loop(0, 8, add_core, 0)

    def rows_of(x, n):
        return pl.ds(pl.multiple_of(x * n, n), n)

    class XFirst:
        def __init__(self, src, mid1, tot, mid2):
            self.src, self.mid1, self.tot, self.mid2 = src, mid1, tot, mid2
            self.i1, self.i2 = m.take(), m.take()

        def one(self):
            for t in (3, 1, 2):
                m.part(self.src(t), self.mid1.at[t - 1], self.i1, p.xring(t))
            m.whole(self.mid1, self.i1)

        def two(self):
            m.got(self.mid1, self.i1)

            def add(n, carry):
                v = self.src(0).at[n][...].astype(F32)
                for t in range(3):
                    v = v + self.mid1[t, n].astype(F32)
                self.tot[n] = v.astype(BF)
                return carry

            lax.fori_loop(0, 4, add, 0)
            for k in (2, 1, 3):
                m.part(self.tot.at[rem(p.y + k, 4)], self.mid2.at[k - 1], self.i2, p.ypeer(k))
            m.whole(self.mid2, self.i2)

        def sum(self):
            m.got(self.mid2, self.i2)
            v = self.tot[p.y].astype(F32)
            for k in range(3):
                v = v + self.mid2[k].astype(F32)
            return v.astype(BF)

    class YFirst:
        def __init__(self, src, part, mid1, tot, mid2):
            self.src, self.part, self.mid1, self.tot, self.mid2 = src, part, mid1, tot, mid2
            self.i1, self.i2 = m.take(), m.take()

        def one(self):
            for k in (2, 1, 3):
                m.part(self.src(rem(p.y + k, 4)), self.mid1.at[k - 1], self.i1, p.ypeer(k))
            m.whole(self.mid1, self.i1)

        def two(self):
            m.got(self.mid1, self.i1)

            def add(n, carry):
                v = self.src(p.y).at[n][...].astype(F32)
                for k in range(3):
                    v = v + self.mid1[k, n].astype(F32)
                self.tot[n] = v.astype(BF)
                return carry

            lax.fori_loop(0, 2, add, 0)
            for t in (3, 1, 2):
                m.part(self.part(self.tot, t), self.mid2.at[t - 1], self.i2, p.xring(t))
            m.whole(self.mid2, self.i2)

        def sum(self):
            m.got(self.mid2, self.i2)
            v = self.part(self.tot, 0)[...].astype(F32)
            for t in range(3):
                v = v + self.mid2[t].astype(F32)
            return v.astype(BF)

    def rows_x(buf, c0, c1):
        return lambda t: buf.at[:, p.xplace(t)[0], rows_of(p.xplace(t)[1], 32), c0:c1]

    def rows_y(buf, c0, c1):
        return lambda y: buf.at[y, :, :, c0:c1]

    def part_y(tot, t):
        xl, xh = p.xplace(t)
        return tot.at[xl, rows_of(xh, 32)]

    def part_d(tot, t):
        xl, xh = p.xplace(t)
        return tot.at[xl, :, rows_of(xh, 16)]

    sums = [
        XFirst(rows_x(r.r1F, 0, 1152), r.ax, r.at, r.ay),
        YFirst(rows_y(r.r1F, 1152, 2304), part_y, r.by, r.bt, r.bx),
        XFirst(
            lambda t: r.sD.at[:, p.xplace(t)[0], :, rows_of(p.xplace(t)[1], 16), 0:512], r.adx, r.adt, r.ady
        ),
        YFirst(lambda y: r.sD.at[y, :, :, :, 512:1024], part_d, r.bdy, r.bdt, r.bdx),
    ]
    for e in sums[0:2]:
        e.one()
    r.own3[...] = dot(r.mixed[0], wd)

    def out_chunk(dz, carry):
        r.p3s[dz - 1] = dot(r.mixed[dz], wd).astype(BF)
        return carry

    lax.fori_loop(1, 4, out_chunk, 0)
    m.got(r.r1D, i_r1 + 1)

    def add_core_down(d, carry):
        a, b = lax.div(d, 2), rem(d, 2)
        where, more = down_pieces(d)
        for n in range(2):
            t = where[n][1]
            r.sD[a, b, n] = (r.r1D[t].astype(F32) + r.gD[t, h32].astype(F32)).astype(BF)

        @pl.when(more)
        def _():
            t = where[2][1]
            r.sX[b] = (r.r1D[t].astype(F32) + r.gD[t, h32].astype(F32)).astype(BF)

        return carry

    lax.fori_loop(0, 8, add_core_down, 0)
    for e in sums[2:4]:
        e.one()
    i_x1 = m.take()
    i_x2 = m.take()
    for t in (3, 1, 2):
        xl, xh = p.xplace(t)
        m.part(r.sX.at[xl, rows_of(xh, 16)], r.xx.at[t - 1], i_x1, p.xring(t))
    m.whole(r.xx, i_x1)

    m.whole(r.p2s, i_p2)
    m.got(r.p2r, i_p2)
    dh2 = r.own[...] + r.p2r[0].astype(F32) + r.p2r[1].astype(F32) + r.p2r[2].astype(F32)
    middle = r.mid[...]
    r2 = lax.rsqrt(jnp.mean(middle * middle, axis=1, keepdims=True) + EPS)
    small2 = jnp.sum(dh2 * middle * r2, axis=0, keepdims=True)
    wdh = dh2 * gain2
    dmid = r.cot[...].astype(F32) + r2 * wdh - middle * (r2 * r2 * r2) * jnp.mean(wdh * middle, axis=1, keepdims=True)
    r.dmid[...] = dmid
    r.da[...] = dmid.astype(BF)
    i_do = m.take()

    def zcols(z):
        return pl.ds(pl.multiple_of(z * 256, 256), 256)

    for dz in (2, 1, 3, 0):
        zz = rem(p.z + dz, 4)
        w = r.wo_v[pl.ds(2 * zz, 2)].reshape(256, 1024)
        r.dob[:, zcols(zz)] = dot(r.da[...], w, NT).astype(BF)
        if dz:
            m.part(r.dob.at[:, zcols(zz)], r.do_all.at[dz], i_do, p.zpeer(dz))
    m.whole(r.do_all.at[1:4], i_do)
    r.do_all[0] = r.dob[:, zq]
    i_p3 = m.take()
    i_dc = m.take()
    for dz in (2, 1, 3):
        m.part(r.da.at[:, zcols(rem(p.z + dz, 4))], r.da_c.at[dz], i_dc, p.zpeer(dz))
    m.whole(r.da_c.at[1:4], i_dc)
    for dz in (2, 1, 3):
        m.part(r.p3s.at[dz - 1], r.p3r.at[dz - 1], i_p3, p.zpeer(-dz))
    m.whole(r.p3s, i_p3)
    r.da_c[0] = r.da[:, zq]

    r.dkv[...] = jnp.zeros_like(r.dkv)
    m.got(r.do_all.at[1:4], i_do)
    for e in sums[0:2]:
        e.two()

    lane = lax.broadcasted_iota(jnp.int32, (1, 256), 1)
    kscale = jnp.where(lane < 128, SCALE, 1.0)
    i_dkv = m.take()
    xs = (p.dp, p.z * 4 + gxs)

    def backward_chunk(j, carry):
        zz = 3 - j
        dz = rem(p.z - zz + 4, 4)
        i = 4 * zz + p.g
        row4, qi4 = allowed_rows(i)
        do = r.do_all[dz].astype(F32)
        for hd, v in enumerate(spread_heads(do[:, 0:128], do[:, 128:256])):
            r.doz[pl.ds(hd * 128, 128), :] = v.astype(BF)
        prod = jnp.transpose(do) * r.oT[dz]
        drow = jnp.concatenate(
            [jnp.sum(prod[h * 64:(h + 1) * 64], axis=0, keepdims=True) for h in range(4)], axis=1
        )
        il = r.invl[dz, 0:1, :]
        qv = r.qz[dz]
        dov = r.doz[...]
        k0 = window(i)
        for t in range(3):
            rows = slice(t * 384, (t + 1) * 384)
            w = weights_of(k0 + 3 * t, qv, row4, qi4) * il
            r.pT[rows] = w.astype(BF)
            dp = dot(r.kv[pl.ds(k0 + 3 * t, 3), :, 128:256].reshape(384, 128), dov, NT)
            r.dsT[rows] = (w * (dp - drow)).astype(BF)
        nine = pl.ds(k0, 9)
        r.dkv[nine, :, 0:128] += dot(r.dsT[...], qv).reshape(9, 128, 128)
        r.dkv[nine, :, 128:256] += dot(r.pT[...], dov).reshape(9, 128, 128)
        r.dkvb[zz] = (r.dkv[pl.ds(4 * zz, 4)] * kscale.reshape(1, 1, 256)).astype(BF)
        m.part(r.dkvb.at[zz, gx], r.dkvr.at[1, zz], i_dkv, p.xpeer())
        m.part(r.dkvb.at[zz, gxs], r.dkvr.at[2, zz], i_dkv, xs)
        m.part(r.dkvb.at[zz, gs], r.dkvr.at[0, zz], i_dkv, p.sib())
        r.dqr[dz] = jnp.transpose(heads_down(dot(keys_turned(k0), r.dsT[...]) * SCALE))
        return carry

    lax.fori_loop(0, 4, backward_chunk, 0)

    m.whole(r.dkvr, i_dkv)

    for e in sums[2:4]:
        e.two()
    m.got(r.xx, i_x1)
    v = r.sX[p.xl, rows_of(p.xh, 16)].astype(F32)
    for t in range(3):
        v = v + r.xx[t].astype(F32)
    r.xt[...] = v.astype(BF)
    kz = rem(p.z - p.y + 4, 4)

    @pl.when(kz != 0)
    def _():
        m.part(r.xt, r.xy.at[kz - 1], i_x2, (p.z * 2 + p.xl, p.sq))

    r.oF[:, 0:1152] = sums[0].sum()
    r.oF[:, 1152:2304] = sums[1].sum()

    def seq_at(z, g):
        return rem(z + 8, 4) * 4 + g

    class Gather:
        def __init__(self, own, buf, order):
            self.own, self.buf, self.order = own, buf, order
            self.il, self.ix, self.iz, self.ic = m.take(), m.take(), m.take(), m.take()

        def on(self, src, s, where):
            if "x" in where:
                m.part(src, s, self.ix, p.xpeer())
            if "z" in where:
                for dz in (2, 1, 3):
                    m.part(src, s, self.iz, p.zpeer(dz))
            if "b" in where:
                for dz in (2, 1, 3):
                    m.part(src, s, self.iz, (p.dp, seq_at(p.z + dz, gx)))
            if "c" in where:
                m.part(src, s, self.ic, p.sib())

        def got(self, n, i):
            m.got(self.buf.at[0:n], i)

        def slot(self, dz, g):
            return self.buf.at[seq_at(p.z - dz, g)]

        def first(self):
            m.local(self.own, self.slot(0, p.g), self.il).start()
            self.on(self.own, self.slot(0, p.g), "zxcb" if self.order == "zx" else "zxc")

        def second(self):
            if self.order == "x":
                self.got(1, self.ix)
                s = self.slot(0, gx)
                self.on(s, s, "zc")
            elif self.order == "z":
                self.got(3, self.iz)
                for dz in (1, 2, 3):
                    s = self.slot(dz, p.g)
                    self.on(s, s, "xc")
            else:
                self.got(1, self.ix)
                self.got(6, self.iz)
                for dz in range(4):
                    for g in (p.g, gx)[dz == 0:]:
                        s = self.slot(dz, g)
                        self.on(s, s, "c")

        def third(self):
            if self.order == "x":
                self.got(6, self.iz)
                for dz in (1, 2, 3):
                    for g in (p.g, gx):
                        s = self.slot(dz, g)
                        self.on(s, s, "c")
            elif self.order == "z":
                self.got(4, self.ix)
                for dz in range(4):
                    s = self.slot(dz, gx)
                    self.on(s, s, "c")

        def last(self):
            n = {"x": (1, 6), "z": (4, 3), "zx": (1, 6)}[self.order]
            m.whole(self.buf.at[0:n[0]], self.ix)
            m.whole(self.buf.at[0:n[1]], self.iz)
            m.whole(self.buf.at[0:8], self.ic)
            self.got(8, self.ic)
            m.local(self.own, self.slot(0, p.g), self.il).wait()

    ag_f = Gather(r.oF, r.fF, "z")
    ag_d = Gather(r.oD, r.fD, "x")
    ag_a = Gather(r.oA, r.fA, "zx")
    ag_f.first()

    m.got(r.o_full.at[1:4], i_of)
    m.got(r.da_c.at[1:4], i_dc)
    m.got(r.p3r, i_p3)
    r.gA[:, :, :, 512:768] = dot(
        r.o_full[...].reshape(512, 1024), r.da_c[...].reshape(512, 256), TN
    ).astype(BF).reshape(4, 2, 128, 256)
    r.block_out[...] = (
        r.mid[...] + r.own3[...] + r.p3r[0].astype(F32) + r.p3r[1].astype(F32) + r.p3r[2].astype(F32)
    ).astype(BF)

    m.got(r.dkvr, i_dkv)
    sq_acc = jnp.zeros((1, 128), F32)
    sk_acc = jnp.zeros((1, 128), F32)
    for dz in range(4):
        zz = z_of(dz)
        i = 4 * zz + p.g
        dkv = r.dkv[i] * kscale
        for n in range(3):
            dkv = dkv + r.dkvr[n, zz].astype(F32)
        cs, sn = r.cosr[dz], r.sinr[dz]
        grads = (r.dqr[dz, :, 0:128], r.dqr[dz, :, 128:256], dkv[:, 0:128])
        for b, gr in enumerate(grads):
            gn = qg if b < 2 else kg
            v = r.qk_raw[dz, :, b * 128:(b + 1) * 128]
            f = lax.rsqrt(head_mean(v * v) + EPS)
            dn = gr * cs - swap_halves(gr) * sn
            add = jnp.sum(dn * v * f, axis=0, keepdims=True)
            if b < 2:
                sq_acc = sq_acc + add
            else:
                sk_acc = sk_acc + add
            wn = dn * gn
            r.dqkv[dz, :, b * 128:(b + 1) * 128] = (f * wn - v * (f * f * f) * head_mean(wn * v)).astype(BF)
        r.dqkv[dz, :, 384:512] = dkv[:, 128:256].astype(BF)
    r.gA[:, :, :, 0:512] = dot(
        r.tok_all[...].reshape(512, 1024), r.dqkv[...].reshape(512, 512), TN
    ).astype(BF).reshape(4, 2, 128, 512)
    m.send(r.gA.at[:, :, other], r.r1A, i_r1 + 2, p.sib())
    i_p4 = m.take()
    m.flush(i_p2)
    for dz in (2, 1, 3):
        r.p2s[dz - 1] = dot(r.dqkv[dz], r.wqkv[...].reshape(1024, 512), NT).astype(BF)
        m.part(r.p2s.at[dz - 1], r.p4r.at[dz - 1], i_p4, p.zpeer(-dz))
    m.whole(r.p2s, i_p4)
    r.own[...] = dot(r.dqkv[0], r.wqkv[...].reshape(1024, 512), NT)
    r.oD[0:2, :, 0:512] = sums[2].sum()
    r.oD[0:2, :, 512:1024] = sums[3].sum()

    @pl.when(kz == 0)
    def _():
        v = r.xt[...].astype(F32)
        m.got(r.xy, i_x2)
        for k in range(3):
            v = v + r.xy[k].astype(F32)
        r.oD[2] = v.astype(BF)

    @pl.when(kz != 0)
    def _():
        r.oD[2] = jnp.zeros((16, 1024), BF)

    ag_d.first()
    m.got(r.r1A, i_r1 + 2)
    r.r1A[...] = (r.r1A[...].astype(F32) + r.gA[:, :, half].astype(F32)).astype(BF)
    sums_a = [
        XFirst(rows_x(r.r1A, 0, 384), r.qax, r.qat, r.qay),
        YFirst(rows_y(r.r1A, 384, 768), part_y, r.qby, r.qbt, r.qbx),
    ]
    for e in sums_a:
        e.one()
    ag_f.second()
    ag_d.second()

    for e in sums_a:
        e.two()

    m.got(r.p4r, i_p4)
    dh = r.own[...] + r.p4r[0].astype(F32) + r.p4r[1].astype(F32) + r.p4r[2].astype(F32)
    x0 = r.tok[...].astype(F32)
    r1 = lax.rsqrt(jnp.mean(x0 * x0, axis=1, keepdims=True) + EPS)
    small1 = jnp.sum(dh * x0 * r1, axis=0, keepdims=True)
    wdh = dh * gain1
    r.input_grad[...] = (
        r.dmid[...] + r1 * wdh - x0 * (r1 * r1 * r1) * jnp.mean(wdh * x0, axis=1, keepdims=True)
    ).astype(BF)

    both = lambda v: v + pltpu.roll(v, 64, 1)
    for d in range(8):
        cols = slice(d * 128, (d + 1) * 128)
        r.gsm[d] = jnp.concatenate(
            [small1[:, cols], small2[:, cols], both(sq_acc), both(sk_acc), jnp.zeros((4, 128), F32)], axis=0
        )
    i_s1 = m.take()
    i_s2 = m.take()
    for k in range(1, 8):
        m.part(r.gsm.at[rem(p.dp + k, 8)], r.gs1.at[k], i_s1, p.dpeer(k))
    m.whole(r.gs1.at[1:8], i_s1)
    r.gs1[0] = r.gsm[p.dp]
    m.got(r.gs1.at[1:8], i_s1)
    r.gs1s[...] = jnp.sum(r.gs1[...], axis=0)
    for k in range(1, 16):
        m.part(r.gs1s, r.gs2.at[k], i_s2, p.speer(k))
    m.whole(r.gs2.at[1:16], i_s2)
    r.gs2[0] = r.gs1s[...]

    r.oA[:, 0:384] = sums_a[0].sum()
    r.oA[:, 384:768] = sums_a[1].sum()
    ag_a.first()
    ag_f.third()
    ag_d.third()
    ag_a.second()
    m.got(r.gs2.at[1:16], i_s2)
    r.g_small[...] = jnp.sum(r.gs2[...], axis=0)
    ag_f.last()
    ag_d.last()
    ag_a.last()

    m.finish()
    w_d.finish()

    @pl.when(kz != 0)
    def _():
        m.copy(r.xt, r.xt, i_x2, p.sib()).wait_send()

    assert m.n <= NSEM, m.n


def block(args):
    vm = pl.BlockSpec(memory_space=pltpu.VMEM)
    hb = pl.BlockSpec(memory_space=pl.ANY)
    return pl.pallas_call(
        kernel,
        out_shape=tuple(jax.ShapeDtypeStruct(s, d) for s, d in OUTPUTS.values()),
        in_specs=[vm] * 7 + [hb] * 7 + [vm],
        out_specs=tuple(hb if name[0] == "f" else vm for name in OUTPUTS),
        scratch_shapes=[pltpu.VMEM(s, d) for s, d in SCRATCH.values()]
        + [pltpu.SemaphoreType.DMA((NSEM,)), pltpu.SemaphoreType.DMA((NSEM,))],
        compiler_params=pltpu.CompilerParams(
            collective_id=0, has_side_effects=True, vmem_limit_bytes=63 * 2**20
        ),
        name="block",
    )(*args)


PLACED = {
    "g_gate": (128, 4608),
    "g_up": (128, 4608),
    "g_down": (576, 1024),
    "g_q": (128, 1024),
    "g_k": (128, 512),
    "g_v": (128, 512),
    "g_out": (128, 1024),
}

LAID = {
    "block_out": ((128, 1024), BF),
    "input_grad": ((128, 1024), BF),
    "g_attn": ((1, 128), F32),
    "g_ffn": ((1, 128), F32),
    "g_qg": ((1, 64), F32),
    "g_kg": ((1, 64), F32),
    **{name: (shape, F32) for name, shape in PLACED.items()},
}


def lay_kernel(f_f, f_d, f_a, b_o, i_g, sm, *refs):
    outs = dict(zip(LAID, refs[:len(LAID)]))
    v_f, v_d, v_a = refs[len(LAID):len(LAID) + 3]
    stage = dict(zip(PLACED, refs[len(LAID) + 3:len(LAID) + 3 + len(PLACED)]))
    isem, osem = refs[len(LAID) + 3 + len(PLACED):]
    p = Place()
    ins = [
        pltpu.make_async_copy(f_f, v_f, isem.at[0]),
        pltpu.make_async_copy(f_d, v_d, isem.at[1]),
        pltpu.make_async_copy(f_a, v_a, isem.at[2]),
    ]
    for q in ins:
        q.start()
    outs["block_out"][...] = b_o[...]
    outs["input_grad"][...] = i_g[...]
    outs["g_attn"][...] = sm[0:1, :]
    outs["g_ffn"][...] = sm[1:2, :]
    outs["g_qg"][...] = sm[2:3, 0:64]
    outs["g_kg"][...] = sm[3:4, 0:64]

    def place(name):
        n = list(PLACED).index(name)
        return pltpu.make_async_copy(stage[name], outs[name], osem.at[n])

    def row_of(s):
        g = rem(s, 4)
        return pl.ds(pl.multiple_of(rem(g, 2) * 64 + lax.div(g, 2) * 32, 32), 32)

    ins[0].wait()
    for name, base in (("g_gate", 0), ("g_up", 1152)):

        def lay(s, carry):
            z = lax.div(s, 4)
            for t in range(9):
                cols = pl.ds(pl.multiple_of(t * 512 + z * 128, 128), 128)
                stage[name][row_of(s), cols] = v_f[s, :, base + t * 128:base + (t + 1) * 128].astype(F32)
            return carry

        lax.fori_loop(0, 16, lay, 0)
        place(name).start()
    ins[1].wait()

    def lay_down(s, carry):
        z = lax.div(s, 4)
        g = rem(s, 4)
        sub = rem(g, 2) * 32 + lax.div(g, 2) * 16
        for n in range(2):
            u = rem(2 * z + n - p.dp + 8, 8)
            stage["g_down"][pl.ds(pl.multiple_of(u * 64 + sub, 16), 16), :] = v_d[s, n].astype(F32)

        @pl.when(lax.div(p.dp, 2) == z)
        def _():
            stage["g_down"][pl.ds(pl.multiple_of(8 * 64 + sub, 16), 16), :] = v_d[s, 2].astype(F32)

        return carry

    lax.fori_loop(0, 16, lay_down, 0)
    place("g_down").start()
    ins[2].wait()

    def lay_attn(s, carry):
        z = lax.div(s, 4)
        row = row_of(s)
        c256 = pl.ds(pl.multiple_of(z * 256, 256), 256)
        c128 = pl.ds(pl.multiple_of(z * 128, 128), 128)
        stage["g_q"][row, c256] = v_a[s, :, 0:256].astype(F32)
        stage["g_k"][row, c128] = v_a[s, :, 256:384].astype(F32)
        stage["g_v"][row, c128] = v_a[s, :, 384:512].astype(F32)
        stage["g_out"][row, c256] = v_a[s, :, 512:768].astype(F32)
        return carry

    lax.fori_loop(0, 16, lay_attn, 0)
    for name in ("g_q", "g_k", "g_v", "g_out"):
        place(name).start()
    for name in PLACED:
        place(name).wait()


def lay_out(o):
    hb = pl.BlockSpec(memory_space=pl.ANY)
    vm = pl.BlockSpec(memory_space=pltpu.VMEM)
    small = ("block_out", "input_grad", "g_attn", "g_ffn", "g_qg", "g_kg")
    got = pl.pallas_call(
        lay_kernel,
        out_shape=tuple(jax.ShapeDtypeStruct(s, d) for s, d in LAID.values()),
        in_specs=[hb] * 3 + [vm] * 3,
        out_specs=tuple(vm if n in small else hb for n in LAID),
        scratch_shapes=[pltpu.VMEM(*OUTPUTS[n]) for n in ("fF", "fD", "fA")]
        + [pltpu.VMEM(s, F32) for s in PLACED.values()]
        + [pltpu.SemaphoreType.DMA((3,)), pltpu.SemaphoreType.DMA((len(PLACED),))],
        compiler_params=pltpu.CompilerParams(vmem_limit_bytes=62 * 2**20),
        name="lay",
    )(o["fF"], o["fD"], o["fA"], o["block_out"], o["input_grad"], o["g_small"])
    return dict(zip(LAID, got))


def local(
    tokens, segment_ids, attn_gain, w_query, w_key, w_value, w_out, ffn_gain, w_gate, w_up, w_down,
    query_gain, key_gain, cotangent,
):
    inverse = ROPE_BASE ** (-(np.arange(32).astype(np.float32) * np.float32(2.0) / np.float32(64)))
    freq = jnp.asarray(np.tile(inverse.astype(np.float32), 4)[None])
    o = block(
        (
            tokens, segment_ids, attn_gain[None], ffn_gain[None], query_gain[None], key_gain[None], freq, w_query, w_key, w_value,
            w_out, w_gate, w_up, w_down, cotangent,
        )
    )
    o = dict(zip(OUTPUTS, o))
    w = lay_out(o)
    return (
        w["block_out"], w["input_grad"], w["g_attn"].reshape(128), w["g_q"], w["g_k"], w["g_v"], w["g_out"],
        w["g_ffn"].reshape(128), w["g_gate"], w["g_up"], w["g_down"], w["g_qg"].reshape(64),
        w["g_kg"].reshape(64),
    )


def solution(mesh):
    both = ("dp", "seq")
    w = P("dp", None)
    return jax.shard_map(
        local,
        mesh=mesh,
        in_specs=(P(both, None), P("dp", "seq"), P("dp"), w, w, w, w, P("dp"), w, w, w, P(), P(), P(both, None)),
        out_specs=(P(both, None), P(both, None), P("dp"), w, w, w, w, P("dp"), w, w, w, P(), P()),
        check_vma=False,
    )
```

```python
import math

import jax
import jax.numpy as jnp
import numpy as np
from jax import lax
from jax.experimental import pallas as pl
from jax.experimental.pallas import tpu as pltpu
from jax.sharding import PartitionSpec as P

MESH = pl.DeviceIdType.MESH
F32 = jnp.float32
BF = jnp.bfloat16
EPS = 1e-05
ROPE_BASE = 1000000.0
NN = (((1,), (0,)), ((), ()))
NT = (((1,), (1,)), ((), ()))
TN = (((0,), (0,)), ((), ()))
SCALE = 0.125
LOG2E = math.log2(math.e)


def dot(a, b, dims=NN, precision=None):
    return lax.dot_general(a, b, dims, preferred_element_type=F32, precision=precision)


def rem(a, b):
    return lax.rem(a, b)


class Place:
    def __init__(self):
        self.dp = lax.axis_index("dp")
        self.sq = lax.axis_index("seq")
        self.y = lax.div(self.dp, 2)
        self.xl = rem(self.dp, 2)
        self.z = lax.div(self.sq, 4)
        self.g = rem(self.sq, 4)
        self.xh = lax.div(self.g, 2)
        self.c = rem(self.sq, 2)

    def zpeer(self, dz):
        return (self.dp, rem(self.z + dz + 4, 4) * 4 + self.g)

    def sib(self):
        return (self.dp, self.sq + 1 - 2 * self.c)

    def xpeer(self):
        return (self.dp, self.z * 4 + (1 - self.xh) * 2 + self.c)

    def dpeer(self, k):
        return (rem(self.dp + k + 8, 8), self.sq)

    def speer(self, k):
        return (self.dp, rem(self.sq + k + 16, 16))

    def ypeer(self, k):
        return (rem(self.y + k + 4, 4) * 2 + self.xl, self.sq)

    def xring(self, t):
        xl = self.xl if t == 3 else 1 - self.xl
        return (self.y * 2 + xl, self.sq if t == 1 else self.z * 4 + (1 - self.xh) * 2 + self.c)

    def xplace(self, t):
        return (self.xl if t in (0, 3) else 1 - self.xl), (self.xh if t in (0, 1) else 1 - self.xh)


def seg_rows(ids):
    start = jnp.zeros_like(ids)
    for j in range(1, 8):
        below = jnp.sum(jnp.where(ids < j, 1.0, 0.0), keepdims=True)
        start = jnp.where(ids == j, below, start)
    return start


def lane_half():
    return lax.rem(lax.broadcasted_iota(jnp.int32, (1, 128), 1), 64) < 32


def swap_halves(x):
    return jnp.where(lane_half(), pltpu.roll(x, 96, 1), pltpu.roll(x, 32, 1))


def head_mean(x):
    a = lax.div(lax.broadcasted_iota(jnp.int32, (128, 128), 0), 64)
    b = lax.div(lax.broadcasted_iota(jnp.int32, (128, 128), 1), 64)
    block = jnp.where(a == b, 1.0 / 64, 0.0)
    return dot(x, block, NN, lax.Precision.HIGHEST)


def spread_heads(first, second):
    lo = lax.broadcasted_iota(jnp.int32, (1, 128), 1) < 64
    return [
        jnp.where(lo, first, 0.0),
        jnp.where(lo, pltpu.roll(first, 64, 1), 0.0),
        jnp.where(lo, 0.0, pltpu.roll(second, 64, 1)),
        jnp.where(lo, 0.0, second),
    ]


INPUTS = ["tok", "seg", "ga", "gf", "gq", "gk", "freq", "wq", "wk", "wv", "wo", "wg", "wu", "wd", "cot"]
OUTPUTS = {
    "block_out": ((128, 1024), BF),
    "input_grad": ((128, 1024), BF),
    "fF": ((16, 32, 2304), BF),
    "fD": ((16, 3, 16, 1024), BF),
    "fA": ((16, 32, 768), BF),
    "g_small": ((8, 128), F32),
}
SCRATCH = {
    "tok_all": ((4, 128, 1024), BF),
    "cot_all": ((4, 128, 1024), BF),
    "meta": ((8, 128), F32),
    "mseq": ((16, 8, 128), F32),
    "mdp": ((8, 8, 128), F32),
    "wqkv": ((8, 128, 512), BF),
    "wo_v": ((8, 128, 1024), BF),
    "wg_v": ((8, 128, 1152), BF),
    "wu_v": ((8, 128, 1152), BF),
    "wd_v": ((18, 64, 1024), BF),
    "st": ((16, 128), F32),
    "qk_raw": ((4, 128, 384), F32),
    "qz": ((4, 512, 128), BF),
    "kv": ((16, 128, 256), BF),
    "kvt": ((128, 2048), BF),
    "pT": ((1152, 512), BF),
    "dsT": ((1152, 512), BF),
    "cosr": ((4, 128, 128), F32),
    "sinr": ((4, 128, 128), F32),
    "invl": ((4, 8, 512), F32),
    "oT": ((4, 256, 128), F32),
    "o_s": ((4, 128, 256), BF),
    "o_in": ((4, 128, 256), BF),
    "o_own": ((128, 1024), BF),
    "o_full": ((4, 128, 1024), BF),
    "mid": ((128, 1024), F32),
    "h2": ((4, 128, 1024), BF),
    "dm": ((4, 128, 1152), BF),
    "mixed": ((4, 128, 1152), BF),
    "dg": ((4, 128, 1152), BF),
    "du": ((4, 128, 1152), BF),
    "p2s": ((3, 128, 1024), BF),
    "p2r": ((3, 128, 1024), BF),
    "own": ((128, 1024), F32),
    "p3s": ((3, 128, 1024), BF),
    "p3r": ((3, 128, 1024), BF),
    "own3": ((128, 1024), F32),
    "dmid": ((128, 1024), F32),
    "da": ((128, 1024), BF),
    "da_c": ((4, 128, 256), BF),
    "dob": ((128, 1024), BF),
    "do_all": ((4, 128, 256), BF),
    "doz": ((512, 128), BF),
    "dkv": ((16, 128, 256), F32),
    "dkvb": ((4, 4, 128, 256), BF),
    "dkvr": ((3, 4, 128, 256), BF),
    "dqr": ((4, 128, 256), F32),
    "dqkv": ((4, 128, 512), BF),
    "p4r": ((3, 128, 1024), BF),
    "gF": ((4, 2, 128, 2304), BF),
    "gD": ((18, 64, 1024), BF),
    "gA": ((4, 2, 128, 768), BF),
    "r1F": ((4, 2, 64, 2304), BF),
    "r1D": ((18, 32, 1024), BF),
    "sD": ((4, 2, 2, 32, 1024), BF),
    "sX": ((2, 32, 1024), BF),
    "ax": ((3, 4, 32, 1152), BF),
    "at": ((4, 32, 1152), BF),
    "ay": ((3, 32, 1152), BF),
    "by": ((3, 2, 64, 1152), BF),
    "bt": ((2, 64, 1152), BF),
    "bx": ((3, 32, 1152), BF),
    "adx": ((3, 4, 2, 16, 512), BF),
    "adt": ((4, 2, 16, 512), BF),
    "ady": ((3, 2, 16, 512), BF),
    "bdy": ((3, 2, 2, 32, 512), BF),
    "bdt": ((2, 2, 32, 512), BF),
    "bdx": ((3, 2, 16, 512), BF),
    "xx": ((3, 16, 1024), BF),
    "xt": ((16, 1024), BF),
    "xy": ((3, 16, 1024), BF),
    "qax": ((3, 4, 32, 384), BF),
    "qat": ((4, 32, 384), BF),
    "qay": ((3, 32, 384), BF),
    "qby": ((3, 2, 64, 384), BF),
    "qbt": ((2, 64, 384), BF),
    "qbx": ((3, 32, 384), BF),
    "r1A": ((4, 2, 64, 768), BF),
    "oF": ((32, 2304), BF),
    "oD": ((3, 16, 1024), BF),
    "oA": ((32, 768), BF),
    "gsm": ((8, 8, 128), F32),
    "gs1": ((8, 8, 128), F32),
    "gs1s": ((8, 128), F32),
    "gs2": ((16, 8, 128), F32),
}
NSEM = 112


class Refs:
    pass


class Comm:
    def __init__(self, place, ssem, rsem):
        self.p, self.ssem, self.rsem = place, ssem, rsem
        self.n = 0
        self.sent = []

    def take(self, count=1):
        base = self.n
        self.n += count
        return base

    def copy(self, src, dst, i, dev):
        return pltpu.make_async_remote_copy(
            src_ref=src, dst_ref=dst, send_sem=self.ssem.at[i], recv_sem=self.rsem.at[i],
            device_id=dev, device_id_type=MESH,
        )

    def send(self, src, dst, i, dev):
        self.copy(src, dst, i, dev).start()
        self.sent.append((src, i))

    def part(self, src, dst, i, dev):
        self.copy(src, dst, i, dev).start()

    def whole(self, ref, i):
        self.sent.append((ref, i))

    def local(self, src, dst, i):
        return pltpu.make_async_copy(src, dst, self.rsem.at[i])

    def got(self, dst, i):
        self.copy(dst, dst, i, self.p.sib()).wait_recv()

    def flush(self, i):
        for src, j in self.sent:
            if j == i:
                self.copy(src, src, i, self.p.sib()).wait_send()
        self.sent = [e for e in self.sent if e[1] != i]

    def finish(self):
        for src, i in self.sent:
            self.copy(src, src, i, self.p.sib()).wait_send()
        self.sent = []


def kernel(*refs):
    r = Refs()
    names = INPUTS + list(OUTPUTS) + list(SCRATCH)
    for name, ref in zip(names, refs):
        setattr(r, name, ref)
    ssem, rsem = refs[len(names):]
    p = Place()
    m = Comm(p, ssem, rsem)

    def z_of(dz):
        return rem(p.z - dz + 4, 4)

    half = pl.ds(pl.multiple_of(p.c * 64, 64), 64)
    other = pl.ds(pl.multiple_of(64 - p.c * 64, 64), 64)
    zq = pl.ds(pl.multiple_of(p.z * 256, 256), 256)
    zk = pl.ds(pl.multiple_of(p.z * 128, 128), 128)
    dps = [rem(p.dp + 8 - k, 8) for k in range(8)]

    i_loc = m.take(4)
    parts = ((r.wq, zq, 0, 256), (r.wk, zk, 256, 128), (r.wv, zk, 384, 128))
    for w, cols, at, wid in parts:
        m.local(w.at[half, cols], r.wqkv.at[p.dp, half, pl.ds(at, wid)], i_loc).start()
    m.local(r.wo.at[half], r.wo_v.at[p.dp, half], i_loc + 1).start()

    def down_pieces(d):
        out = []
        for n in range(2):
            u = rem(2 * p.z + n - d + 8, 8)
            big = 9 * d + u
            out.append((u, 2 * lax.div(big, 8) + rem(big, 2)))
        big = 9 * d + 8
        return out + [(8, 2 * lax.div(big, 8) + rem(big, 2))], lax.div(d, 2) == p.z

    c32 = p.c * 32
    h32 = pl.ds(pl.multiple_of(c32, 32), 32)
    o32 = pl.ds(pl.multiple_of(32 - c32, 32), 32)
    i_ld = m.take(3)
    pieces, has_extra = down_pieces(p.dp)

    def down_local(n):
        u, hidx = pieces[n]
        src = r.wd.at[pl.ds(pl.multiple_of(u * 64 + c32, 32), 32)]
        return pltpu.make_async_copy(src, r.wd_v.at[hidx, h32], rsem.at[i_ld + n])

    for n in range(2):
        down_local(n).start()

    @pl.when(has_extra)
    def _():
        down_local(2).start()

    for src, dst, i in ((r.wg, r.wg_v, i_loc + 2), (r.wu, r.wu_v, i_loc + 3)):
        for t in range(9):
            cols = pl.ds(pl.multiple_of(t * 512 + p.z * 128, 128), 128)
            m.local(src.at[half, cols], dst.at[p.dp, half, pl.ds(t * 128, 128)], i).start()

    r.meta[0:1, :] = r.ga[...].astype(F32)
    r.meta[1:2, :] = r.gf[...].astype(F32)
    r.meta[2:3, :] = r.seg[...].astype(F32)
    r.meta[3:8, :] = jnp.zeros((5, 128), F32)

    bar = pltpu.get_barrier_semaphore()
    for k in range(1, 16):
        pl.semaphore_signal(bar, inc=1, device_id=p.speer(k), device_id_type=MESH)
    for k in range(1, 8):
        pl.semaphore_signal(bar, inc=1, device_id=p.dpeer(k), device_id_type=MESH)
    pl.semaphore_signal(bar, inc=1, device_id=p.xring(2), device_id_type=MESH)
    pl.semaphore_wait(bar, 23)

    class Shards:
        def __init__(self, buf, i_share):
            self.buf, self.share = buf, i_share
            self.iy, self.ix = m.take(3) - 1, m.take(1)

        def row(self, k, xl):
            return rem(p.y - k + 4, 4) * 2 + xl

        def quarter(self, t):
            return pl.ds(pl.multiple_of(p.c * 64 + (t - 1) * 32, 32), 32)

        def along_y(self):
            s = self.buf.at[p.dp, half]
            for k in (2, 1, 3):
                m.send(s, s, self.iy + k, p.ypeer(k))

        def along_x(self, k):
            d = self.row(k, p.xl)
            if k:
                m.got(self.buf.at[d, half], self.iy + k)
            for t in (1, 2):
                s = self.buf.at[d, self.quarter(t)]
                m.part(s, s, self.ix, p.xring(t))

        def to_core(self):
            m.whole(self.buf.at[0:4, half], self.ix)
            m.got(self.buf.at[0:4, half], self.ix)
            s = self.buf.at[:, half]
            m.send(s, s, self.share, p.sib())

        def done(self):
            m.got(self.buf.at[:, other], self.share)

    class Down:
        def __init__(self, i_share):
            self.share = i_share
            self.iy, self.ix = m.take(3) - 1, m.take(1)

        def start(self, d, t, i, dev):
            where, more = down_pieces(d)
            for n in range(3):
                rows = h32 if t == 0 else pl.ds(pl.multiple_of(c32 + (t - 1) * 16, 16), 16)
                s = r.wd_v.at[where[n][1], rows]
                if n < 2:
                    m.part(s, s, i, dev)
                else:

                    @pl.when(more)
                    def _():
                        m.part(s, s, i, dev)

        def wait(self, d, act):
            _, more = down_pieces(d)

            @pl.when(more)
            def _():
                act(r.wd_v.at[0:3, h32])

            @pl.when(jnp.logical_not(more))
            def _():
                act(r.wd_v.at[0:2, h32])

        def along_y(self):
            for k in (2, 1, 3):
                self.start(p.dp, 0, self.iy + k, p.ypeer(k))

        def along_x(self, k):
            d = rem(p.y - k + 4, 4) * 2 + p.xl
            if k:
                self.wait(d, lambda ref: m.got(ref, self.iy + k))
            for t in (1, 2):
                self.start(d, t, self.ix, p.xring(t))

        def to_core(self):
            m.whole(r.wd_v.at[0:9, h32], self.ix)
            m.got(r.wd_v.at[0:9, h32], self.ix)
            m.send(r.wd_v.at[:, h32], r.wd_v.at[:, h32], self.share, p.sib())

        def done(self):
            m.got(r.wd_v.at[:, o32], self.share)

        def finish(self):
            for k in (1, 2, 3):
                self.wait(p.dp, lambda ref: m.copy(ref, ref, self.iy + k, p.sib()).wait_send())

    i_share = m.take(5)
    w_qkv = Shards(r.wqkv, i_share)
    w_o = Shards(r.wo_v, i_share + 1)
    w_d = Down(i_share + 2)
    w_g = Shards(r.wg_v, i_share + 3)
    w_u = Shards(r.wu_v, i_share + 4)
    i_tok = m.take(3) - 1
    for dz in (2, 1, 3):
        m.send(r.tok, r.tok_all.at[dz], i_tok + dz, p.zpeer(dz))
    m.local(r.wqkv.at[0, half], r.wqkv.at[0, half], i_loc).wait()
    w_qkv.along_y()
    w_qkv.along_x(0)
    i_mseq = m.take()
    for k in range(1, 16):
        m.part(r.meta, r.mseq.at[p.sq], i_mseq, p.speer(k))
    m.whole(r.mseq.at[0:15], i_mseq)
    i_mdp = m.take()
    for k in range(1, 8):
        m.part(r.meta, r.mdp.at[p.dp], i_mdp, p.dpeer(k))
    m.whole(r.mdp.at[0:7], i_mdp)
    r.mseq[p.sq] = r.meta[...]
    r.mdp[p.dp] = r.meta[...]
    for k in (1, 3, 2):
        w_qkv.along_x(k)
    m.local(r.wo_v.at[0, half], r.wo_v.at[0, half], i_loc + 1).wait()
    w_o.along_y()
    for n in range(2):
        down_local(n).wait()

    @pl.when(has_extra)
    def _():
        down_local(2).wait()

    w_d.along_y()

    m.got(r.mseq.at[0:15], i_mseq)
    r.st[...] = seg_rows(r.mseq[:, 2, :])
    m.got(r.mdp.at[0:7], i_mdp)
    gain1 = jnp.concatenate([r.mdp[j, 0:1, :] for j in range(8)], axis=1)
    gain2 = jnp.concatenate([r.mdp[j, 1:2, :] for j in range(8)], axis=1)
    w_qkv.to_core()
    m.local(r.wg_v.at[0, half], r.wg_v.at[0, half], i_loc + 2).wait()
    w_g.along_y()
    m.local(r.wu_v.at[0, half], r.wu_v.at[0, half], i_loc + 3).wait()
    w_u.along_y()

    lanesign = jnp.where(lane_half(), -1.0, 1.0)
    freq = r.freq[...]
    for dz in range(4):
        i = 4 * z_of(dz) + p.g
        row = r.st[pl.ds(i, 1), :]
        pos = (lax.broadcasted_iota(jnp.int32, (1, 128), 1) + i * 128).astype(F32) - row
        ang = jnp.transpose(jnp.broadcast_to(pos, (128, 128))) * freq
        r.cosr[dz] = jnp.cos(ang)
        r.sinr[dz] = jnp.sin(ang) * lanesign
    w_qkv.done()

    wfull = r.wqkv[...].reshape(1024, 512)
    qg = jnp.concatenate([r.gq[...].astype(F32)] * 2, axis=1)
    kg = jnp.concatenate([r.gk[...].astype(F32)] * 2, axis=1)
    i_kv = m.take()
    i_kvx = m.take(4)
    i_kvf = m.take()

    def project(dz, x):
        x = x.astype(F32)
        r1 = lax.rsqrt(jnp.mean(x * x, axis=1, keepdims=True) + EPS)
        h = (x * r1 * gain1).astype(BF)
        r.tok_all[dz] = h
        o = dot(h, wfull)
        cs, sn = r.cosr[dz], r.sinr[dz]
        r.qk_raw[dz] = o[:, 0:384]
        rot = []
        for b, gn in ((0, qg), (1, qg), (2, kg)):
            v = o[:, b * 128:(b + 1) * 128]
            v = v * lax.rsqrt(head_mean(v * v) + EPS) * gn
            rot.append(v * cs + swap_halves(v) * sn)
        for hd, v in enumerate(spread_heads(rot[0], rot[1])):
            r.qz[dz, pl.ds(hd * 128, 128), :] = v.astype(BF)
        i = 4 * z_of(dz) + p.g
        r.kv[i, :, 0:128] = rot[2].astype(BF)
        r.kv[i, :, 128:256] = o[:, 384:512].astype(BF)
        m.send(r.kv.at[i], r.kv.at[i], i_kvx + dz, p.xpeer())
        m.part(r.kv.at[i], r.kv.at[i], i_kv, p.sib())

    project(0, r.tok[...])
    for k in (0, 1, 3, 2):
        w_o.along_x(k)
    for dz in (1, 3, 2):
        m.got(r.tok_all.at[dz], i_tok + dz)
        project(dz, r.tok_all[dz])
    i_cot = m.take()
    for dz in (1, 3, 2):
        m.part(r.cot, r.cot_all.at[dz], i_cot, p.zpeer(dz))
    m.whole(r.cot_all.at[1:4], i_cot)
    r.cot_all[0] = r.cot[...]
    for k in (0, 1, 3, 2):
        w_d.along_x(k)
    gs = p.g + 1 - 2 * p.c
    gx = (1 - p.xh) * 2 + p.c
    gxs = (1 - p.xh) * 2 + 1 - p.c
    for dz in (0, 1, 3, 2):
        zz = 4 * z_of(dz)
        m.got(r.kv.at[zz + gx], i_kvx + dz)
        m.part(r.kv.at[zz + gx], r.kv.at[zz + gx], i_kvf, p.sib())
    four = r.kv.at[0:4]
    for i in (i_kv, i_kvf):
        m.whole(four, i)
        m.got(four, i)

    def turn(first):
        def one(j, carry):
            t = jnp.transpose(r.kv[j, :, first:first + 128].astype(F32))
            r.kvt[:, pl.ds(pl.multiple_of(j * 128, 128), 128)] = t.astype(BF)
            return carry

        lax.fori_loop(0, 16, one, 0)

    turn(128)
    for k in (0, 1, 3, 2):
        w_g.along_x(k)
    w_o.to_core()

    def allowed_rows(i):
        row = r.st[pl.ds(i, 1), :].astype(jnp.int32)
        qi = lax.broadcasted_iota(jnp.int32, (1, 128), 1) + i * 128
        return jnp.concatenate([row] * 4, axis=1), jnp.concatenate([qi] * 4, axis=1)

    def window(i):
        return jnp.minimum(jnp.maximum(i - 8, 0), 7)

    def weights_of(kb, qv, row4, qi4):
        s = dot(r.kv[pl.ds(kb, 3), :, 0:128].reshape(384, 128), qv, NT)
        ki = lax.broadcasted_iota(jnp.int32, (384, 512), 0) + kb * 128
        return jnp.where((ki >= row4) & (ki <= qi4), jnp.exp2(s * (SCALE * LOG2E)), 0.0)

    def keys_turned(k0):
        return r.kvt[:, pl.ds(pl.multiple_of(k0 * 128, 128), 1152)]

    def heads_down(o):
        return jnp.concatenate(
            [o[(h // 2) * 64:(h // 2) * 64 + 64, h * 128:(h + 1) * 128] for h in range(4)], axis=0
        )

    def forward_chunk(dz):
        i = 4 * z_of(dz) + p.g
        k0 = window(i)
        row4, qi4 = allowed_rows(i)
        qv = r.qz[dz]
        total = jnp.zeros((8, 512), F32)
        for t in range(3):
            w = weights_of(k0 + 3 * t, qv, row4, qi4)
            total = total + jnp.sum(w.reshape(48, 8, 512), axis=0)
            r.pT[t * 384:(t + 1) * 384] = w.astype(BF)
        il = 1.0 / jnp.sum(total, axis=0, keepdims=True)
        r.invl[dz] = jnp.broadcast_to(il, (8, 512))
        full = heads_down(dot(keys_turned(k0), r.pT[...]) * il)
        r.oT[dz] = full
        r.o_s[dz] = jnp.transpose(full).astype(BF)

    i_o = m.take()
    for j in range(4):
        dz = (j + 1) % 4
        forward_chunk(dz)
        if dz:
            m.part(r.o_s.at[dz], r.o_in.at[p.z], i_o, p.zpeer(-dz))
        else:
            r.o_in[p.z] = r.o_s[0]
        if j == 1:
            for k in (0, 1, 3, 2):
                w_u.along_x(k)
            w_d.to_core()
    m.whole(r.o_in.at[0:3], i_o)

    w_g.to_core()
    m.got(r.o_in.at[0:3], i_o)
    for j in range(4):
        r.o_own[:, j * 256:(j + 1) * 256] = r.o_in[j]
    w_o.done()
    x0 = r.tok[...].astype(F32)
    middle = x0 + dot(r.o_own[...], r.wo_v[...].reshape(1024, 1024))
    r.mid[...] = middle
    r2 = lax.rsqrt(jnp.mean(middle * middle, axis=1, keepdims=True) + EPS)
    r.h2[0] = (middle * r2 * gain2).astype(BF)
    i_h2 = m.take(3) - 1
    for dz in (2, 1, 3):
        m.send(r.h2.at[0], r.h2.at[dz], i_h2 + dz, p.zpeer(dz))
    i_of = m.take()
    for dz in (2, 1, 3):
        m.part(r.o_own, r.o_full.at[dz], i_of, p.zpeer(dz))
    m.whole(r.o_full.at[1:4], i_of)
    r.o_full[0] = r.o_own[...]

    turn(0)
    w_u.to_core()
    m.got(r.cot_all.at[1:4], i_cot)
    w_d.done()
    wd = r.wd_v[...].reshape(1152, 1024)
    cots = r.cot_all[...].reshape(512, 1024)

    def cols384(t):
        return pl.ds(pl.multiple_of(t * 384, 128), 384)

    def dm_tile(t, carry):
        w = r.wd_v[pl.ds(t * 6, 6)].reshape(384, 1024)
        r.dm[:, :, cols384(t)] = dot(cots, w, NT).astype(BF).reshape(4, 128, 384)
        return carry

    lax.fori_loop(0, 3, dm_tile, 0)
    w_g.done()
    w_u.done()

    i_p2 = m.take()
    for pair in range(2):
        two = slice(2 * pair, 2 * pair + 2)
        for dz in ((1,), (2, 3))[pair]:
            m.got(r.h2.at[dz], i_h2 + dz)
        hh = r.h2[two].reshape(256, 1024)

        def ffn_tile(t, carry):
            cols = cols384(t)
            gate = dot(hh, r.wg_v[:, :, cols].reshape(1024, 384))
            up = dot(hh, r.wu_v[:, :, cols].reshape(1024, 384))
            sig = 1.0 / (1.0 + jnp.exp(-gate))
            act = gate * sig
            dmt = r.dm[two, :, cols].astype(F32).reshape(256, 384)
            r.mixed[two, :, cols] = (act * up).astype(BF).reshape(2, 128, 384)
            r.dg[two, :, cols] = (dmt * up * sig * (1.0 + gate * (1.0 - sig))).astype(BF).reshape(2, 128, 384)
            r.du[two, :, cols] = (dmt * act).astype(BF).reshape(2, 128, 384)
            return carry

        lax.fori_loop(0, 3, ffn_tile, 0)

    i_r1 = m.take(4)
    h2t = r.h2[...].reshape(512, 1024)

    def gate_tile(t, carry):
        w = r.dg[:, :, cols384(t)].reshape(512, 384)
        r.gF[:, :, :, cols384(t)] = dot(h2t, w, TN).astype(BF).reshape(4, 2, 128, 384)
        return carry

    def up_tile(t, carry):
        w = r.du[:, :, cols384(t)].reshape(512, 384)
        r.gF[:, :, :, cols384(t + 3)] = dot(h2t, w, TN).astype(BF).reshape(4, 2, 128, 384)
        return carry

    lax.fori_loop(0, 3, gate_tile, 0)
    m.send(r.gF.at[:, :, other, 0:1152], r.r1F.at[:, :, :, 0:1152], i_r1, p.sib())
    lax.fori_loop(0, 3, up_tile, 0)
    m.send(r.gF.at[:, :, other, 1152:2304], r.r1F.at[:, :, :, 1152:2304], i_r1 + 3, p.sib())
    for pair in (1, 0):
        two = slice(2 * pair, 2 * pair + 2)
        part = dot(r.dg[two].reshape(256, 1152), r.wg_v[...].reshape(1024, 1152), NT)
        part += dot(r.du[two].reshape(256, 1152), r.wu_v[...].reshape(1024, 1152), NT)
        if pair:
            r.p2s[1] = part[0:128].astype(BF)
            m.part(r.p2s.at[1], r.p2r.at[1], i_p2, p.zpeer(-2))
            r.p2s[2] = part[128:256].astype(BF)
            m.part(r.p2s.at[2], r.p2r.at[2], i_p2, p.zpeer(-3))
        else:
            r.p2s[0] = part[128:256].astype(BF)
            m.part(r.p2s.at[0], r.p2r.at[0], i_p2, p.zpeer(-1))
            r.own[...] = part[0:128]

    def down_tile(t, carry):
        w = r.mixed[:, :, cols384(t)].reshape(512, 384)
        r.gD[pl.ds(t * 6, 6)] = dot(w, cots, TN).astype(BF).reshape(6, 64, 1024)
        return carry

    lax.fori_loop(0, 3, down_tile, 0)
    m.send(r.gD.at[:, o32], r.r1D, i_r1 + 1, p.sib())

    m.got(r.r1F.at[:, :, :, 0:1152], i_r1)
    m.got(r.r1F.at[:, :, :, 1152:2304], i_r1 + 3)

    def add_core(d, carry):
        a, b = lax.div(d, 2), rem(d, 2)
        r.r1F[a, b] = (r.r1F[a, b].astype(F32) + r.gF[a, b, half].astype(F32)).astype(BF)
        return carry

    lax.fori_loop(0, 8, add_core, 0)

    def rows_of(x, n):
        return pl.ds(pl.multiple_of(x * n, n), n)

    class XFirst:
        def __init__(self, src, mid1, tot, mid2):
            self.src, self.mid1, self.tot, self.mid2 = src, mid1, tot, mid2
            self.i1, self.i2 = m.take(), m.take()

        def one(self):
            for t in (3, 1, 2):
                m.part(self.src(t), self.mid1.at[t - 1], self.i1, p.xring(t))
            m.whole(self.mid1, self.i1)

        def two(self):
            m.got(self.mid1, self.i1)

            def add(n, carry):
                v = self.src(0).at[n][...].astype(F32)
                for t in range(3):
                    v = v + self.mid1[t, n].astype(F32)
                self.tot[n] = v.astype(BF)
                return carry

            lax.fori_loop(0, 4, add, 0)
            for k in (2, 1, 3):
                m.part(self.tot.at[rem(p.y + k, 4)], self.mid2.at[k - 1], self.i2, p.ypeer(k))
            m.whole(self.mid2, self.i2)

        def sum(self):
            m.got(self.mid2, self.i2)
            v = self.tot[p.y].astype(F32)
            for k in range(3):
                v = v + self.mid2[k].astype(F32)
            return v.astype(BF)

    class YFirst:
        def __init__(self, src, part, mid1, tot, mid2):
            self.src, self.part, self.mid1, self.tot, self.mid2 = src, part, mid1, tot, mid2
            self.i1, self.i2 = m.take(), m.take()

        def one(self):
            for k in (2, 1, 3):
                m.part(self.src(rem(p.y + k, 4)), self.mid1.at[k - 1], self.i1, p.ypeer(k))
            m.whole(self.mid1, self.i1)

        def two(self):
            m.got(self.mid1, self.i1)

            def add(n, carry):
                v = self.src(p.y).at[n][...].astype(F32)
                for k in range(3):
                    v = v + self.mid1[k, n].astype(F32)
                self.tot[n] = v.astype(BF)
                return carry

            lax.fori_loop(0, 2, add, 0)
            for t in (3, 1, 2):
                m.part(self.part(self.tot, t), self.mid2.at[t - 1], self.i2, p.xring(t))
            m.whole(self.mid2, self.i2)

        def sum(self):
            m.got(self.mid2, self.i2)
            v = self.part(self.tot, 0)[...].astype(F32)
            for t in range(3):
                v = v + self.mid2[t].astype(F32)
            return v.astype(BF)

    def rows_x(buf, c0, c1):
        return lambda t: buf.at[:, p.xplace(t)[0], rows_of(p.xplace(t)[1], 32), c0:c1]

    def rows_y(buf, c0, c1):
        return lambda y: buf.at[y, :, :, c0:c1]

    def part_y(tot, t):
        xl, xh = p.xplace(t)
        return tot.at[xl, rows_of(xh, 32)]

    def part_d(tot, t):
        xl, xh = p.xplace(t)
        return tot.at[xl, :, rows_of(xh, 16)]

    sums = [
        XFirst(rows_x(r.r1F, 0, 1152), r.ax, r.at, r.ay),
        YFirst(rows_y(r.r1F, 1152, 2304), part_y, r.by, r.bt, r.bx),
        XFirst(
            lambda t: r.sD.at[:, p.xplace(t)[0], :, rows_of(p.xplace(t)[1], 16), 0:512], r.adx, r.adt, r.ady
        ),
        YFirst(lambda y: r.sD.at[y, :, :, :, 512:1024], part_d, r.bdy, r.bdt, r.bdx),
    ]
    for e in sums[0:2]:
        e.one()
    r.own3[...] = dot(r.mixed[0], wd)

    def out_chunk(dz, carry):
        r.p3s[dz - 1] = dot(r.mixed[dz], wd).astype(BF)
        return carry

    lax.fori_loop(1, 4, out_chunk, 0)
    m.got(r.r1D, i_r1 + 1)

    def add_core_down(d, carry):
        a, b = lax.div(d, 2), rem(d, 2)
        where, more = down_pieces(d)
        for n in range(2):
            t = where[n][1]
            r.sD[a, b, n] = (r.r1D[t].astype(F32) + r.gD[t, h32].astype(F32)).astype(BF)

        @pl.when(more)
        def _():
            t = where[2][1]
            r.sX[b] = (r.r1D[t].astype(F32) + r.gD[t, h32].astype(F32)).astype(BF)

        return carry

    lax.fori_loop(0, 8, add_core_down, 0)
    for e in sums[2:4]:
        e.one()
    i_x1 = m.take()
    i_x2 = m.take()
    for t in (3, 1, 2):
        xl, xh = p.xplace(t)
        m.part(r.sX.at[xl, rows_of(xh, 16)], r.xx.at[t - 1], i_x1, p.xring(t))
    m.whole(r.xx, i_x1)

    m.whole(r.p2s, i_p2)
    m.got(r.p2r, i_p2)
    dh2 = r.own[...] + r.p2r[0].astype(F32) + r.p2r[1].astype(F32) + r.p2r[2].astype(F32)
    middle = r.mid[...]
    r2 = lax.rsqrt(jnp.mean(middle * middle, axis=1, keepdims=True) + EPS)
    small2 = jnp.sum(dh2 * middle * r2, axis=0, keepdims=True)
    wdh = dh2 * gain2
    dmid = r.cot[...].astype(F32) + r2 * wdh - middle * (r2 * r2 * r2) * jnp.mean(wdh * middle, axis=1, keepdims=True)
    r.dmid[...] = dmid
    r.da[...] = dmid.astype(BF)
    i_do = m.take()

    def zcols(z):
        return pl.ds(pl.multiple_of(z * 256, 256), 256)

    for dz in (2, 1, 3, 0):
        zz = rem(p.z + dz, 4)
        w = r.wo_v[pl.ds(2 * zz, 2)].reshape(256, 1024)
        r.dob[:, zcols(zz)] = dot(r.da[...], w, NT).astype(BF)
        if dz:
            m.part(r.dob.at[:, zcols(zz)], r.do_all.at[dz], i_do, p.zpeer(dz))
    m.whole(r.do_all.at[1:4], i_do)
    r.do_all[0] = r.dob[:, zq]
    i_p3 = m.take()
    i_dc = m.take()
    for dz in (2, 1, 3):
        m.part(r.da.at[:, zcols(rem(p.z + dz, 4))], r.da_c.at[dz], i_dc, p.zpeer(dz))
    m.whole(r.da_c.at[1:4], i_dc)
    for dz in (2, 1, 3):
        m.part(r.p3s.at[dz - 1], r.p3r.at[dz - 1], i_p3, p.zpeer(-dz))
    m.whole(r.p3s, i_p3)
    r.da_c[0] = r.da[:, zq]

    r.dkv[...] = jnp.zeros_like(r.dkv)
    m.got(r.do_all.at[1:4], i_do)
    for e in sums[0:2]:
        e.two()

    lane = lax.broadcasted_iota(jnp.int32, (1, 256), 1)
    kscale = jnp.where(lane < 128, SCALE, 1.0)
    i_dkv = m.take()
    xs = (p.dp, p.z * 4 + gxs)

    def backward_chunk(j, carry):
        zz = 3 - j
        dz = rem(p.z - zz + 4, 4)
        i = 4 * zz + p.g
        row4, qi4 = allowed_rows(i)
        do = r.do_all[dz].astype(F32)
        for hd, v in enumerate(spread_heads(do[:, 0:128], do[:, 128:256])):
            r.doz[pl.ds(hd * 128, 128), :] = v.astype(BF)
        prod = jnp.transpose(do) * r.oT[dz]
        drow = jnp.concatenate(
            [jnp.sum(prod[h * 64:(h + 1) * 64], axis=0, keepdims=True) for h in range(4)], axis=1
        )
        il = r.invl[dz, 0:1, :]
        qv = r.qz[dz]
        dov = r.doz[...]
        k0 = window(i)
        for t in range(3):
            rows = slice(t * 384, (t + 1) * 384)
            w = weights_of(k0 + 3 * t, qv, row4, qi4) * il
            r.pT[rows] = w.astype(BF)
            dp = dot(r.kv[pl.ds(k0 + 3 * t, 3), :, 128:256].reshape(384, 128), dov, NT)
            r.dsT[rows] = (w * (dp - drow)).astype(BF)
        nine = pl.ds(k0, 9)
        r.dkv[nine, :, 0:128] += dot(r.dsT[...], qv).reshape(9, 128, 128)
        r.dkv[nine, :, 128:256] += dot(r.pT[...], dov).reshape(9, 128, 128)
        r.dkvb[zz] = (r.dkv[pl.ds(4 * zz, 4)] * kscale.reshape(1, 1, 256)).astype(BF)
        m.part(r.dkvb.at[zz, gx], r.dkvr.at[1, zz], i_dkv, p.xpeer())
        m.part(r.dkvb.at[zz, gxs], r.dkvr.at[2, zz], i_dkv, xs)
        m.part(r.dkvb.at[zz, gs], r.dkvr.at[0, zz], i_dkv, p.sib())
        r.dqr[dz] = jnp.transpose(heads_down(dot(keys_turned(k0), r.dsT[...]) * SCALE))
        return carry

    lax.fori_loop(0, 4, backward_chunk, 0)

    m.whole(r.dkvr, i_dkv)

    for e in sums[2:4]:
        e.two()
    m.got(r.xx, i_x1)
    v = r.sX[p.xl, rows_of(p.xh, 16)].astype(F32)
    for t in range(3):
        v = v + r.xx[t].astype(F32)
    r.xt[...] = v.astype(BF)
    kz = rem(p.z - p.y + 4, 4)

    @pl.when(kz != 0)
    def _():
        m.part(r.xt, r.xy.at[kz - 1], i_x2, (p.z * 2 + p.xl, p.sq))

    r.oF[:, 0:1152] = sums[0].sum()
    r.oF[:, 1152:2304] = sums[1].sum()

    def seq_at(z, g):
        return rem(z + 8, 4) * 4 + g

    class Gather:
        def __init__(self, own, buf, order):
            self.own, self.buf, self.order = own, buf, order
            self.il, self.ix, self.iz, self.ic = m.take(), m.take(), m.take(), m.take()

        def on(self, src, s, where):
            if "x" in where:
                m.part(src, s, self.ix, p.xpeer())
            if "z" in where:
                for dz in (2, 1, 3):
                    m.part(src, s, self.iz, p.zpeer(dz))
            if "b" in where:
                for dz in (2, 1, 3):
                    m.part(src, s, self.iz, (p.dp, seq_at(p.z + dz, gx)))
            if "c" in where:
                m.part(src, s, self.ic, p.sib())

        def got(self, n, i):
            m.got(self.buf.at[0:n], i)

        def slot(self, dz, g):
            return self.buf.at[seq_at(p.z - dz, g)]

        def first(self):
            m.local(self.own, self.slot(0, p.g), self.il).start()
            self.on(self.own, self.slot(0, p.g), "zxcb" if self.order == "zx" else "zxc")

        def second(self):
            if self.order == "x":
                self.got(1, self.ix)
                s = self.slot(0, gx)
                self.on(s, s, "zc")
            elif self.order == "z":
                self.got(3, self.iz)
                for dz in (1, 2, 3):
                    s = self.slot(dz, p.g)
                    self.on(s, s, "xc")
            else:
                self.got(1, self.ix)
                self.got(6, self.iz)
                for dz in range(4):
                    for g in (p.g, gx)[dz == 0:]:
                        s = self.slot(dz, g)
                        self.on(s, s, "c")

        def third(self):
            if self.order == "x":
                self.got(6, self.iz)
                for dz in (1, 2, 3):
                    for g in (p.g, gx):
                        s = self.slot(dz, g)
                        self.on(s, s, "c")
            elif self.order == "z":
                self.got(4, self.ix)
                for dz in range(4):
                    s = self.slot(dz, gx)
                    self.on(s, s, "c")

        def last(self):
            n = {"x": (1, 6), "z": (4, 3), "zx": (1, 6)}[self.order]
            m.whole(self.buf.at[0:n[0]], self.ix)
            m.whole(self.buf.at[0:n[1]], self.iz)
            m.whole(self.buf.at[0:8], self.ic)
            self.got(8, self.ic)
            m.local(self.own, self.slot(0, p.g), self.il).wait()

    ag_f = Gather(r.oF, r.fF, "z")
    ag_d = Gather(r.oD, r.fD, "x")
    ag_a = Gather(r.oA, r.fA, "zx")
    ag_f.first()

    m.got(r.o_full.at[1:4], i_of)
    m.got(r.da_c.at[1:4], i_dc)
    m.got(r.p3r, i_p3)
    r.gA[:, :, :, 512:768] = dot(
        r.o_full[...].reshape(512, 1024), r.da_c[...].reshape(512, 256), TN
    ).astype(BF).reshape(4, 2, 128, 256)
    r.block_out[...] = (
        r.mid[...] + r.own3[...] + r.p3r[0].astype(F32) + r.p3r[1].astype(F32) + r.p3r[2].astype(F32)
    ).astype(BF)

    m.got(r.dkvr, i_dkv)
    sq_acc = jnp.zeros((1, 128), F32)
    sk_acc = jnp.zeros((1, 128), F32)
    for dz in range(4):
        zz = z_of(dz)
        i = 4 * zz + p.g
        dkv = r.dkv[i] * kscale
        for n in range(3):
            dkv = dkv + r.dkvr[n, zz].astype(F32)
        cs, sn = r.cosr[dz], r.sinr[dz]
        grads = (r.dqr[dz, :, 0:128], r.dqr[dz, :, 128:256], dkv[:, 0:128])
        for b, gr in enumerate(grads):
            gn = qg if b < 2 else kg
            v = r.qk_raw[dz, :, b * 128:(b + 1) * 128]
            f = lax.rsqrt(head_mean(v * v) + EPS)
            dn = gr * cs - swap_halves(gr) * sn
            add = jnp.sum(dn * v * f, axis=0, keepdims=True)
            if b < 2:
                sq_acc = sq_acc + add
            else:
                sk_acc = sk_acc + add
            wn = dn * gn
            r.dqkv[dz, :, b * 128:(b + 1) * 128] = (f * wn - v * (f * f * f) * head_mean(wn * v)).astype(BF)
        r.dqkv[dz, :, 384:512] = dkv[:, 128:256].astype(BF)
    r.gA[:, :, :, 0:512] = dot(
        r.tok_all[...].reshape(512, 1024), r.dqkv[...].reshape(512, 512), TN
    ).astype(BF).reshape(4, 2, 128, 512)
    m.send(r.gA.at[:, :, other], r.r1A, i_r1 + 2, p.sib())
    i_p4 = m.take()
    m.flush(i_p2)
    for dz in (2, 1, 3):
        r.p2s[dz - 1] = dot(r.dqkv[dz], r.wqkv[...].reshape(1024, 512), NT).astype(BF)
        m.part(r.p2s.at[dz - 1], r.p4r.at[dz - 1], i_p4, p.zpeer(-dz))
    m.whole(r.p2s, i_p4)
    r.own[...] = dot(r.dqkv[0], r.wqkv[...].reshape(1024, 512), NT)
    r.oD[0:2, :, 0:512] = sums[2].sum()
    r.oD[0:2, :, 512:1024] = sums[3].sum()

    @pl.when(kz == 0)
    def _():
        v = r.xt[...].astype(F32)
        m.got(r.xy, i_x2)
        for k in range(3):
            v = v + r.xy[k].astype(F32)
        r.oD[2] = v.astype(BF)

    @pl.when(kz != 0)
    def _():
        r.oD[2] = jnp.zeros((16, 1024), BF)

    ag_d.first()
    m.got(r.r1A, i_r1 + 2)
    r.r1A[...] = (r.r1A[...].astype(F32) + r.gA[:, :, half].astype(F32)).astype(BF)
    sums_a = [
        XFirst(rows_x(r.r1A, 0, 384), r.qax, r.qat, r.qay),
        YFirst(rows_y(r.r1A, 384, 768), part_y, r.qby, r.qbt, r.qbx),
    ]
    for e in sums_a:
        e.one()
    ag_f.second()
    ag_d.second()
    for e in sums_a:
        e.two()

    m.got(r.p4r, i_p4)
    dh = r.own[...] + r.p4r[0].astype(F32) + r.p4r[1].astype(F32) + r.p4r[2].astype(F32)
    x0 = r.tok[...].astype(F32)
    r1 = lax.rsqrt(jnp.mean(x0 * x0, axis=1, keepdims=True) + EPS)
    small1 = jnp.sum(dh * x0 * r1, axis=0, keepdims=True)
    wdh = dh * gain1
    r.input_grad[...] = (
        r.dmid[...] + r1 * wdh - x0 * (r1 * r1 * r1) * jnp.mean(wdh * x0, axis=1, keepdims=True)
    ).astype(BF)

    both = lambda v: v + pltpu.roll(v, 64, 1)
    for d in range(8):
        cols = slice(d * 128, (d + 1) * 128)
        r.gsm[d] = jnp.concatenate(
            [small1[:, cols], small2[:, cols], both(sq_acc), both(sk_acc), jnp.zeros((4, 128), F32)], axis=0
        )
    i_s1 = m.take()
    i_s2 = m.take()
    for k in range(1, 8):
        m.part(r.gsm.at[rem(p.dp + k, 8)], r.gs1.at[k], i_s1, p.dpeer(k))
    m.whole(r.gs1.at[1:8], i_s1)
    r.gs1[0] = r.gsm[p.dp]
    r.oA[:, 0:384] = sums_a[0].sum()
    r.oA[:, 384:768] = sums_a[1].sum()
    ag_a.first()
    ag_f.third()
    m.got(r.gs1.at[1:8], i_s1)
    r.gs1s[...] = jnp.sum(r.gs1[...], axis=0)
    for k in range(1, 16):
        m.part(r.gs1s, r.gs2.at[k], i_s2, p.speer(k))
    m.whole(r.gs2.at[1:16], i_s2)
    r.gs2[0] = r.gs1s[...]
    ag_d.third()
    ag_a.second()
    m.got(r.gs2.at[1:16], i_s2)
    r.g_small[...] = jnp.sum(r.gs2[...], axis=0)
    ag_f.last()
    ag_d.last()
    ag_a.last()

    m.finish()
    w_d.finish()

    @pl.when(kz != 0)
    def _():
        m.copy(r.xt, r.xt, i_x2, p.sib()).wait_send()

    assert m.n <= NSEM, m.n


def block(args):
    vm = pl.BlockSpec(memory_space=pltpu.VMEM)
    hb = pl.BlockSpec(memory_space=pl.ANY)
    return pl.pallas_call(
        kernel,
        out_shape=tuple(jax.ShapeDtypeStruct(s, d) for s, d in OUTPUTS.values()),
        in_specs=[vm] * 7 + [hb] * 7 + [vm],
        out_specs=tuple(hb if name[0] == "f" else vm for name in OUTPUTS),
        scratch_shapes=[pltpu.VMEM(s, d) for s, d in SCRATCH.values()]
        + [pltpu.SemaphoreType.DMA((NSEM,)), pltpu.SemaphoreType.DMA((NSEM,))],
        compiler_params=pltpu.CompilerParams(
            collective_id=0, has_side_effects=True, vmem_limit_bytes=63 * 2**20
        ),
        name="block",
    )(*args)


PLACED = {
    "g_gate": (128, 4608),
    "g_up": (128, 4608),
    "g_down": (576, 1024),
    "g_q": (128, 1024),
    "g_k": (128, 512),
    "g_v": (128, 512),
    "g_out": (128, 1024),
}

LAID = {
    "block_out": ((128, 1024), BF),
    "input_grad": ((128, 1024), BF),
    "g_attn": ((1, 128), F32),
    "g_ffn": ((1, 128), F32),
    "g_qg": ((1, 64), F32),
    "g_kg": ((1, 64), F32),
    **{name: (shape, F32) for name, shape in PLACED.items()},
}


def lay_kernel(f_f, f_d, f_a, b_o, i_g, sm, *refs):
    outs = dict(zip(LAID, refs[:len(LAID)]))
    v_f, v_d, v_a = refs[len(LAID):len(LAID) + 3]
    stage = dict(zip(PLACED, refs[len(LAID) + 3:len(LAID) + 3 + len(PLACED)]))
    isem, osem = refs[len(LAID) + 3 + len(PLACED):]
    p = Place()
    ins = [
        pltpu.make_async_copy(f_f.at[:, :, 0:1152], v_f.at[:, :, 0:1152], isem.at[0]),
        pltpu.make_async_copy(f_f.at[:, :, 1152:2304], v_f.at[:, :, 1152:2304], isem.at[3]),
        pltpu.make_async_copy(f_d, v_d, isem.at[1]),
        pltpu.make_async_copy(f_a, v_a, isem.at[2]),
    ]
    for q in ins:
        q.start()
    outs["block_out"][...] = b_o[...]
    outs["input_grad"][...] = i_g[...]
    outs["g_attn"][...] = sm[0:1, :]
    outs["g_ffn"][...] = sm[1:2, :]
    outs["g_qg"][...] = sm[2:3, 0:64]
    outs["g_kg"][...] = sm[3:4, 0:64]

    def place(name):
        n = list(PLACED).index(name)
        return pltpu.make_async_copy(stage[name], outs[name], osem.at[n])

    def row_of(s):
        g = rem(s, 4)
        return pl.ds(pl.multiple_of(rem(g, 2) * 64 + lax.div(g, 2) * 32, 32), 32)

    for name, base, q in (("g_gate", 0, ins[0]), ("g_up", 1152, ins[1])):
        q.wait()

        def lay(g, carry):
            row = row_of(g)
            for z in range(4):
                for t in range(9):
                    cols = slice(t * 512 + z * 128, t * 512 + z * 128 + 128)
                    v = v_f[4 * z + g, :, base + t * 128:base + (t + 1) * 128]
                    stage[name][row, cols] = v.astype(F32)
            n = list(PLACED).index(name)
            pltpu.make_async_copy(stage[name].at[row], outs[name].at[row], osem.at[n]).start()
            return carry

        lax.fori_loop(0, 4, lay, 0)
    ins[2].wait()

    def lay_down(s, carry):
        z = lax.div(s, 4)
        g = rem(s, 4)
        sub = rem(g, 2) * 32 + lax.div(g, 2) * 16
        for n in range(2):
            u = rem(2 * z + n - p.dp + 8, 8)
            stage["g_down"][pl.ds(pl.multiple_of(u * 64 + sub, 16), 16), :] = v_d[s, n].astype(F32)

        @pl.when(lax.div(p.dp, 2) == z)
        def _():
            stage["g_down"][pl.ds(pl.multiple_of(8 * 64 + sub, 16), 16), :] = v_d[s, 2].astype(F32)

        return carry

    lax.fori_loop(0, 16, lay_down, 0)
    place("g_down").start()
    ins[3].wait()

    def lay_attn(s, carry):
        z = lax.div(s, 4)
        row = row_of(s)
        c256 = pl.ds(pl.multiple_of(z * 256, 256), 256)
        c128 = pl.ds(pl.multiple_of(z * 128, 128), 128)
        stage["g_q"][row, c256] = v_a[s, :, 0:256].astype(F32)
        stage["g_k"][row, c128] = v_a[s, :, 256:384].astype(F32)
        stage["g_v"][row, c128] = v_a[s, :, 384:512].astype(F32)
        stage["g_out"][row, c256] = v_a[s, :, 512:768].astype(F32)
        return carry

    lax.fori_loop(0, 16, lay_attn, 0)
    for name in ("g_q", "g_k", "g_v", "g_out"):
        place(name).start()
    for name in PLACED:
        place(name).wait()


def lay_out(o):
    hb = pl.BlockSpec(memory_space=pl.ANY)
    vm = pl.BlockSpec(memory_space=pltpu.VMEM)
    small = ("block_out", "input_grad", "g_attn", "g_ffn", "g_qg", "g_kg")
    got = pl.pallas_call(
        lay_kernel,
        out_shape=tuple(jax.ShapeDtypeStruct(s, d) for s, d in LAID.values()),
        in_specs=[hb] * 3 + [vm] * 3,
        out_specs=tuple(vm if n in small else hb for n in LAID),
        scratch_shapes=[pltpu.VMEM(*OUTPUTS[n]) for n in ("fF", "fD", "fA")]
        + [pltpu.VMEM(s, F32) for s in PLACED.values()]
        + [pltpu.SemaphoreType.DMA((4,)), pltpu.SemaphoreType.DMA((len(PLACED),))],
        compiler_params=pltpu.CompilerParams(vmem_limit_bytes=62 * 2**20),
        name="lay",
    )(o["fF"], o["fD"], o["fA"], o["block_out"], o["input_grad"], o["g_small"])
    return dict(zip(LAID, got))


def local(
    tokens, segment_ids, attn_gain, w_query, w_key, w_value, w_out, ffn_gain, w_gate, w_up, w_down,
    query_gain, key_gain, cotangent,
):
    inverse = ROPE_BASE ** (-(np.arange(32).astype(np.float32) * np.float32(2.0) / np.float32(64)))
    freq = jnp.asarray(np.tile(inverse.astype(np.float32), 4)[None])
    o = block(
        (
            tokens, segment_ids, attn_gain[None], ffn_gain[None], query_gain[None], key_gain[None], freq, w_query, w_key, w_value,
            w_out, w_gate, w_up, w_down, cotangent,
        )
    )
    o = dict(zip(OUTPUTS, o))
    w = lay_out(o)
    return (
        w["block_out"], w["input_grad"], w["g_attn"].reshape(128), w["g_q"], w["g_k"], w["g_v"], w["g_out"],
        w["g_ffn"].reshape(128), w["g_gate"], w["g_up"], w["g_down"], w["g_qg"].reshape(64),
        w["g_kg"].reshape(64),
    )


def solution(mesh):
    both = ("dp", "seq")
    w = P("dp", None)
    return jax.shard_map(
        local,
        mesh=mesh,
        in_specs=(P(both, None), P("dp", "seq"), P("dp"), w, w, w, w, P("dp"), w, w, w, P(), P(), P(both, None)),
        out_specs=(P(both, None), P(both, None), P("dp"), w, w, w, w, P("dp"), w, w, w, P(), P()),
        check_vma=False,
    )
```

```python
import math

import jax
import jax.numpy as jnp
import numpy as np
from jax import lax
from jax.experimental import pallas as pl
from jax.experimental.pallas import tpu as pltpu
from jax.sharding import PartitionSpec as P

MESH = pl.DeviceIdType.MESH
F32 = jnp.float32
BF = jnp.bfloat16
EPS = 1e-05
ROPE_BASE = 1000000.0
NN = (((1,), (0,)), ((), ()))
NT = (((1,), (1,)), ((), ()))
TN = (((0,), (0,)), ((), ()))
SCALE = 0.125
LOG2E = math.log2(math.e)


def dot(a, b, dims=NN, precision=None):
    return lax.dot_general(a, b, dims, preferred_element_type=F32, precision=precision)


def rem(a, b):
    return lax.rem(a, b)


class Place:
    def __init__(self):
        self.dp = lax.axis_index("dp")
        self.sq = lax.axis_index("seq")
        self.y = lax.div(self.dp, 2)
        self.xl = rem(self.dp, 2)
        self.z = lax.div(self.sq, 4)
        self.g = rem(self.sq, 4)
        self.xh = lax.div(self.g, 2)
        self.c = rem(self.sq, 2)

    def zpeer(self, dz):
        return (self.dp, rem(self.z + dz + 4, 4) * 4 + self.g)

    def sib(self):
        return (self.dp, self.sq + 1 - 2 * self.c)

    def xpeer(self):
        return (self.dp, self.z * 4 + (1 - self.xh) * 2 + self.c)

    def dpeer(self, k):
        return (rem(self.dp + k + 8, 8), self.sq)

    def speer(self, k):
        return (self.dp, rem(self.sq + k + 16, 16))

    def ypeer(self, k):
        return (rem(self.y + k + 4, 4) * 2 + self.xl, self.sq)

    def xring(self, t):
        xl = self.xl if t == 3 else 1 - self.xl
        return (self.y * 2 + xl, self.sq if t == 1 else self.z * 4 + (1 - self.xh) * 2 + self.c)

    def xplace(self, t):
        return (self.xl if t in (0, 3) else 1 - self.xl), (self.xh if t in (0, 1) else 1 - self.xh)


def seg_rows(ids):
    start = jnp.zeros_like(ids)
    for j in range(1, 8):
        below = jnp.sum(jnp.where(ids < j, 1.0, 0.0), keepdims=True)
        start = jnp.where(ids == j, below, start)
    return start


def lane_half():
    return lax.rem(lax.broadcasted_iota(jnp.int32, (1, 128), 1), 64) < 32


def swap_halves(x):
    return jnp.where(lane_half(), pltpu.roll(x, 96, 1), pltpu.roll(x, 32, 1))


def head_mean(x):
    a = lax.div(lax.broadcasted_iota(jnp.int32, (128, 128), 0), 64)
    b = lax.div(lax.broadcasted_iota(jnp.int32, (128, 128), 1), 64)
    block = jnp.where(a == b, 1.0 / 64, 0.0)
    return dot(x, block, NN, lax.Precision.HIGHEST)


def spread_heads(first, second):
    lo = lax.broadcasted_iota(jnp.int32, (1, 128), 1) < 64
    return [
        jnp.where(lo, first, 0.0),
        jnp.where(lo, pltpu.roll(first, 64, 1), 0.0),
        jnp.where(lo, 0.0, pltpu.roll(second, 64, 1)),
        jnp.where(lo, 0.0, second),
    ]


INPUTS = ["tok", "seg", "ga", "gf", "gq", "gk", "freq", "wq", "wk", "wv", "wo", "wg", "wu", "wd", "cot"]
OUTPUTS = {
    "block_out": ((128, 1024), BF),
    "input_grad": ((128, 1024), BF),
    "fF": ((16, 32, 2304), BF),
    "fD": ((16, 3, 16, 1024), BF),
    "fA": ((16, 32, 768), BF),
    "g_small": ((8, 128), F32),
}
SCRATCH = {
    "tok_all": ((4, 128, 1024), BF),
    "cot_all": ((4, 128, 1024), BF),
    "meta": ((8, 128), F32),
    "mseq": ((16, 8, 128), F32),
    "mdp": ((8, 8, 128), F32),
    "wqkv": ((8, 128, 512), BF),
    "wo_v": ((8, 128, 1024), BF),
    "wg_v": ((8, 128, 1152), BF),
    "wu_v": ((8, 128, 1152), BF),
    "wd_v": ((18, 64, 1024), BF),
    "st": ((16, 128), F32),
    "qk_raw": ((4, 128, 384), F32),
    "qz": ((4, 512, 128), BF),
    "kv": ((16, 128, 256), BF),
    "kvt": ((128, 2048), BF),
    "pT": ((1152, 512), BF),
    "dsT": ((1152, 512), BF),
    "cosr": ((4, 128, 128), F32),
    "sinr": ((4, 128, 128), F32),
    "invl": ((4, 8, 512), F32),
    "oT": ((4, 256, 128), F32),
    "o_s": ((4, 128, 256), BF),
    "o_in": ((4, 128, 256), BF),
    "o_own": ((128, 1024), BF),
    "o_full": ((4, 128, 1024), BF),
    "mid": ((128, 1024), F32),
    "h2": ((4, 128, 1024), BF),
    "dm": ((4, 128, 1152), BF),
    "mixed": ((4, 128, 1152), BF),
    "dg": ((4, 128, 1152), BF),
    "du": ((4, 128, 1152), BF),
    "p2s": ((3, 128, 1024), BF),
    "p2r": ((3, 128, 1024), BF),
    "own": ((128, 1024), F32),
    "p3s": ((3, 128, 1024), BF),
    "p3r": ((3, 128, 1024), BF),
    "own3": ((128, 1024), F32),
    "dmid": ((128, 1024), F32),
    "da": ((128, 1024), BF),
    "da_c": ((4, 128, 256), BF),
    "dob": ((128, 1024), BF),
    "do_all": ((4, 128, 256), BF),
    "doz": ((512, 128), BF),
    "dkv": ((16, 128, 256), F32),
    "dkvb": ((4, 4, 128, 256), BF),
    "dkvr": ((3, 4, 128, 256), BF),
    "dqr": ((4, 128, 256), F32),
    "dqkv": ((4, 128, 512), BF),
    "p4r": ((3, 128, 1024), BF),
    "gF": ((4, 2, 128, 2304), BF),
    "gD": ((18, 64, 1024), BF),
    "gA": ((4, 2, 128, 768), BF),
    "r1F": ((4, 2, 64, 2304), BF),
    "r1D": ((18, 32, 1024), BF),
    "sD": ((4, 2, 2, 32, 1024), BF),
    "sX": ((2, 32, 1024), BF),
    "ax": ((3, 4, 32, 1152), BF),
    "at": ((4, 32, 1152), BF),
    "ay": ((3, 32, 1152), BF),
    "by": ((3, 2, 64, 1152), BF),
    "bt": ((2, 64, 1152), BF),
    "bx": ((3, 32, 1152), BF),
    "adx": ((3, 4, 2, 16, 512), BF),
    "adt": ((4, 2, 16, 512), BF),
    "ady": ((3, 2, 16, 512), BF),
    "bdy": ((3, 2, 2, 32, 512), BF),
    "bdt": ((2, 2, 32, 512), BF),
    "bdx": ((3, 2, 16, 512), BF),
    "xx": ((3, 16, 1024), BF),
    "xt": ((16, 1024), BF),
    "xy": ((3, 16, 1024), BF),
    "qax": ((3, 4, 32, 384), BF),
    "qat": ((4, 32, 384), BF),
    "qay": ((3, 32, 384), BF),
    "qby": ((3, 2, 64, 384), BF),
    "qbt": ((2, 64, 384), BF),
    "qbx": ((3, 32, 384), BF),
    "r1A": ((4, 2, 64, 768), BF),
    "oF": ((32, 2304), BF),
    "oD": ((3, 16, 1024), BF),
    "oA": ((32, 768), BF),
    "gsm": ((8, 8, 128), F32),
    "gs1": ((8, 8, 128), F32),
    "gs1s": ((8, 128), F32),
    "gs2": ((16, 8, 128), F32),
}
NSEM = 112


class Refs:
    pass


class Comm:
    def __init__(self, place, ssem, rsem):
        self.p, self.ssem, self.rsem = place, ssem, rsem
        self.n = 0
        self.sent = []

    def take(self, count=1):
        base = self.n
        self.n += count
        return base

    def copy(self, src, dst, i, dev):
        return pltpu.make_async_remote_copy(
            src_ref=src, dst_ref=dst, send_sem=self.ssem.at[i], recv_sem=self.rsem.at[i],
            device_id=dev, device_id_type=MESH,
        )

    def send(self, src, dst, i, dev):
        self.copy(src, dst, i, dev).start()
        self.sent.append((src, i))

    def part(self, src, dst, i, dev):
        self.copy(src, dst, i, dev).start()

    def whole(self, ref, i):
        self.sent.append((ref, i))

    def local(self, src, dst, i):
        return pltpu.make_async_copy(src, dst, self.rsem.at[i])

    def got(self, dst, i):
        self.copy(dst, dst, i, self.p.sib()).wait_recv()

    def flush(self, i):
        for src, j in self.sent:
            if j == i:
                self.copy(src, src, i, self.p.sib()).wait_send()
        self.sent = [e for e in self.sent if e[1] != i]

    def finish(self):
        for src, i in self.sent:
            self.copy(src, src, i, self.p.sib()).wait_send()
        self.sent = []


def kernel(*refs):
    r = Refs()
    names = INPUTS + list(OUTPUTS) + list(SCRATCH)
    for name, ref in zip(names, refs):
        setattr(r, name, ref)
    ssem, rsem = refs[len(names):]
    p = Place()
    m = Comm(p, ssem, rsem)

    def z_of(dz):
        return rem(p.z - dz + 4, 4)

    half = pl.ds(pl.multiple_of(p.c * 64, 64), 64)
    other = pl.ds(pl.multiple_of(64 - p.c * 64, 64), 64)
    zq = pl.ds(pl.multiple_of(p.z * 256, 256), 256)
    zk = pl.ds(pl.multiple_of(p.z * 128, 128), 128)
    dps = [rem(p.dp + 8 - k, 8) for k in range(8)]

    i_loc = m.take(4)
    parts = ((r.wq, zq, 0, 256), (r.wk, zk, 256, 128), (r.wv, zk, 384, 128))
    for w, cols, at, wid in parts:
        m.local(w.at[half, cols], r.wqkv.at[p.dp, half, pl.ds(at, wid)], i_loc).start()
    m.local(r.wo.at[half], r.wo_v.at[p.dp, half], i_loc + 1).start()

    def down_pieces(d):
        out = []
        for n in range(2):
            u = rem(2 * p.z + n - d + 8, 8)
            big = 9 * d + u
            out.append((u, 2 * lax.div(big, 8) + rem(big, 2)))
        big = 9 * d + 8
        return out + [(8, 2 * lax.div(big, 8) + rem(big, 2))], lax.div(d, 2) == p.z

    c32 = p.c * 32
    h32 = pl.ds(pl.multiple_of(c32, 32), 32)
    o32 = pl.ds(pl.multiple_of(32 - c32, 32), 32)
    i_ld = m.take(3)
    pieces, has_extra = down_pieces(p.dp)

    def down_local(n):
        u, hidx = pieces[n]
        src = r.wd.at[pl.ds(pl.multiple_of(u * 64 + c32, 32), 32)]
        return pltpu.make_async_copy(src, r.wd_v.at[hidx, h32], rsem.at[i_ld + n])

    for n in range(2):
        down_local(n).start()

    @pl.when(has_extra)
    def _():
        down_local(2).start()

    for src, dst, i in ((r.wg, r.wg_v, i_loc + 2), (r.wu, r.wu_v, i_loc + 3)):
        for t in range(9):
            cols = pl.ds(pl.multiple_of(t * 512 + p.z * 128, 128), 128)
            m.local(src.at[half, cols], dst.at[p.dp, half, pl.ds(t * 128, 128)], i).start()

    r.meta[0:1, :] = r.ga[...].astype(F32)
    r.meta[1:2, :] = r.gf[...].astype(F32)
    r.meta[2:3, :] = r.seg[...].astype(F32)
    r.meta[3:8, :] = jnp.zeros((5, 128), F32)

    bar = pltpu.get_barrier_semaphore()
    for k in range(1, 16):
        pl.semaphore_signal(bar, inc=1, device_id=p.speer(k), device_id_type=MESH)
    for k in range(1, 8):
        pl.semaphore_signal(bar, inc=1, device_id=p.dpeer(k), device_id_type=MESH)
    pl.semaphore_signal(bar, inc=1, device_id=p.xring(2), device_id_type=MESH)
    pl.semaphore_wait(bar, 23)

    class Shards:
        def __init__(self, buf, i_share):
            self.buf, self.share = buf, i_share
            self.iy, self.ix = m.take(3) - 1, m.take(1)

        def row(self, k, xl):
            return rem(p.y - k + 4, 4) * 2 + xl

        def quarter(self, t):
            return pl.ds(pl.multiple_of(p.c * 64 + (t - 1) * 32, 32), 32)

        def along_y(self):
            s = self.buf.at[p.dp, half]
            for k in (2, 1, 3):
                m.send(s, s, self.iy + k, p.ypeer(k))

        def along_x(self, k):
            d = self.row(k, p.xl)
            if k:
                m.got(self.buf.at[d, half], self.iy + k)
            for t in (1, 2):
                s = self.buf.at[d, self.quarter(t)]
                m.part(s, s, self.ix, p.xring(t))

        def to_core(self):
            m.whole(self.buf.at[0:4, half], self.ix)
            m.got(self.buf.at[0:4, half], self.ix)
            s = self.buf.at[:, half]
            m.send(s, s, self.share, p.sib())

        def done(self):
            m.got(self.buf.at[:, other], self.share)

    class Down:
        def __init__(self, i_share):
            self.share = i_share
            self.iy, self.ix = m.take(3) - 1, m.take(1)

        def start(self, d, t, i, dev):
            where, more = down_pieces(d)
            for n in range(3):
                rows = h32 if t == 0 else pl.ds(pl.multiple_of(c32 + (t - 1) * 16, 16), 16)
                s = r.wd_v.at[where[n][1], rows]
                if n < 2:
                    m.part(s, s, i, dev)
                else:

                    @pl.when(more)
                    def _():
                        m.part(s, s, i, dev)

        def wait(self, d, act):
            _, more = down_pieces(d)

            @pl.when(more)
            def _():
                act(r.wd_v.at[0:3, h32])

            @pl.when(jnp.logical_not(more))
            def _():
                act(r.wd_v.at[0:2, h32])

        def along_y(self):
            for k in (2, 1, 3):
                self.start(p.dp, 0, self.iy + k, p.ypeer(k))

        def along_x(self, k):
            d = rem(p.y - k + 4, 4) * 2 + p.xl
            if k:
                self.wait(d, lambda ref: m.got(ref, self.iy + k))
            for t in (1, 2):
                self.start(d, t, self.ix, p.xring(t))

        def to_core(self):
            m.whole(r.wd_v.at[0:9, h32], self.ix)
            m.got(r.wd_v.at[0:9, h32], self.ix)
            m.send(r.wd_v.at[:, h32], r.wd_v.at[:, h32], self.share, p.sib())

        def done(self):
            m.got(r.wd_v.at[:, o32], self.share)

        def finish(self):
            for k in (1, 2, 3):
                self.wait(p.dp, lambda ref: m.copy(ref, ref, self.iy + k, p.sib()).wait_send())

    i_share = m.take(5)
    w_qkv = Shards(r.wqkv, i_share)
    w_o = Shards(r.wo_v, i_share + 1)
    w_d = Down(i_share + 2)
    w_g = Shards(r.wg_v, i_share + 3)
    w_u = Shards(r.wu_v, i_share + 4)
    i_tok = m.take(3) - 1
    for dz in (2, 1, 3):
        m.send(r.tok, r.tok_all.at[dz], i_tok + dz, p.zpeer(dz))
    m.local(r.wqkv.at[0, half], r.wqkv.at[0, half], i_loc).wait()
    w_qkv.along_y()
    w_qkv.along_x(0)
    i_mseq = m.take()
    for k in range(1, 16):
        m.part(r.meta, r.mseq.at[p.sq], i_mseq, p.speer(k))
    m.whole(r.mseq.at[0:15], i_mseq)
    i_mdp = m.take()
    for k in range(1, 8):
        m.part(r.meta, r.mdp.at[p.dp], i_mdp, p.dpeer(k))
    m.whole(r.mdp.at[0:7], i_mdp)
    r.mseq[p.sq] = r.meta[...]
    r.mdp[p.dp] = r.meta[...]
    for k in (1, 3, 2):
        w_qkv.along_x(k)
    m.local(r.wo_v.at[0, half], r.wo_v.at[0, half], i_loc + 1).wait()
    w_o.along_y()
    for n in range(2):
        down_local(n).wait()

    @pl.when(has_extra)
    def _():
        down_local(2).wait()

    w_d.along_y()

    m.got(r.mseq.at[0:15], i_mseq)
    r.st[...] = seg_rows(r.mseq[:, 2, :])
    m.got(r.mdp.at[0:7], i_mdp)
    gain1 = jnp.concatenate([r.mdp[j, 0:1, :] for j in range(8)], axis=1)
    gain2 = jnp.concatenate([r.mdp[j, 1:2, :] for j in range(8)], axis=1)
    w_qkv.to_core()
    m.local(r.wg_v.at[0, half], r.wg_v.at[0, half], i_loc + 2).wait()
    w_g.along_y()
    m.local(r.wu_v.at[0, half], r.wu_v.at[0, half], i_loc + 3).wait()
    w_u.along_y()

    lanesign = jnp.where(lane_half(), -1.0, 1.0)
    freq = r.freq[...]
    for dz in range(4):
        i = 4 * z_of(dz) + p.g
        row = r.st[pl.ds(i, 1), :]
        pos = (lax.broadcasted_iota(jnp.int32, (1, 128), 1) + i * 128).astype(F32) - row
        ang = jnp.transpose(jnp.broadcast_to(pos, (128, 128))) * freq
        r.cosr[dz] = jnp.cos(ang)
        r.sinr[dz] = jnp.sin(ang) * lanesign
    w_qkv.done()

    wfull = r.wqkv[...].reshape(1024, 512)
    qg = jnp.concatenate([r.gq[...].astype(F32)] * 2, axis=1)
    kg = jnp.concatenate([r.gk[...].astype(F32)] * 2, axis=1)
    i_kv = m.take()
    i_kvx = m.take(4)
    i_kvf = m.take()

    def project(dz, x):
        x = x.astype(F32)
        r1 = lax.rsqrt(jnp.mean(x * x, axis=1, keepdims=True) + EPS)
        h = (x * r1 * gain1).astype(BF)
        r.tok_all[dz] = h
        o = dot(h, wfull)
        cs, sn = r.cosr[dz], r.sinr[dz]
        r.qk_raw[dz] = o[:, 0:384]
        rot = []
        for b, gn in ((0, qg), (1, qg), (2, kg)):
            v = o[:, b * 128:(b + 1) * 128]
            v = v * lax.rsqrt(head_mean(v * v) + EPS) * gn
            rot.append(v * cs + swap_halves(v) * sn)
        for hd, v in enumerate(spread_heads(rot[0], rot[1])):
            r.qz[dz, pl.ds(hd * 128, 128), :] = v.astype(BF)
        i = 4 * z_of(dz) + p.g
        r.kv[i, :, 0:128] = rot[2].astype(BF)
        r.kv[i, :, 128:256] = o[:, 384:512].astype(BF)
        m.send(r.kv.at[i], r.kv.at[i], i_kvx + dz, p.xpeer())
        m.part(r.kv.at[i], r.kv.at[i], i_kv, p.sib())

    project(0, r.tok[...])
    for k in (0, 1, 3, 2):
        w_o.along_x(k)
    for dz in (1, 3, 2):
        m.got(r.tok_all.at[dz], i_tok + dz)
        project(dz, r.tok_all[dz])
    i_cot = m.take()
    for dz in (1, 3, 2):
        m.part(r.cot, r.cot_all.at[dz], i_cot, p.zpeer(dz))
    m.whole(r.cot_all.at[1:4], i_cot)
    r.cot_all[0] = r.cot[...]
    for k in (0, 1, 3, 2):
        w_d.along_x(k)
    gs = p.g + 1 - 2 * p.c
    gx = (1 - p.xh) * 2 + p.c
    gxs = (1 - p.xh) * 2 + 1 - p.c
    for dz in (0, 1, 3, 2):
        zz = 4 * z_of(dz)
        m.got(r.kv.at[zz + gx], i_kvx + dz)
        m.part(r.kv.at[zz + gx], r.kv.at[zz + gx], i_kvf, p.sib())
    four = r.kv.at[0:4]
    for i in (i_kv, i_kvf):
        m.whole(four, i)
        m.got(four, i)

    def turn(first):
        def one(j, carry):
            t = jnp.transpose(r.kv[j, :, first:first + 128].astype(F32))
            r.kvt[:, pl.ds(pl.multiple_of(j * 128, 128), 128)] = t.astype(BF)
            return carry

        lax.fori_loop(0, 16, one, 0)

    turn(128)
    for k in (0, 1, 3, 2):
        w_g.along_x(k)
    w_o.to_core()

    def allowed_rows(i):
        row = r.st[pl.ds(i, 1), :].astype(jnp.int32)
        qi = lax.broadcasted_iota(jnp.int32, (1, 128), 1) + i * 128
        return jnp.concatenate([row] * 4, axis=1), jnp.concatenate([qi] * 4, axis=1)

    def window(i):
        return jnp.minimum(jnp.maximum(i - 8, 0), 7)

    def weights_of(kb, qv, row4, qi4):
        s = dot(r.kv[pl.ds(kb, 3), :, 0:128].reshape(384, 128), qv, NT)
        ki = lax.broadcasted_iota(jnp.int32, (384, 512), 0) + kb * 128
        return jnp.where((ki >= row4) & (ki <= qi4), jnp.exp2(s * (SCALE * LOG2E)), 0.0)

    def keys_turned(k0):
        return r.kvt[:, pl.ds(pl.multiple_of(k0 * 128, 128), 1152)]

    def heads_down(o):
        return jnp.concatenate(
            [o[(h // 2) * 64:(h // 2) * 64 + 64, h * 128:(h + 1) * 128] for h in range(4)], axis=0
        )

    def forward_chunk(dz):
        i = 4 * z_of(dz) + p.g
        k0 = window(i)
        row4, qi4 = allowed_rows(i)
        qv = r.qz[dz]
        total = jnp.zeros((8, 512), F32)
        for t in range(3):
            w = weights_of(k0 + 3 * t, qv, row4, qi4)
            total = total + jnp.sum(w.reshape(48, 8, 512), axis=0)
            r.pT[t * 384:(t + 1) * 384] = w.astype(BF)
        il = 1.0 / jnp.sum(total, axis=0, keepdims=True)
        r.invl[dz] = jnp.broadcast_to(il, (8, 512))
        full = heads_down(dot(keys_turned(k0), r.pT[...]) * il)
        r.oT[dz] = full
        r.o_s[dz] = jnp.transpose(full).astype(BF)

    i_o = m.take()
    for j in range(4):
        dz = (j + 1) % 4
        forward_chunk(dz)
        if dz:
            m.part(r.o_s.at[dz], r.o_in.at[p.z], i_o, p.zpeer(-dz))
        else:
            r.o_in[p.z] = r.o_s[0]
        if j == 1:
            for k in (0, 1, 3, 2):
                w_u.along_x(k)
            w_d.to_core()
    m.whole(r.o_in.at[0:3], i_o)

    w_g.to_core()
    m.got(r.o_in.at[0:3], i_o)
    for j in range(4):
        r.o_own[:, j * 256:(j + 1) * 256] = r.o_in[j]
    w_o.done()
    x0 = r.tok[...].astype(F32)
    middle = x0 + dot(r.o_own[...], r.wo_v[...].reshape(1024, 1024))
    r.mid[...] = middle
    r2 = lax.rsqrt(jnp.mean(middle * middle, axis=1, keepdims=True) + EPS)
    r.h2[0] = (middle * r2 * gain2).astype(BF)
    i_h2 = m.take(3) - 1
    for dz in (2, 1, 3):
        m.send(r.h2.at[0], r.h2.at[dz], i_h2 + dz, p.zpeer(dz))
    i_of = m.take()
    for dz in (2, 1, 3):
        m.part(r.o_own, r.o_full.at[dz], i_of, p.zpeer(dz))
    m.whole(r.o_full.at[1:4], i_of)
    r.o_full[0] = r.o_own[...]

    turn(0)
    w_u.to_core()
    m.got(r.cot_all.at[1:4], i_cot)
    w_d.done()
    wd = r.wd_v[...].reshape(1152, 1024)
    cots = r.cot_all[...].reshape(512, 1024)

    def cols384(t):
        return pl.ds(pl.multiple_of(t * 384, 128), 384)

    def dm_tile(t, carry):
        w = r.wd_v[pl.ds(t * 6, 6)].reshape(384, 1024)
        r.dm[:, :, cols384(t)] = dot(cots, w, NT).astype(BF).reshape(4, 128, 384)
        return carry

    lax.fori_loop(0, 3, dm_tile, 0)
    w_g.done()
    w_u.done()

    i_p2 = m.take()
    for pair in range(2):
        two = slice(2 * pair, 2 * pair + 2)
        for dz in ((1,), (2, 3))[pair]:
            m.got(r.h2.at[dz], i_h2 + dz)
        hh = r.h2[two].reshape(256, 1024)

        def ffn_tile(t, carry):
            cols = cols384(t)
            gate = dot(hh, r.wg_v[:, :, cols].reshape(1024, 384))
            up = dot(hh, r.wu_v[:, :, cols].reshape(1024, 384))
            sig = 1.0 / (1.0 + jnp.exp(-gate))
            act = gate * sig
            dmt = r.dm[two, :, cols].astype(F32).reshape(256, 384)
            r.mixed[two, :, cols] = (act * up).astype(BF).reshape(2, 128, 384)
            r.dg[two, :, cols] = (dmt * up * sig * (1.0 + gate * (1.0 - sig))).astype(BF).reshape(2, 128, 384)
            r.du[two, :, cols] = (dmt * act).astype(BF).reshape(2, 128, 384)
            return carry

        lax.fori_loop(0, 3, ffn_tile, 0)

    i_r1 = m.take(4)
    h2t = r.h2[...].reshape(512, 1024)

    def gate_tile(t, carry):
        w = r.dg[:, :, cols384(t)].reshape(512, 384)
        r.gF[:, :, :, cols384(t)] = dot(h2t, w, TN).astype(BF).reshape(4, 2, 128, 384)
        return carry

    def up_tile(t, carry):
        w = r.du[:, :, cols384(t)].reshape(512, 384)
        r.gF[:, :, :, cols384(t + 3)] = dot(h2t, w, TN).astype(BF).reshape(4, 2, 128, 384)
        return carry

    lax.fori_loop(0, 3, gate_tile, 0)
    m.send(r.gF.at[:, :, other, 0:1152], r.r1F.at[:, :, :, 0:1152], i_r1, p.sib())
    lax.fori_loop(0, 3, up_tile, 0)
    m.send(r.gF.at[:, :, other, 1152:2304], r.r1F.at[:, :, :, 1152:2304], i_r1 + 3, p.sib())
    for pair in (1, 0):
        two = slice(2 * pair, 2 * pair + 2)
        part = dot(r.dg[two].reshape(256, 1152), r.wg_v[...].reshape(1024, 1152), NT)
        part += dot(r.du[two].reshape(256, 1152), r.wu_v[...].reshape(1024, 1152), NT)
        if pair:
            r.p2s[1] = part[0:128].astype(BF)
            m.part(r.p2s.at[1], r.p2r.at[1], i_p2, p.zpeer(-2))
            r.p2s[2] = part[128:256].astype(BF)
            m.part(r.p2s.at[2], r.p2r.at[2], i_p2, p.zpeer(-3))
        else:
            r.p2s[0] = part[128:256].astype(BF)
            m.part(r.p2s.at[0], r.p2r.at[0], i_p2, p.zpeer(-1))
            r.own[...] = part[0:128]

    def down_tile(t, carry):
        w = r.mixed[:, :, cols384(t)].reshape(512, 384)
        r.gD[pl.ds(t * 6, 6)] = dot(w, cots, TN).astype(BF).reshape(6, 64, 1024)
        return carry

    lax.fori_loop(0, 3, down_tile, 0)
    m.send(r.gD.at[:, o32], r.r1D, i_r1 + 1, p.sib())

    m.got(r.r1F.at[:, :, :, 0:1152], i_r1)
    m.got(r.r1F.at[:, :, :, 1152:2304], i_r1 + 3)

    def add_core(d, carry):
        a, b = lax.div(d, 2), rem(d, 2)
        r.r1F[a, b] = (r.r1F[a, b].astype(F32) + r.gF[a, b, half].astype(F32)).astype(BF)
        return carry

    lax.fori_loop(0, 8, add_core, 0)

    def rows_of(x, n):
        return pl.ds(pl.multiple_of(x * n, n), n)

    class XFirst:
        def __init__(self, src, mid1, tot, mid2):
            self.src, self.mid1, self.tot, self.mid2 = src, mid1, tot, mid2
            self.i1, self.i2 = m.take(), m.take()

        def one(self):
            for t in (3, 1, 2):
                m.part(self.src(t), self.mid1.at[t - 1], self.i1, p.xring(t))
            m.whole(self.mid1, self.i1)

        def two(self):
            m.got(self.mid1, self.i1)

            def add(n, carry):
                v = self.src(0).at[n][...].astype(F32)
                for t in range(3):
                    v = v + self.mid1[t, n].astype(F32)
                self.tot[n] = v.astype(BF)
                return carry

            lax.fori_loop(0, 4, add, 0)
            for k in (2, 1, 3):
                m.part(self.tot.at[rem(p.y + k, 4)], self.mid2.at[k - 1], self.i2, p.ypeer(k))
            m.whole(self.mid2, self.i2)

        def sum(self):
            m.got(self.mid2, self.i2)
            v = self.tot[p.y].astype(F32)
            for k in range(3):
                v = v + self.mid2[k].astype(F32)
            return v.astype(BF)

    class YFirst:
        def __init__(self, src, part, mid1, tot, mid2):
            self.src, self.part, self.mid1, self.tot, self.mid2 = src, part, mid1, tot, mid2
            self.i1, self.i2 = m.take(), m.take()

        def one(self):
            for k in (2, 1, 3):
                m.part(self.src(rem(p.y + k, 4)), self.mid1.at[k - 1], self.i1, p.ypeer(k))
            m.whole(self.mid1, self.i1)

        def two(self):
            m.got(self.mid1, self.i1)

            def add(n, carry):
                v = self.src(p.y).at[n][...].astype(F32)
                for k in range(3):
                    v = v + self.mid1[k, n].astype(F32)
                self.tot[n] = v.astype(BF)
                return carry

            lax.fori_loop(0, 2, add, 0)
            for t in (3, 1, 2):
                m.part(self.part(self.tot, t), self.mid2.at[t - 1], self.i2, p.xring(t))
            m.whole(self.mid2, self.i2)

        def sum(self):
            m.got(self.mid2, self.i2)
            v = self.part(self.tot, 0)[...].astype(F32)
            for t in range(3):
                v = v + self.mid2[t].astype(F32)
            return v.astype(BF)

    def rows_x(buf, c0, c1):
        return lambda t: buf.at[:, p.xplace(t)[0], rows_of(p.xplace(t)[1], 32), c0:c1]

    def rows_y(buf, c0, c1):
        return lambda y: buf.at[y, :, :, c0:c1]

    def part_y(tot, t):
        xl, xh = p.xplace(t)
        return tot.at[xl, rows_of(xh, 32)]

    def part_d(tot, t):
        xl, xh = p.xplace(t)
        return tot.at[xl, :, rows_of(xh, 16)]

    sums = [
        XFirst(rows_x(r.r1F, 0, 1152), r.ax, r.at, r.ay),
        YFirst(rows_y(r.r1F, 1152, 2304), part_y, r.by, r.bt, r.bx),
        XFirst(
            lambda t: r.sD.at[:, p.xplace(t)[0], :, rows_of(p.xplace(t)[1], 16), 0:512], r.adx, r.adt, r.ady
        ),
        YFirst(lambda y: r.sD.at[y, :, :, :, 512:1024], part_d, r.bdy, r.bdt, r.bdx),
    ]
    for e in sums[0:2]:
        e.one()
    r.own3[...] = dot(r.mixed[0], wd)

    def out_chunk(dz, carry):
        r.p3s[dz - 1] = dot(r.mixed[dz], wd).astype(BF)
        return carry

    lax.fori_loop(1, 4, out_chunk, 0)
    m.got(r.r1D, i_r1 + 1)

    def add_core_down(d, carry):
        a, b = lax.div(d, 2), rem(d, 2)
        where, more = down_pieces(d)
        for n in range(2):
            t = where[n][1]
            r.sD[a, b, n] = (r.r1D[t].astype(F32) + r.gD[t, h32].astype(F32)).astype(BF)

        @pl.when(more)
        def _():
            t = where[2][1]
            r.sX[b] = (r.r1D[t].astype(F32) + r.gD[t, h32].astype(F32)).astype(BF)

        return carry

    lax.fori_loop(0, 8, add_core_down, 0)
    for e in sums[2:4]:
        e.one()
    i_x1 = m.take()
    i_x2 = m.take()
    for t in (3, 1, 2):
        xl, xh = p.xplace(t)
        m.part(r.sX.at[xl, rows_of(xh, 16)], r.xx.at[t - 1], i_x1, p.xring(t))
    m.whole(r.xx, i_x1)

    m.whole(r.p2s, i_p2)
    m.got(r.p2r, i_p2)
    dh2 = r.own[...] + r.p2r[0].astype(F32) + r.p2r[1].astype(F32) + r.p2r[2].astype(F32)
    middle = r.mid[...]
    r2 = lax.rsqrt(jnp.mean(middle * middle, axis=1, keepdims=True) + EPS)
    small2 = jnp.sum(dh2 * middle * r2, axis=0, keepdims=True)
    wdh = dh2 * gain2
    dmid = r.cot[...].astype(F32) + r2 * wdh - middle * (r2 * r2 * r2) * jnp.mean(wdh * middle, axis=1, keepdims=True)
    r.dmid[...] = dmid
    r.da[...] = dmid.astype(BF)
    i_do = m.take()

    def zcols(z):
        return pl.ds(pl.multiple_of(z * 256, 256), 256)

    for dz in (2, 1, 3, 0):
        zz = rem(p.z + dz, 4)
        w = r.wo_v[pl.ds(2 * zz, 2)].reshape(256, 1024)
        r.dob[:, zcols(zz)] = dot(r.da[...], w, NT).astype(BF)
        if dz:
            m.part(r.dob.at[:, zcols(zz)], r.do_all.at[dz], i_do, p.zpeer(dz))
    m.whole(r.do_all.at[1:4], i_do)
    r.do_all[0] = r.dob[:, zq]
    i_p3 = m.take()
    i_dc = m.take()
    for dz in (2, 1, 3):
        m.part(r.da.at[:, zcols(rem(p.z + dz, 4))], r.da_c.at[dz], i_dc, p.zpeer(dz))
    m.whole(r.da_c.at[1:4], i_dc)
    for dz in (2, 1, 3):
        m.part(r.p3s.at[dz - 1], r.p3r.at[dz - 1], i_p3, p.zpeer(-dz))
    m.whole(r.p3s, i_p3)
    r.da_c[0] = r.da[:, zq]

    r.dkv[...] = jnp.zeros_like(r.dkv)
    m.got(r.do_all.at[1:4], i_do)
    for e in sums[0:2]:
        e.two()

    lane = lax.broadcasted_iota(jnp.int32, (1, 256), 1)
    kscale = jnp.where(lane < 128, SCALE, 1.0)
    i_dkv = m.take()
    xs = (p.dp, p.z * 4 + gxs)

    def backward_chunk(j, carry):
        zz = 3 - j
        dz = rem(p.z - zz + 4, 4)
        i = 4 * zz + p.g
        row4, qi4 = allowed_rows(i)
        do = r.do_all[dz].astype(F32)
        for hd, v in enumerate(spread_heads(do[:, 0:128], do[:, 128:256])):
            r.doz[pl.ds(hd * 128, 128), :] = v.astype(BF)
        prod = jnp.transpose(do) * r.oT[dz]
        drow = jnp.concatenate(
            [jnp.sum(prod[h * 64:(h + 1) * 64], axis=0, keepdims=True) for h in range(4)], axis=1
        )
        il = r.invl[dz, 0:1, :]
        qv = r.qz[dz]
        dov = r.doz[...]
        k0 = window(i)
        for t in range(3):
            rows = slice(t * 384, (t + 1) * 384)
            w = weights_of(k0 + 3 * t, qv, row4, qi4) * il
            r.pT[rows] = w.astype(BF)
            dp = dot(r.kv[pl.ds(k0 + 3 * t, 3), :, 128:256].reshape(384, 128), dov, NT)
            r.dsT[rows] = (w * (dp - drow)).astype(BF)
        nine = pl.ds(k0, 9)
        r.dkv[nine, :, 0:128] += dot(r.dsT[...], qv).reshape(9, 128, 128)
        r.dkv[nine, :, 128:256] += dot(r.pT[...], dov).reshape(9, 128, 128)
        r.dkvb[zz] = (r.dkv[pl.ds(4 * zz, 4)] * kscale.reshape(1, 1, 256)).astype(BF)
        m.part(r.dkvb.at[zz, gx], r.dkvr.at[1, zz], i_dkv, p.xpeer())
        m.part(r.dkvb.at[zz, gxs], r.dkvr.at[2, zz], i_dkv, xs)
        m.part(r.dkvb.at[zz, gs], r.dkvr.at[0, zz], i_dkv, p.sib())
        r.dqr[dz] = jnp.transpose(heads_down(dot(keys_turned(k0), r.dsT[...]) * SCALE))
        return carry

    lax.fori_loop(0, 4, backward_chunk, 0)

    m.whole(r.dkvr, i_dkv)

    for e in sums[2:4]:
        e.two()
    m.got(r.xx, i_x1)
    v = r.sX[p.xl, rows_of(p.xh, 16)].astype(F32)
    for t in range(3):
        v = v + r.xx[t].astype(F32)
    r.xt[...] = v.astype(BF)
    kz = rem(p.z - p.y + 4, 4)

    @pl.when(kz != 0)
    def _():
        m.part(r.xt, r.xy.at[kz - 1], i_x2, (p.z * 2 + p.xl, p.sq))

    r.oF[:, 0:1152] = sums[0].sum()
    r.oF[:, 1152:2304] = sums[1].sum()

    def seq_at(z, g):
        return rem(z + 8, 4) * 4 + g

    class Gather:
        def __init__(self, own, buf, order):
            self.own, self.buf, self.order = own, buf, order
            self.il, self.ix, self.iz, self.ic = m.take(), m.take(), m.take(), m.take()

        def on(self, src, s, where):
            if "x" in where:
                m.part(src, s, self.ix, p.xpeer())
            if "z" in where:
                for dz in (2, 1, 3):
                    m.part(src, s, self.iz, p.zpeer(dz))
            if "b" in where:
                for dz in (2, 1, 3):
                    m.part(src, s, self.iz, (p.dp, seq_at(p.z + dz, gx)))
            if "c" in where:
                m.part(src, s, self.ic, p.sib())

        def got(self, n, i):
            m.got(self.buf.at[0:n], i)

        def slot(self, dz, g):
            return self.buf.at[seq_at(p.z - dz, g)]

        def first(self):
            m.local(self.own, self.slot(0, p.g), self.il).start()
            self.on(self.own, self.slot(0, p.g), "zxcb" if self.order == "zx" else "zxc")

        def second(self):
            if self.order == "x":
                self.got(1, self.ix)
                s = self.slot(0, gx)
                self.on(s, s, "zc")
            elif self.order == "z":
                self.got(3, self.iz)
                for dz in (1, 2, 3):
                    s = self.slot(dz, p.g)
                    self.on(s, s, "xc")
            else:
                self.got(1, self.ix)
                self.got(6, self.iz)
                for dz in range(4):
                    for g in (p.g, gx)[dz == 0:]:
                        s = self.slot(dz, g)
                        self.on(s, s, "c")

        def third(self):
            if self.order == "x":
                self.got(6, self.iz)
                for dz in (1, 2, 3):
                    for g in (p.g, gx):
                        s = self.slot(dz, g)
                        self.on(s, s, "c")
            elif self.order == "z":
                self.got(4, self.ix)
                for dz in range(4):
                    s = self.slot(dz, gx)
                    self.on(s, s, "c")

        def last(self):
            n = {"x": (1, 6), "z": (4, 3), "zx": (1, 6)}[self.order]
            m.whole(self.buf.at[0:n[0]], self.ix)
            m.whole(self.buf.at[0:n[1]], self.iz)
            m.whole(self.buf.at[0:8], self.ic)
            self.got(8, self.ic)
            m.local(self.own, self.slot(0, p.g), self.il).wait()

    ag_f = Gather(r.oF, r.fF, "z")
    ag_d = Gather(r.oD, r.fD, "x")
    ag_a = Gather(r.oA, r.fA, "zx")
    ag_f.first()

    m.got(r.o_full.at[1:4], i_of)
    m.got(r.da_c.at[1:4], i_dc)
    m.got(r.p3r, i_p3)
    r.gA[:, :, :, 512:768] = dot(
        r.o_full[...].reshape(512, 1024), r.da_c[...].reshape(512, 256), TN
    ).astype(BF).reshape(4, 2, 128, 256)
    r.block_out[...] = (
        r.mid[...] + r.own3[...] + r.p3r[0].astype(F32) + r.p3r[1].astype(F32) + r.p3r[2].astype(F32)
    ).astype(BF)

    m.got(r.dkvr, i_dkv)
    sq_acc = jnp.zeros((1, 128), F32)
    sk_acc = jnp.zeros((1, 128), F32)
    for dz in range(4):
        zz = z_of(dz)
        i = 4 * zz + p.g
        dkv = r.dkv[i] * kscale
        for n in range(3):
            dkv = dkv + r.dkvr[n, zz].astype(F32)
        cs, sn = r.cosr[dz], r.sinr[dz]
        grads = (r.dqr[dz, :, 0:128], r.dqr[dz, :, 128:256], dkv[:, 0:128])
        for b, gr in enumerate(grads):
            gn = qg if b < 2 else kg
            v = r.qk_raw[dz, :, b * 128:(b + 1) * 128]
            f = lax.rsqrt(head_mean(v * v) + EPS)
            dn = gr * cs - swap_halves(gr) * sn
            add = jnp.sum(dn * v * f, axis=0, keepdims=True)
            if b < 2:
                sq_acc = sq_acc + add
            else:
                sk_acc = sk_acc + add
            wn = dn * gn
            r.dqkv[dz, :, b * 128:(b + 1) * 128] = (f * wn - v * (f * f * f) * head_mean(wn * v)).astype(BF)
        r.dqkv[dz, :, 384:512] = dkv[:, 128:256].astype(BF)
    i_p4 = m.take()
    m.flush(i_p2)
    for dz in (2, 1, 3):
        r.p2s[dz - 1] = dot(r.dqkv[dz], r.wqkv[...].reshape(1024, 512), NT).astype(BF)
        m.part(r.p2s.at[dz - 1], r.p4r.at[dz - 1], i_p4, p.zpeer(-dz))
    m.whole(r.p2s, i_p4)
    r.own[...] = dot(r.dqkv[0], r.wqkv[...].reshape(1024, 512), NT)
    r.gA[:, :, :, 0:512] = dot(
        r.tok_all[...].reshape(512, 1024), r.dqkv[...].reshape(512, 512), TN
    ).astype(BF).reshape(4, 2, 128, 512)
    m.send(r.gA.at[:, :, other], r.r1A, i_r1 + 2, p.sib())
    r.oD[0:2, :, 0:512] = sums[2].sum()
    r.oD[0:2, :, 512:1024] = sums[3].sum()

    @pl.when(kz == 0)
    def _():
        v = r.xt[...].astype(F32)
        m.got(r.xy, i_x2)
        for k in range(3):
            v = v + r.xy[k].astype(F32)
        r.oD[2] = v.astype(BF)

    @pl.when(kz != 0)
    def _():
        r.oD[2] = jnp.zeros((16, 1024), BF)

    ag_d.first()
    m.got(r.r1A, i_r1 + 2)
    r.r1A[...] = (r.r1A[...].astype(F32) + r.gA[:, :, half].astype(F32)).astype(BF)
    sums_a = [
        XFirst(rows_x(r.r1A, 0, 384), r.qax, r.qat, r.qay),
        YFirst(rows_y(r.r1A, 384, 768), part_y, r.qby, r.qbt, r.qbx),
    ]
    for e in sums_a:
        e.one()
    ag_f.second()
    ag_d.second()
    for e in sums_a:
        e.two()

    m.got(r.p4r, i_p4)
    dh = r.own[...] + r.p4r[0].astype(F32) + r.p4r[1].astype(F32) + r.p4r[2].astype(F32)
    x0 = r.tok[...].astype(F32)
    r1 = lax.rsqrt(jnp.mean(x0 * x0, axis=1, keepdims=True) + EPS)
    small1 = jnp.sum(dh * x0 * r1, axis=0, keepdims=True)
    wdh = dh * gain1
    r.input_grad[...] = (
        r.dmid[...] + r1 * wdh - x0 * (r1 * r1 * r1) * jnp.mean(wdh * x0, axis=1, keepdims=True)
    ).astype(BF)

    both = lambda v: v + pltpu.roll(v, 64, 1)
    for d in range(8):
        cols = slice(d * 128, (d + 1) * 128)
        r.gsm[d] = jnp.concatenate(
            [small1[:, cols], small2[:, cols], both(sq_acc), both(sk_acc), jnp.zeros((4, 128), F32)], axis=0
        )
    i_s1 = m.take()
    i_s2 = m.take()
    for k in range(1, 8):
        m.part(r.gsm.at[rem(p.dp + k, 8)], r.gs1.at[k], i_s1, p.dpeer(k))
    m.whole(r.gs1.at[1:8], i_s1)
    r.gs1[0] = r.gsm[p.dp]
    r.oA[:, 0:384] = sums_a[0].sum()
    r.oA[:, 384:768] = sums_a[1].sum()
    ag_a.first()
    ag_f.third()
    m.got(r.gs1.at[1:8], i_s1)
    r.gs1s[...] = jnp.sum(r.gs1[...], axis=0)
    for k in range(1, 16):
        m.part(r.gs1s, r.gs2.at[k], i_s2, p.speer(k))
    m.whole(r.gs2.at[1:16], i_s2)
    r.gs2[0] = r.gs1s[...]
    ag_d.third()
    ag_a.second()
    m.got(r.gs2.at[1:16], i_s2)
    r.g_small[...] = jnp.sum(r.gs2[...], axis=0)
    ag_f.last()
    ag_d.last()
    ag_a.last()

    m.finish()
    w_d.finish()

    @pl.when(kz != 0)
    def _():
        m.copy(r.xt, r.xt, i_x2, p.sib()).wait_send()

    assert m.n <= NSEM, m.n


def block(args):
    vm = pl.BlockSpec(memory_space=pltpu.VMEM)
    hb = pl.BlockSpec(memory_space=pl.ANY)
    return pl.pallas_call(
        kernel,
        out_shape=tuple(jax.ShapeDtypeStruct(s, d) for s, d in OUTPUTS.values()),
        in_specs=[vm] * 7 + [hb] * 7 + [vm],
        out_specs=tuple(hb if name[0] == "f" else vm for name in OUTPUTS),
        scratch_shapes=[pltpu.VMEM(s, d) for s, d in SCRATCH.values()]
        + [pltpu.SemaphoreType.DMA((NSEM,)), pltpu.SemaphoreType.DMA((NSEM,))],
        compiler_params=pltpu.CompilerParams(
            collective_id=0, has_side_effects=True, vmem_limit_bytes=63 * 2**20
        ),
        name="block",
    )(*args)


PLACED = {
    "g_gate": (128, 4608),
    "g_up": (128, 4608),
    "g_down": (576, 1024),
    "g_q": (128, 1024),
    "g_k": (128, 512),
    "g_v": (128, 512),
    "g_out": (128, 1024),
}

LAID = {
    "block_out": ((128, 1024), BF),
    "input_grad": ((128, 1024), BF),
    "g_attn": ((1, 128), F32),
    "g_ffn": ((1, 128), F32),
    "g_qg": ((1, 64), F32),
    "g_kg": ((1, 64), F32),
    **{name: (shape, F32) for name, shape in PLACED.items()},
}


def lay_kernel(f_f, f_d, f_a, b_o, i_g, sm, *refs):
    outs = dict(zip(LAID, refs[:len(LAID)]))
    v_f, v_d, v_a = refs[len(LAID):len(LAID) + 3]
    stage = dict(zip(PLACED, refs[len(LAID) + 3:len(LAID) + 3 + len(PLACED)]))
    isem, osem = refs[len(LAID) + 3 + len(PLACED):]
    p = Place()
    ins = [
        pltpu.make_async_copy(f_f.at[:, :, 0:1152], v_f.at[:, :, 0:1152], isem.at[0]),
        pltpu.make_async_copy(f_f.at[:, :, 1152:2304], v_f.at[:, :, 1152:2304], isem.at[3]),
        pltpu.make_async_copy(f_d, v_d, isem.at[1]),
        pltpu.make_async_copy(f_a, v_a, isem.at[2]),
    ]
    for q in ins:
        q.start()
    outs["block_out"][...] = b_o[...]
    outs["input_grad"][...] = i_g[...]
    outs["g_attn"][...] = sm[0:1, :]
    outs["g_ffn"][...] = sm[1:2, :]
    outs["g_qg"][...] = sm[2:3, 0:64]
    outs["g_kg"][...] = sm[3:4, 0:64]

    def place(name):
        n = list(PLACED).index(name)
        return pltpu.make_async_copy(stage[name], outs[name], osem.at[n])

    def row_of(s):
        g = rem(s, 4)
        return pl.ds(pl.multiple_of(rem(g, 2) * 64 + lax.div(g, 2) * 32, 32), 32)

    for name, base, q in (("g_gate", 0, ins[0]), ("g_up", 1152, ins[1])):
        q.wait()

        def lay(g, carry):
            row = row_of(g)
            for z in range(4):
                for t in range(9):
                    cols = slice(t * 512 + z * 128, t * 512 + z * 128 + 128)
                    v = v_f[4 * z + g, :, base + t * 128:base + (t + 1) * 128]
                    stage[name][row, cols] = v.astype(F32)
            n = list(PLACED).index(name)
            pltpu.make_async_copy(stage[name].at[row], outs[name].at[row], osem.at[n]).start()
            return carry

        lax.fori_loop(0, 4, lay, 0)
    ins[2].wait()

    def lay_down(s, carry):
        z = lax.div(s, 4)
        g = rem(s, 4)
        sub = rem(g, 2) * 32 + lax.div(g, 2) * 16
        for n in range(2):
            u = rem(2 * z + n - p.dp + 8, 8)
            stage["g_down"][pl.ds(pl.multiple_of(u * 64 + sub, 16), 16), :] = v_d[s, n].astype(F32)

        @pl.when(lax.div(p.dp, 2) == z)
        def _():
            stage["g_down"][pl.ds(pl.multiple_of(8 * 64 + sub, 16), 16), :] = v_d[s, 2].astype(F32)

        return carry

    lax.fori_loop(0, 16, lay_down, 0)
    place("g_down").start()
    ins[3].wait()

    def lay_attn(s, carry):
        z = lax.div(s, 4)
        row = row_of(s)
        c256 = pl.ds(pl.multiple_of(z * 256, 256), 256)
        c128 = pl.ds(pl.multiple_of(z * 128, 128), 128)
        stage["g_q"][row, c256] = v_a[s, :, 0:256].astype(F32)
        stage["g_k"][row, c128] = v_a[s, :, 256:384].astype(F32)
        stage["g_v"][row, c128] = v_a[s, :, 384:512].astype(F32)
        stage["g_out"][row, c256] = v_a[s, :, 512:768].astype(F32)
        return carry

    lax.fori_loop(0, 16, lay_attn, 0)
    for name in ("g_q", "g_k", "g_v", "g_out"):
        place(name).start()
    for name in PLACED:
        place(name).wait()


def lay_out(o):
    hb = pl.BlockSpec(memory_space=pl.ANY)
    vm = pl.BlockSpec(memory_space=pltpu.VMEM)
    small = ("block_out", "input_grad", "g_attn", "g_ffn", "g_qg", "g_kg")
    got = pl.pallas_call(
        lay_kernel,
        out_shape=tuple(jax.ShapeDtypeStruct(s, d) for s, d in LAID.values()),
        in_specs=[hb] * 3 + [vm] * 3,
        out_specs=tuple(vm if n in small else hb for n in LAID),
        scratch_shapes=[pltpu.VMEM(*OUTPUTS[n]) for n in ("fF", "fD", "fA")]
        + [pltpu.VMEM(s, F32) for s in PLACED.values()]
        + [pltpu.SemaphoreType.DMA((4,)), pltpu.SemaphoreType.DMA((len(PLACED),))],
        compiler_params=pltpu.CompilerParams(vmem_limit_bytes=62 * 2**20),
        name="lay",
    )(o["fF"], o["fD"], o["fA"], o["block_out"], o["input_grad"], o["g_small"])
    return dict(zip(LAID, got))


def local(
    tokens, segment_ids, attn_gain, w_query, w_key, w_value, w_out, ffn_gain, w_gate, w_up, w_down,
    query_gain, key_gain, cotangent,
):
    inverse = ROPE_BASE ** (-(np.arange(32).astype(np.float32) * np.float32(2.0) / np.float32(64)))
    freq = jnp.asarray(np.tile(inverse.astype(np.float32), 4)[None])
    o = block(
        (
            tokens, segment_ids, attn_gain[None], ffn_gain[None], query_gain[None], key_gain[None], freq, w_query, w_key, w_value,
            w_out, w_gate, w_up, w_down, cotangent,
        )
    )
    o = dict(zip(OUTPUTS, o))
    w = lay_out(o)
    return (
        w["block_out"], w["input_grad"], w["g_attn"].reshape(128), w["g_q"], w["g_k"], w["g_v"], w["g_out"],
        w["g_ffn"].reshape(128), w["g_gate"], w["g_up"], w["g_down"], w["g_qg"].reshape(64),
        w["g_kg"].reshape(64),
    )


def solution(mesh):
    both = ("dp", "seq")
    w = P("dp", None)
    return jax.shard_map(
        local,
        mesh=mesh,
        in_specs=(P(both, None), P("dp", "seq"), P("dp"), w, w, w, w, P("dp"), w, w, w, P(), P(), P(both, None)),
        out_specs=(P(both, None), P(both, None), P("dp"), w, w, w, w, P("dp"), w, w, w, P(), P()),
        check_vma=False,
    )
```
